32 devices in a mesh: vec: 4 (over y, x), amp: 8 (over z, core).
Axes of the slice: x: 2, y: 2, z: 4, core: 2. Of those that a mesh axis runs over, the one named last changes fastest.
Arguments:
- chol: bfloat16 [16, 1024, 8192], P(None, 'amp', 'vec'), may hold values from -2.5 to 2.5
- amplitudes: bfloat16 [16, 256, 1024], P(None, 'amp'), may hold values from -0.125 to 0.125
- task_list: int32 [16, 4], replicated, may hold values from 0 to 15
- counts: int32 [8], replicated, may hold values from 0 to 2, as said below
Outputs:
- residual: bfloat16 [16, 256, 1024], P('vec', 'amp')
The draws below stay inside these ranges and needn't reach their ends.
Inputs may be any that keep to these rules, and one draw needn't show every extreme that they name: The counts sum to 8, and one of them equals 2.
All inputs are finite; a program needn't handle non-finite values.
Results may differ from the reference program's by a relative error of at most 0.0055.
Values may be sent and summed in bfloat16 or wider, within the bound.
No kernel may reach another device: no remote copies, remote signals or barrier semaphores. Data moves between devices by JAX's collectives and lax.ppermute only.
A program may use at most 128 MiB of HBM per device.

```python
from functools import partial
import jax
import jax.numpy as jnp
from jax import lax

VB = 32
NAUX = 8192
OPAIRS = 256
PAIRS = 1024
GROUPS = 4
GROUP_WIDTH = 2048
TILES = 16
MOST = 2
TASKS = 8
LISTS = 16
N_AMP = 8


def draw_counts(key, part):
    slot_total = N_AMP * MOST
    shuffled = jax.random.permutation(key, slot_total).astype(jnp.int32)
    busiest = shuffled[0] // MOST
    position = jnp.zeros((slot_total,), jnp.int32).at[shuffled].set(jnp.arange(slot_total, dtype=jnp.int32))
    slot_ids = jnp.arange(slot_total, dtype=jnp.int32)
    ranking = jnp.where(slot_ids // MOST == busiest, position - slot_total, position)
    chosen = jnp.argsort(ranking)[:TASKS]
    owner_ids = (chosen // MOST).astype(jnp.int32)
    return jnp.sum((owner_ids[:, None] == jnp.arange(N_AMP, dtype=jnp.int32)[None, :]).astype(jnp.int32), axis=0)


def set_ends(drawn, stream_key, low, high):
    longest = drawn.shape.index(max(drawn.shape))
    spots = []
    for shift in (0, 1):
        where = [jax.random.randint(jax.random.fold_in(stream_key, axis), (), 0, length) for axis, length in enumerate(drawn.shape)]
        where[longest] = (where[longest] + shift) % drawn.shape[longest]
        spots.append(tuple(where))
    return drawn.at[spots[0]].set(low).at[spots[1]].set(high)


def with_spikes(values, own_key, source, target, parts, factor):
    def block_of(dim):
        return (jnp.arange(values.shape[dim]) // (values.shape[dim] // parts)).reshape((-1,) + (1,) * (values.ndim - 1 - dim))

    first = jax.random.permutation(own_key, parts)[block_of(target)]
    second = (block_of(target) + parts // 2) % parts
    return jnp.where((block_of(source) == first) | (block_of(source) == second), factor * values, values)


def levels(rng, extent, split, low, high):
    def one(dim, blocks):
        steps = jax.random.uniform(jax.random.fold_in(jax.random.fold_in(rng, 6), dim), (blocks,), jnp.float32, low / len(split), high / len(split))
        return jnp.repeat(jnp.exp(steps), extent[dim] // blocks).reshape((-1,) + (1,) * (len(extent) - dim - 1))

    level = one(*split[0])
    for cut in split[1:]:
        level = level * one(*cut)
    return level


def gaussian(own_key, extent, deviation, most, cuts=(), held_as=jnp.bfloat16):
    array = jax.random.normal(own_key, extent, jnp.float32) * deviation
    if len(cuts) > 0:
        array = levels(own_key, extent, cuts, -0.22, 0.18) * array
    return jnp.clip(array, min=-most, max=most).astype(held_as)


def gaussian_with(key, dims, scale, limit, cuts, heavy, kind=jnp.bfloat16):
    array = scale * jax.random.normal(key, dims, jnp.float32)
    if cuts:
        array = array * levels(key, dims, cuts, -0.22, 0.18)
    return jnp.clip(with_spikes(array, jax.random.fold_in(key, 3), *heavy), -limit, limit).astype(kind)


def setup_inputs(seed: int = 0) -> dict:
    key_of = jax.random.split(jax.random.key(seed), 5)
    chol = gaussian_with(key_of[0], (TILES, PAIRS, NAUX), 0.125, 2.5, ((1, 8), (2, 4)), (2, 0, 4, 2.0))
    amplitudes = gaussian(key_of[1], (TILES, OPAIRS, PAIRS), (PAIRS * NAUX // 4096) ** -0.5, 0.125, ((1, 8),))
    task_list = set_ends(jax.random.randint(key_of[2], (LISTS, 4), 0, TILES), jax.random.fold_in(key_of[2], 1), 0, TILES - 1).astype(jnp.int32)
    counts = draw_counts(jax.random.fold_in(key_of[4], 71), 0)
    return dict(chol=chol, amplitudes=amplitudes, task_list=task_list, counts=counts)


def integral_tile(x_rows, y_rows):
    products = jnp.dot(x_rows, y_rows.T, preferred_element_type=jnp.float32)
    return products.reshape(VB, VB, VB, VB).transpose(0, 2, 1, 3).reshape(PAIRS, PAIRS).astype(jnp.bfloat16)


def task_term(chol, amplitudes, task_entry):
    x_groups = chol[task_entry[0]].reshape(PAIRS, GROUPS, GROUP_WIDTH).transpose(1, 0, 2)
    y_groups = chol[task_entry[1]].reshape(PAIRS, GROUPS, GROUP_WIDTH).transpose(1, 0, 2)
    amp_rows = amplitudes[task_entry[2]]

    def add_group(running, group_pair):
        integral = integral_tile(group_pair[0], group_pair[1])
        partial_term = jnp.dot(amp_rows, integral.T, preferred_element_type=jnp.float32).astype(jnp.bfloat16)
        return running + partial_term.astype(jnp.float32), None

    running, _ = lax.scan(add_group, jnp.zeros((OPAIRS, PAIRS), jnp.float32), (x_groups, y_groups))
    return running


def reference(chol, amplitudes, task_list, counts):
    offsets = jnp.cumsum(counts) - counts
    task_rank = jnp.arange(TASKS, dtype=jnp.int32)[:, None]
    inside = (task_rank >= offsets[None, :]) & (task_rank < (offsets + counts)[None, :])
    owners = jnp.arange(N_AMP, dtype=jnp.int32)[None, :]
    entries = jnp.sum(jnp.where(inside, owners * MOST + task_rank - offsets[None, :], 0), axis=1).astype(jnp.int32)
    chosen = task_list[entries]
    contribs = lax.map(partial(task_term, chol, amplitudes), chosen)
    residual = jnp.zeros((TILES, OPAIRS, PAIRS), jnp.float32).at[chosen[:, 3]].add(contribs)
    return residual.astype(jnp.bfloat16)
```

```python
import functools

import jax
import jax.numpy as jnp
import numpy as np
from jax import lax
from jax.experimental import pallas as pl
from jax.experimental.pallas import tpu as pltpu
from jax.sharding import PartitionSpec as P

VB = 32
PAIRS = VB * VB
CORES = 2
CHIPS = 4
LANES = 128
VMEM = 48 * 1024 * 1024


def plan_layout(tasks, tiles):
    fields = {}
    at = 0
    for name, size in (("order", tiles), ("local", tasks), ("spread", tasks), ("amp", tasks),
                       ("out", tasks), ("swap", tasks), ("size", 1)):
        fields[name] = (at, size)
        at += size
    return fields, at


def popcount(bits):
    bits = bits - ((bits >> 1) & 0x55555555)
    bits = (bits & 0x33333333) + ((bits >> 2) & 0x33333333)
    bits = (bits + (bits >> 4)) & 0x0F0F0F0F
    return (bits + (bits >> 8) + (bits >> 16) + (bits >> 24)) & 0xFF


def plan_kernel(tasks, tiles, most, task_ref, count_ref, plan_ref, work):
    fields, _ = plan_layout(tasks, tiles)
    first = {name: place[0] for name, place in fields.items()}
    at = jnp.int32(0)
    for owner in range(count_ref.shape[0]):
        for entry in range(most):
            live = entry < count_ref[owner]

            @pl.when(live)
            def _():
                for column in range(4):
                    work[at * 4 + column] = task_ref[owner * most + entry, column]

            at = at + live.astype(jnp.int32)
    x = [work[task * 4] for task in range(tasks)]
    y = [work[task * 4 + 1] for task in range(tasks)]
    one = jnp.int32(1)
    codes = 1 << tasks
    code = lax.broadcasted_iota(jnp.int32, (codes // LANES, LANES), 0) * LANES + lax.broadcasted_iota(
        jnp.int32, (codes // LANES, LANES), 1
    )
    bits = jnp.zeros_like(code)
    used = jnp.int32(0)
    for task in range(tasks):
        bits = bits | jnp.where((code >> task) & 1 == 1, one << y[task], one << x[task])
        used = used | (one << y[task]) | (one << x[task])
    best = jnp.min(popcount(bits) * codes + code) & (codes - 1)
    cover = jnp.int32(0)
    for task in range(tasks):
        cover = cover | (one << jnp.where((best >> task) & 1 == 1, y[task], x[task]))
    place = jnp.int32(0)
    sizes = []
    for group in (cover, used & ~cover, ~used):
        for tile in range(tiles):
            member = (group >> tile) & 1 == 1

            @pl.when(member)
            def _():
                plan_ref[first["order"] + place] = jnp.int32(tile)
                work[4 * tasks + tile] = place

            place = place + member.astype(jnp.int32)
        sizes.append(place)
    plan_ref[first["size"]] = jnp.maximum(sizes[0], (sizes[1] + 1) // 2)
    for task in range(tasks):
        swap = (best >> task) & 1 == 0
        plan_ref[first["local"] + task] = work[4 * tasks + jnp.where(swap, y[task], x[task])]
        plan_ref[first["spread"] + task] = work[4 * tasks + jnp.where(swap, x[task], y[task])]
        plan_ref[first["amp"] + task] = work[task * 4 + 2]
        plan_ref[first["out"] + task] = work[task * 4 + 3]
        plan_ref[first["swap"] + task] = swap.astype(jnp.int32)


def make_plan(tasks, tiles, task_list, counts):
    fields, length = plan_layout(tasks, tiles)
    most = task_list.shape[0] // counts.shape[0]
    plan = pl.pallas_call(
        functools.partial(plan_kernel, tasks, tiles, most),
        out_shape=jax.ShapeDtypeStruct((length,), jnp.int32),
        in_specs=[pl.BlockSpec(memory_space=pltpu.SMEM)] * 2,
        out_specs=pl.BlockSpec(memory_space=pltpu.SMEM),
        scratch_shapes=[pltpu.SMEM((4 * tasks + tiles,), jnp.int32)],
        name="plan",
    )(task_list, counts)
    return plan, {name: plan[at : at + size] for name, (at, size) in fields.items()}


def swap_fours(block):
    row = lax.broadcasted_iota(jnp.int32, block.shape, 0)
    group = lax.broadcasted_iota(jnp.int32, block.shape, 1) // VB
    rows = block.shape[0]
    for bit in (1, 2):
        upper = (row & bit) != 0
        right = (group & bit) != 0
        other = jnp.where(upper, pltpu.roll(block, bit, 0), pltpu.roll(block, rows - bit, 0))
        if bit * 2 * VB == LANES:
            moved = pltpu.roll(other, bit * VB, 1)
        else:
            moved = jnp.where(
                right, pltpu.roll(other, bit * VB, 1), pltpu.roll(other, LANES - bit * VB, 1)
            )
        block = jnp.where(upper == right, block, moved)
    return block


def ladder_kernel(
    first, slots, plan, own_a, own_b, sib_a, sib_b, fed_a, fed_b, sfed_a, sfed_b, mid_a, mid_b,
    amp_ref, order_ref, out_ref, local, spread, integral, sems,
):
    task = pl.program_id(0)
    tasks = pl.num_programs(0)
    rows = own_a.shape[1]
    pairs = ((own_a, own_b), (sib_a, sib_b), (fed_a, fed_b), (sfed_a, sfed_b))
    wide = (own_a, fed_a, mid_a, mid_b)

    def fetch(which, slot):
        at = plan[first["local"] + which]
        for block, (early, late) in enumerate(pairs):
            target = local.at[slot, pl.ds(block * rows, rows)]

            @pl.when(at < slots)
            def _():
                pltpu.make_async_copy(early.at[at], target, sems.at[slot, block]).start()

            @pl.when(at >= slots)
            def _():
                pltpu.make_async_copy(late.at[at - slots], target, sems.at[slot, block]).start()

        at = plan[first["spread"] + which]
        for block, source in enumerate(wide):
            target = spread.at[slot, pl.ds(block * rows, rows)]
            pltpu.make_async_copy(source.at[at], target, sems.at[slot, len(pairs) + block]).start()

    @pl.when(task == 0)
    def _():
        fetch(0, 0)

    @pl.when(task + 1 < tasks)
    def _():
        fetch(task + 1, (task + 1) % 2)

    slot = task % 2
    for block in range(len(pairs)):
        target = local.at[slot, pl.ds(block * rows, rows)]
        pltpu.make_async_copy(own_a.at[0], target, sems.at[slot, block]).wait()
    for block in range(len(wide)):
        target = spread.at[slot, pl.ds(block * rows, rows)]
        pltpu.make_async_copy(own_a.at[0], target, sems.at[slot, len(pairs) + block]).wait()

    across = (((1,), (1,)), ((), ()))
    products = lax.dot_general(local[slot], spread[slot], across, preferred_element_type=jnp.float32)
    ordered = jnp.dot(order_ref[...], products.astype(jnp.bfloat16), preferred_element_type=jnp.float32)
    group = ordered.shape[0] * 4 // VB
    for high in range(VB // 4):
        for wide_block in range(ordered.shape[1] // LANES):
            block = ordered[high * group : (high + 1) * group, wide_block * LANES : (wide_block + 1) * LANES]
            integral[wide_block * group : (wide_block + 1) * group, high * LANES : (high + 1) * LANES] = (
                swap_fours(block).astype(jnp.bfloat16)
            )
    term = lax.dot_general(amp_ref[0], integral[...], across, preferred_element_type=jnp.float32)
    split = out_ref.shape[2]
    for part in range(out_ref.shape[0]):
        out_ref[part, 0] = term[part * split : (part + 1) * split].astype(jnp.bfloat16)


def row_order(rows):
    new = np.arange(rows)
    width = rows * 4 // VB
    old = (new % width // 4) * VB + (new // width) * 4 + new % 4
    return (jnp.arange(rows)[None, :] == jnp.asarray(old, jnp.int32)[:, None]).astype(jnp.bfloat16)


def ladder(first, slots, parts, plan, blocks, amps):
    rows, depth = blocks[0].shape[1:]
    tasks, occupied, _ = amps.shape
    side = 4 * rows
    terms = (side // VB) ** 2
    any_spec = pl.BlockSpec(memory_space=pl.ANY)
    flops = tasks * 2 * (side * side * depth + side**3 + occupied * terms * PAIRS)
    return pl.pallas_call(
        functools.partial(ladder_kernel, first, slots),
        out_shape=jax.ShapeDtypeStruct((parts, tasks, occupied // parts, terms), jnp.bfloat16),
        grid_spec=pltpu.PrefetchScalarGridSpec(
            num_scalar_prefetch=1,
            grid=(tasks,),
            in_specs=[any_spec] * len(blocks)
            + [
                pl.BlockSpec((1, occupied, PAIRS), lambda task, plan: (task, 0, 0)),
                pl.BlockSpec((side, side), lambda task, plan: (0, 0)),
            ],
            out_specs=pl.BlockSpec(
                (parts, 1, occupied // parts, terms), lambda task, plan: (0, task, 0, 0)
            ),
            scratch_shapes=[
                pltpu.VMEM((2, side, depth), jnp.bfloat16),
                pltpu.VMEM((2, side, depth), jnp.bfloat16),
                pltpu.VMEM((terms, PAIRS), jnp.bfloat16),
                pltpu.SemaphoreType.DMA((2, 8)),
            ],
        ),
        compiler_params=pltpu.CompilerParams(vmem_limit_bytes=VMEM),
        cost_estimate=pl.CostEstimate(
            flops=flops, bytes_accessed=tasks * 2 * (2 * side * depth + occupied * PAIRS), transcendentals=0
        ),
        name="ladder",
    )(plan, *blocks, amps, row_order(side))


def routes():
    last = CHIPS - 1
    feed = [(0, 1), (last, last - 1)]
    middle = [(1, 2), (2, 1)]
    both = lambda hops: [(a * CORES + c, b * CORES + c) for a, b in hops for c in range(CORES)]
    sibling = [(a * CORES + c, a * CORES + 1 - c) for a in range(CHIPS) for c in range(CORES)]
    return both(feed), both(middle), sibling


def gathered_amps(amplitudes, chosen, swapped):
    columns = lax.axis_size("vec")
    rows = amplitudes.shape[1] // columns
    mine = lax.dynamic_slice_in_dim(amplitudes, lax.axis_index("vec") * rows, rows, axis=1)
    mine = jnp.take(mine, chosen, axis=0)
    turned = mine.reshape(-1, rows, VB, VB).swapaxes(2, 3).reshape(mine.shape)
    mine = jnp.where(swapped[:, None, None] == 1, turned, mine)
    whole = lax.all_gather(mine, ("vec", "amp"), axis=0, tiled=False)
    return whole.transpose(1, 0, 2, 3).reshape(mine.shape[0], -1, PAIRS)


def products(first, slots, tiles, chol, amplitudes, plan, named):
    feed, middle, sibling = routes()
    send = functools.partial(lax.ppermute, axis_name="amp")
    own_a = jnp.take(chol, named["order"][:slots], axis=0)
    fed_a = send(own_a, perm=feed)
    mid_a = send(own_a, perm=middle)
    rest = min(2 * slots, tiles) - slots
    own_b = jnp.take(chol, named["order"][slots : slots + rest], axis=0)
    sib_a = send(own_a, perm=sibling)
    sib_b = send(own_b, perm=sibling)
    amps = gathered_amps(amplitudes, named["amp"], named["swap"])
    fed_b = send(own_b, perm=feed)
    mid_b = send(fed_a, perm=middle)
    sfed_a = send(fed_a, perm=sibling)
    sfed_b = send(fed_b, perm=sibling)
    blocks = (own_a, own_b, sib_a, sib_b, fed_a, fed_b, sfed_a, sfed_b, mid_a, mid_b)
    return ladder(first, slots, lax.axis_size("vec"), plan, blocks, amps)


def target_columns():
    worker, wide, low, fine = np.meshgrid(
        np.arange(2 * CORES), np.arange(CHIPS), np.arange(4 * VB // 8), np.arange(4), indexing="ij"
    )
    core = worker % CORES
    chip = 1 + worker // CORES
    near = np.where(chip == 1, 0, CHIPS - 1)
    far = np.where(chip == 1, 2, 1)
    end = np.where(chip == 1, CHIPS - 1, 0)
    each = VB // (CHIPS * CORES)
    block = low // each
    local_chip = np.where(block < 2, chip, near)
    local_core = np.where(block % 2 == 0, core, 1 - core)
    local = (local_chip * CORES + local_core) * each + low % each
    spread_chip = np.choose(wide, [chip, near, far, end])
    spread = (spread_chip * CORES + core) * each + fine
    return local.reshape(-1), spread.reshape(-1)


def scatter_terms(terms, named, tiles):
    columns, tasks, rows, width = terms.shape
    owners = lax.axis_size("amp")
    each = rows // owners
    mine = lax.all_to_all(terms, "vec", split_axis=0, concat_axis=0, tiled=True)
    mine = jnp.sum(mine.astype(jnp.float32), axis=0).astype(jnp.bfloat16)
    mine = mine.reshape(tasks, owners, each, width).swapaxes(0, 1)
    mine = lax.all_to_all(mine, "amp", split_axis=0, concat_axis=0, tiled=True)
    mine = mine[CORES : CORES * (CHIPS - 1)].transpose(1, 2, 0, 3).reshape(tasks * each, PAIRS)
    local, spread = target_columns()
    canonical = jnp.arange(PAIRS, dtype=jnp.int32)[None, :]
    straight = (jnp.asarray(local * VB + spread, jnp.int32)[:, None] == canonical).astype(jnp.bfloat16)
    turned = (jnp.asarray(spread * VB + local, jnp.int32)[:, None] == canonical).astype(jnp.bfloat16)
    dot = functools.partial(jnp.dot, preferred_element_type=jnp.float32)
    straight, turned = dot(mine, straight), dot(mine, turned)
    swapped = jnp.repeat(named["swap"], each)[:, None] == 1
    placed = jnp.where(swapped, turned, straight).astype(jnp.bfloat16).reshape(tasks, each * PAIRS)
    chosen = (jnp.arange(tiles, dtype=jnp.int32)[:, None] == named["out"][None, :]).astype(jnp.bfloat16)
    summed = dot(chosen, placed).astype(jnp.bfloat16).reshape(columns, tiles // columns, each, PAIRS)
    summed = lax.all_to_all(summed, "vec", split_axis=0, concat_axis=0, tiled=True)
    return summed.transpose(1, 0, 2, 3).reshape(tiles // columns, columns * each, PAIRS)


def line_local(chol, amplitudes, task_list, counts):
    tasks = lax.axis_size("amp")
    tiles = chol.shape[0]
    plan, named = make_plan(tasks, tiles, task_list, counts)
    first = {name: place[0] for name, place in plan_layout(tasks, tiles)[0].items()}
    sizes = [tasks // 2, tasks // 2 + 1, tasks // 2 + 2, tasks]
    branch = functools.reduce(
        lambda total, size: total + (named["size"][0] > size).astype(jnp.int32), sizes[:-1], jnp.int32(0)
    )
    run = lambda slots: lambda: products(first, slots, tiles, chol, amplitudes, plan, named)
    terms = lax.switch(branch, [run(slots) for slots in sizes])
    return scatter_terms(terms, named, tiles)


def integral_tile(x_rows, y_rows):
    products = lax.dot_general(
        x_rows, y_rows, (((1,), (1,)), ((), ())), preferred_element_type=jnp.float32
    )
    return (
        products.reshape(VB, VB, VB, VB).transpose(0, 2, 1, 3).reshape(PAIRS, PAIRS).astype(jnp.bfloat16)
    )


def task_term(x_rows, y_rows, amp_rows):
    products = lax.dot_general(
        amp_rows, integral_tile(x_rows, y_rows), (((1,), (1,)), ((), ())), preferred_element_type=jnp.float32
    )
    return products.astype(jnp.bfloat16)


def spread_local(chol, amplitudes, task_list, counts):
    owners = lax.axis_size("amp")
    most = task_list.shape[0] // owners
    rank = jnp.arange(owners, dtype=jnp.int32)[:, None]
    offsets = jnp.cumsum(counts) - counts
    inside = (rank >= offsets) & (rank < offsets + counts)
    starts = jnp.arange(owners, dtype=jnp.int32) * most
    fields = task_list[jnp.sum(jnp.where(inside, starts + rank - offsets, 0), axis=1)]
    trade = functools.partial(lax.all_to_all, axis_name="amp", tiled=True)
    fetch = lambda array, which: trade(jnp.take(array, which, axis=0), split_axis=0, concat_axis=0).reshape(
        -1, array.shape[2]
    )
    term = task_term(fetch(chol, fields[:, 0]), fetch(chol, fields[:, 1]), fetch(amplitudes, fields[:, 2]))
    returned = trade(term.reshape(owners, -1, PAIRS), split_axis=0, concat_axis=0)
    tiles = amplitudes.shape[0]
    chosen = (jnp.arange(tiles, dtype=jnp.int32)[:, None] == fields[:, 3][None, :]).astype(jnp.bfloat16)
    summed = jnp.dot(chosen, returned.reshape(owners, -1), preferred_element_type=jnp.float32)
    summed = summed.reshape(tiles, -1, PAIRS)
    return lax.psum_scatter(summed, "vec", scatter_dimension=0, tiled=True).astype(jnp.bfloat16)


def solution(mesh):
    placed = (P(None, "amp", "vec"), P(None, "amp", None), P(), P())
    local = line_local if mesh.shape["amp"] == CHIPS * CORES else spread_local
    return jax.shard_map(
        local, mesh=mesh, in_specs=placed, out_specs=P("vec", "amp", None), check_vma=False
    )
```

```python
import functools

import jax
import jax.numpy as jnp
import numpy as np
from jax import lax
from jax.experimental import pallas as pl
from jax.experimental.pallas import tpu as pltpu
from jax.sharding import PartitionSpec as P

VB = 32
PAIRS = VB * VB
CORES = 2
CHIPS = 4
LANES = 128
VMEM = 60 * 1024 * 1024


def plan_layout(tasks, tiles):
    fields = {}
    at = 0
    for name, size in (("order", tiles), ("local", tasks), ("spread", tasks), ("amp", tasks),
                       ("out", tasks), ("swap", tasks), ("size", 1)):
        fields[name] = (at, size)
        at += size
    return fields, at


def popcount(bits):
    bits = bits - ((bits >> 1) & 0x55555555)
    bits = (bits & 0x33333333) + ((bits >> 2) & 0x33333333)
    bits = (bits + (bits >> 4)) & 0x0F0F0F0F
    return (bits + (bits >> 8) + (bits >> 16) + (bits >> 24)) & 0xFF


def plan_kernel(tasks, tiles, most, task_ref, count_ref, plan_ref, work):
    fields, _ = plan_layout(tasks, tiles)
    first = {name: place[0] for name, place in fields.items()}
    at = jnp.int32(0)
    for owner in range(count_ref.shape[0]):
        for entry in range(most):
            live = entry < count_ref[owner]

            @pl.when(live)
            def _():
                for column in range(4):
                    work[at * 4 + column] = task_ref[owner * most + entry, column]

            at = at + live.astype(jnp.int32)
    x = [work[task * 4] for task in range(tasks)]
    y = [work[task * 4 + 1] for task in range(tasks)]
    one = jnp.int32(1)
    codes = 1 << tasks
    code = lax.broadcasted_iota(jnp.int32, (codes // LANES, LANES), 0) * LANES + lax.broadcasted_iota(
        jnp.int32, (codes // LANES, LANES), 1
    )
    bits = jnp.zeros_like(code)
    used = jnp.int32(0)
    for task in range(tasks):
        bits = bits | jnp.where((code >> task) & 1 == 1, one << y[task], one << x[task])
        used = used | (one << y[task]) | (one << x[task])
    best = jnp.min(popcount(bits) * codes + code) & (codes - 1)
    cover = jnp.int32(0)
    for task in range(tasks):
        cover = cover | (one << jnp.where((best >> task) & 1 == 1, y[task], x[task]))
    place = jnp.int32(0)
    sizes = []
    for group in (cover, used & ~cover, ~used):
        for tile in range(tiles):
            member = (group >> tile) & 1 == 1

            @pl.when(member)
            def _():
                plan_ref[first["order"] + place] = jnp.int32(tile)
                work[4 * tasks + tile] = place

            place = place + member.astype(jnp.int32)
        sizes.append(place)
    plan_ref[first["size"]] = jnp.maximum(sizes[0], (sizes[1] + 1) // 2)
    for task in range(tasks):
        swap = (best >> task) & 1 == 0
        plan_ref[first["local"] + task] = work[4 * tasks + jnp.where(swap, y[task], x[task])]
        plan_ref[first["spread"] + task] = work[4 * tasks + jnp.where(swap, x[task], y[task])]
        plan_ref[first["amp"] + task] = work[task * 4 + 2]
        plan_ref[first["out"] + task] = work[task * 4 + 3]
        plan_ref[first["swap"] + task] = swap.astype(jnp.int32)


def make_plan(tasks, tiles, task_list, counts):
    fields, length = plan_layout(tasks, tiles)
    most = task_list.shape[0] // counts.shape[0]
    plan = pl.pallas_call(
        functools.partial(plan_kernel, tasks, tiles, most),
        out_shape=jax.ShapeDtypeStruct((length,), jnp.int32),
        in_specs=[pl.BlockSpec(memory_space=pltpu.SMEM)] * 2,
        out_specs=pl.BlockSpec(memory_space=pltpu.SMEM),
        scratch_shapes=[pltpu.SMEM((4 * tasks + tiles,), jnp.int32)],
        name="plan",
    )(task_list, counts)
    return plan, {name: plan[at : at + size] for name, (at, size) in fields.items()}


def collect_kernel(first, plan, chol, out, sems):
    copies = [
        pltpu.make_async_copy(chol.at[plan[first + slot]], out.at[slot], sems.at[slot])
        for slot in range(out.shape[0])
    ]
    for copy in copies:
        copy.start()
    for copy in copies:
        copy.wait()


def collect(first, slots, plan, chol):
    return pl.pallas_call(
        functools.partial(collect_kernel, first),
        out_shape=jax.ShapeDtypeStruct((slots, *chol.shape[1:]), chol.dtype),
        in_specs=[pl.BlockSpec(memory_space=pltpu.SMEM), pl.BlockSpec(memory_space=pl.ANY)],
        out_specs=pl.BlockSpec(memory_space=pl.ANY),
        scratch_shapes=[pltpu.SemaphoreType.DMA((slots,))],
        compiler_params=pltpu.CompilerParams(vmem_limit_bytes=VMEM),
        name="collect",
    )(plan, chol)


def swap_fours(blocks):
    group = lax.broadcasted_iota(jnp.int32, blocks[0].shape, 1) // VB
    for bit in (1, 2):
        right = (group & bit) != 0
        shift = bit * VB
        moved = list(blocks)
        for low in range(4):
            if low & bit:
                continue
            high = low | bit
            moved[low] = jnp.where(right, pltpu.roll(blocks[high], shift, 1), blocks[low])
            moved[high] = jnp.where(right, blocks[high], pltpu.roll(blocks[low], LANES - shift, 1))
        blocks = moved
    return blocks


def chip_order(upper):
    straight = [1, 0, 2, 3]
    return [jnp.where(upper, CHIPS - 1 - chip, chip) for chip in straight]


def ladder_kernel(
    first, slots, begin, plan, own_a, own_b, sib_a, sib_b, fed_a, fed_b, sfed_a, sfed_b, mid_a, mid_b,
    amp_own, amp_sib, order_ref, *rest,
):
    *outs, local, spread, amps, integral, sems = rest
    step = pl.program_id(0)
    steps = pl.num_programs(0)
    rows = own_a.shape[1]
    pairs = ((own_a, own_b), (sib_a, sib_b), (fed_a, fed_b), (sfed_a, sfed_b))
    wide = (own_a, fed_a, mid_a, mid_b)
    column = lax.axis_index("vec")
    place = lax.axis_index("amp")
    core = lax.rem(place, CORES)
    chips = chip_order(place >= CHIPS * CORES // 2)
    each, amp_rows = amp_own.shape[2:4]
    straight = len(pairs) + len(wide)

    def amp_copies(task, slot):
        copies = []
        for which, (source, holder) in enumerate(((amp_own, core), (amp_sib, 1 - core))):
            for chip in range(CHIPS):
                at = pl.multiple_of((chips[chip] * CORES + holder) * amp_rows, amp_rows)
                copies.append(
                    pltpu.make_async_copy(
                        source.at[task // each, chip, lax.rem(task, each)],
                        amps.at[slot, pl.ds(at, amp_rows)],
                        sems.at[slot, straight + which * CHIPS + chip],
                    )
                )
        return copies

    def fetch(which, slot):
        task = begin + (which ^ column)
        at = plan[first["local"] + task]
        for block, (early, late) in enumerate(pairs):
            target = local.at[slot, pl.ds(block * rows, rows)]

            @pl.when(at < slots)
            def _():
                pltpu.make_async_copy(early.at[at], target, sems.at[slot, block]).start()

            @pl.when(at >= slots)
            def _():
                pltpu.make_async_copy(late.at[at - slots], target, sems.at[slot, block]).start()

        at = plan[first["spread"] + task]
        for block, source in enumerate(wide):
            target = spread.at[slot, pl.ds(block * rows, rows)]
            pltpu.make_async_copy(source.at[at], target, sems.at[slot, len(pairs) + block]).start()
        for copy in amp_copies(task, slot):
            copy.start()

    @pl.when(step == 0)
    def _():
        fetch(0, 0)

    @pl.when(step + 1 < steps)
    def _():
        fetch(step + 1, lax.rem(step + 1, 2))

    slot = lax.rem(step, 2)
    for block in range(len(pairs)):
        target = local.at[slot, pl.ds(block * rows, rows)]
        pltpu.make_async_copy(own_a.at[0], target, sems.at[slot, block]).wait()
    for block in range(len(wide)):
        target = spread.at[slot, pl.ds(block * rows, rows)]
        pltpu.make_async_copy(own_a.at[0], target, sems.at[slot, len(pairs) + block]).wait()
    for copy in amp_copies(begin + (step ^ column), slot):
        copy.wait()

    across = (((1,), (1,)), ((), ()))
    products = lax.dot_general(local[slot], spread[slot], across, preferred_element_type=jnp.float32)
    ordered = jnp.dot(order_ref[...], products.astype(jnp.bfloat16), preferred_element_type=jnp.float32)
    quarter = ordered.shape[0] // 4
    group = ordered.shape[0] // VB
    for high in range(VB // 4):
        for wide_block in range(ordered.shape[1] // LANES):
            lanes = slice(wide_block * LANES, (wide_block + 1) * LANES)
            blocks = [
                ordered[low * quarter + high * group : low * quarter + (high + 1) * group, lanes]
                for low in range(4)
            ]
            for low, block in enumerate(swap_fours(blocks)):
                at = (wide_block * 4 + low) * group
                integral[at : at + group, high * LANES : (high + 1) * LANES] = block.astype(jnp.bfloat16)
    term = lax.dot_general(amps[slot], integral[...], across, preferred_element_type=jnp.float32)
    for which, out in enumerate(outs):

        @pl.when(step == which)
        def _():
            out[...] = term.astype(jnp.bfloat16)


def row_order(rows):
    new = np.arange(rows)
    group = rows // VB
    low, high, place = new // (rows // 4), new // group % (VB // 4), new % group
    old = place * VB + high * 4 + low
    return (jnp.arange(rows)[None, :] == jnp.asarray(old, jnp.int32)[:, None]).astype(jnp.bfloat16)


def ladder(first, slots, begin, plan, blocks, amps, order):
    rows, depth = blocks[0].shape[1:]
    columns = lax.axis_size("vec")
    occupied = CHIPS * CORES * amps[0].shape[3]
    side = 4 * rows
    terms = (side // VB) ** 2
    any_spec = pl.BlockSpec(memory_space=pl.ANY)
    flops = columns * 2 * (side * side * depth + side**3 + occupied * terms * PAIRS)
    return pl.pallas_call(
        functools.partial(ladder_kernel, first, slots, begin),
        out_shape=[jax.ShapeDtypeStruct((occupied, terms), jnp.bfloat16)] * columns,
        grid_spec=pltpu.PrefetchScalarGridSpec(
            num_scalar_prefetch=1,
            grid=(columns,),
            in_specs=[any_spec] * (len(blocks) + len(amps))
            + [pl.BlockSpec((side, side), lambda step, plan: (0, 0))],
            out_specs=[pl.BlockSpec((occupied, terms), lambda step, plan: (0, 0))] * columns,
            scratch_shapes=[
                pltpu.VMEM((2, side, depth), jnp.bfloat16),
                pltpu.VMEM((2, side, depth), jnp.bfloat16),
                pltpu.VMEM((2, occupied, PAIRS), jnp.bfloat16),
                pltpu.VMEM((terms, PAIRS), jnp.bfloat16),
                pltpu.SemaphoreType.DMA((2, 16)),
            ],
        ),
        compiler_params=pltpu.CompilerParams(vmem_limit_bytes=VMEM),
        cost_estimate=pl.CostEstimate(
            flops=flops, bytes_accessed=columns * 2 * (2 * side * depth + occupied * PAIRS), transcendentals=0
        ),
        name="ladder",
    )(plan, *blocks, *amps, order)


def routes():
    last = CHIPS - 1
    feed = [(0, 1), (last, last - 1)]
    middle = [(1, 2), (2, 1)]
    both = lambda hops: [(a * CORES + c, b * CORES + c) for a, b in hops for c in range(CORES)]
    sibling = [(a * CORES + c, a * CORES + 1 - c) for a in range(CHIPS) for c in range(CORES)]
    return both(feed), both(middle), sibling


def swap_columns(array, bit, columns):
    return lax.ppermute(array, "vec", perm=[(column, column ^ bit) for column in range(columns)])


def gathered_amps(amplitudes, named):
    feed, middle, sibling = routes()
    send = functools.partial(lax.ppermute, axis_name="amp")
    each = named["amp"].shape[0] // lax.axis_size("vec")
    column = lax.axis_index("vec")
    part = lambda name: lax.dynamic_slice_in_dim(named[name], column * each, each)
    mine = jnp.take(amplitudes, part("amp"), axis=0, mode="clip")
    turned = mine.reshape(*mine.shape[:2], VB, VB).swapaxes(2, 3).reshape(mine.shape)
    mine = jnp.where(part("swap")[:, None, None] == 1, turned, mine)[None]
    near = jnp.concatenate([mine, send(mine, perm=feed)])
    line = jnp.concatenate([near, send(near, perm=middle)])
    whole = lax.all_gather(line, "vec", axis=0, tiled=False)
    return whole, send(whole, perm=sibling)


def products(first, slots, tiles, chol, amplitudes, plan, named):
    feed, middle, sibling = routes()
    send = functools.partial(lax.ppermute, axis_name="amp")
    start = first["order"]
    own_a = collect(start, slots, plan, chol)
    fed_a = send(own_a, perm=feed)
    mid_a = send(own_a, perm=middle)
    own_b = collect(start + slots, min(2 * slots, tiles) - slots, plan, chol)
    amps = gathered_amps(amplitudes, named)
    sib_a = send(own_a, perm=sibling)
    own_b, fed_a = lax.optimization_barrier((own_b, fed_a))
    mid_b = send(fed_a, perm=middle)
    fed_b = send(own_b, perm=feed)
    sib_b = send(own_b, perm=sibling)
    sfed_a = send(fed_a, perm=sibling)
    sfed_b = send(fed_b, perm=sibling)
    blocks = (own_a, own_b, sib_a, sib_b, fed_a, fed_b, sfed_a, sfed_b, mid_a, mid_b)
    columns = lax.axis_size("vec")
    order = row_order(4 * chol.shape[1])
    halves = []
    for begin in range(0, named["amp"].shape[0], columns):
        terms = ladder(first, slots, begin, plan, blocks, amps, order)
        arrived = [terms[0]] + [swap_columns(terms[bit], bit, columns) for bit in range(1, columns)]
        halves.append(sum(term.astype(jnp.float32) for term in arrived).astype(jnp.bfloat16))
    return jnp.stack(halves)


def target_columns():
    worker, wide, fine, low = np.meshgrid(
        np.arange(2 * CORES), np.arange(CHIPS), np.arange(4), np.arange(4 * VB // 8), indexing="ij"
    )
    core = worker % CORES
    chip = 1 + worker // CORES
    near = np.where(chip == 1, 0, CHIPS - 1)
    far = np.where(chip == 1, 2, 1)
    end = np.where(chip == 1, CHIPS - 1, 0)
    each = VB // (CHIPS * CORES)
    block = low // each
    local_chip = np.where(block < 2, chip, near)
    local_core = np.where(block % 2 == 0, core, 1 - core)
    local = (local_chip * CORES + local_core) * each + low % each
    spread_chip = np.choose(wide, [chip, near, far, end])
    spread = (spread_chip * CORES + core) * each + fine
    return local.reshape(-1), spread.reshape(-1)


def scatter_terms(terms, named, tiles):
    columns = lax.axis_size("vec")
    column = lax.axis_index("vec")
    owners = lax.axis_size("amp")
    halves, rows, width = terms.shape
    each = rows // owners
    mine = terms.reshape(halves, owners, each, width).swapaxes(0, 1)
    mine = lax.all_to_all(mine, "amp", split_axis=0, concat_axis=0, tiled=True)
    mine = mine[CORES : CORES * (CHIPS - 1)].transpose(1, 2, 0, 3).reshape(halves * each, PAIRS)
    local, spread = target_columns()
    canonical = jnp.arange(PAIRS, dtype=jnp.int32)[None, :]
    straight = (jnp.asarray(local * VB + spread, jnp.int32)[:, None] == canonical).astype(jnp.bfloat16)
    turned = (jnp.asarray(spread * VB + local, jnp.int32)[:, None] == canonical).astype(jnp.bfloat16)
    dot = functools.partial(jnp.dot, preferred_element_type=jnp.float32)
    straight, turned = dot(mine, straight), dot(mine, turned)
    swap = named["swap"].reshape(halves, columns)
    out = named["out"].reshape(halves, columns)
    swapped = jnp.repeat(lax.dynamic_index_in_dim(swap, column, 1), each, axis=0) == 1
    placed = jnp.where(swapped, turned, straight).astype(jnp.bfloat16).reshape(halves, each, PAIRS)
    held = tiles // columns
    here = column * held + jnp.arange(held, dtype=jnp.int32)
    total = jnp.zeros((held, each, PAIRS), jnp.float32)
    for bit in range(columns):
        arrived = placed if bit == 0 else swap_columns(placed, bit, columns)
        targets = lax.dynamic_index_in_dim(out, column ^ bit, 1, keepdims=False)
        for half in range(halves):
            named_here = (here == targets[half])[:, None, None]
            total = total + jnp.where(named_here, arrived[half].astype(jnp.float32)[None], 0.0)
    return total.astype(jnp.bfloat16)


def line_local(chol, amplitudes, task_list, counts):
    tasks = lax.axis_size("amp")
    tiles = chol.shape[0]
    plan, named = make_plan(tasks, tiles, task_list, counts)
    first = {name: place[0] for name, place in plan_layout(tasks, tiles)[0].items()}
    sizes = [tasks // 2, tasks // 2 + 1, tasks // 2 + 2, tasks]
    branch = functools.reduce(
        lambda total, size: total + (named["size"][0] > size).astype(jnp.int32), sizes[:-1], jnp.int32(0)
    )
    run = lambda slots: lambda: products(first, slots, tiles, chol, amplitudes, plan, named)
    terms = lax.switch(branch, [run(slots) for slots in sizes])
    return scatter_terms(terms, named, tiles)


def integral_tile(x_rows, y_rows):
    products = lax.dot_general(
        x_rows, y_rows, (((1,), (1,)), ((), ())), preferred_element_type=jnp.float32
    )
    return (
        products.reshape(VB, VB, VB, VB).transpose(0, 2, 1, 3).reshape(PAIRS, PAIRS).astype(jnp.bfloat16)
    )


def task_term(x_rows, y_rows, amp_rows):
    products = lax.dot_general(
        amp_rows, integral_tile(x_rows, y_rows), (((1,), (1,)), ((), ())), preferred_element_type=jnp.float32
    )
    return products.astype(jnp.bfloat16)


def spread_local(chol, amplitudes, task_list, counts):
    owners = lax.axis_size("amp")
    most = task_list.shape[0] // owners
    rank = jnp.arange(owners, dtype=jnp.int32)[:, None]
    offsets = jnp.cumsum(counts) - counts
    inside = (rank >= offsets) & (rank < offsets + counts)
    starts = jnp.arange(owners, dtype=jnp.int32) * most
    fields = task_list[jnp.sum(jnp.where(inside, starts + rank - offsets, 0), axis=1)]
    trade = functools.partial(lax.all_to_all, axis_name="amp", tiled=True)
    fetch = lambda array, which: trade(jnp.take(array, which, axis=0), split_axis=0, concat_axis=0).reshape(
        -1, array.shape[2]
    )
    term = task_term(fetch(chol, fields[:, 0]), fetch(chol, fields[:, 1]), fetch(amplitudes, fields[:, 2]))
    returned = trade(term.reshape(owners, -1, PAIRS), split_axis=0, concat_axis=0)
    tiles = amplitudes.shape[0]
    chosen = (jnp.arange(tiles, dtype=jnp.int32)[:, None] == fields[:, 3][None, :]).astype(jnp.bfloat16)
    summed = jnp.dot(chosen, returned.reshape(owners, -1), preferred_element_type=jnp.float32)
    summed = summed.reshape(tiles, -1, PAIRS)
    return lax.psum_scatter(summed, "vec", scatter_dimension=0, tiled=True).astype(jnp.bfloat16)


def solution(mesh):
    placed = (P(None, "amp", "vec"), P(None, "amp", None), P(), P())
    local = line_local if mesh.shape["amp"] == CHIPS * CORES else spread_local
    return jax.shard_map(
        local, mesh=mesh, in_specs=placed, out_specs=P("vec", "amp", None), check_vma=False
    )
```

```python
import functools

import jax
import jax.numpy as jnp
import numpy as np
from jax import lax
from jax.experimental import pallas as pl
from jax.experimental.pallas import tpu as pltpu
from jax.sharding import PartitionSpec as P

VB = 32
PAIRS = VB * VB
CORES = 2
CHIPS = 4
LANES = 128
PARTS = 2
VMEM = 60 * 1024 * 1024


def plan_layout(tasks, tiles):
    fields = {}
    at = 0
    for name, size in (("order", tiles), ("local", tasks), ("spread", tasks), ("amp", tasks),
                       ("out", tasks), ("swap", tasks), ("size", 1)):
        fields[name] = (at, size)
        at += size
    return fields, at


def popcount(bits):
    bits = bits - ((bits >> 1) & 0x55555555)
    bits = (bits & 0x33333333) + ((bits >> 2) & 0x33333333)
    bits = (bits + (bits >> 4)) & 0x0F0F0F0F
    return (bits + (bits >> 8) + (bits >> 16) + (bits >> 24)) & 0xFF


def plan_kernel(tasks, tiles, most, task_ref, count_ref, plan_ref, work):
    fields, _ = plan_layout(tasks, tiles)
    first = {name: place[0] for name, place in fields.items()}
    at = jnp.int32(0)
    for owner in range(count_ref.shape[0]):
        for entry in range(most):
            live = entry < count_ref[owner]

            @pl.when(live)
            def _():
                for column in range(4):
                    work[at * 4 + column] = task_ref[owner * most + entry, column]

            at = at + live.astype(jnp.int32)
    x = [work[task * 4] for task in range(tasks)]
    y = [work[task * 4 + 1] for task in range(tasks)]
    one = jnp.int32(1)
    codes = 1 << tasks
    code = lax.broadcasted_iota(jnp.int32, (codes // LANES, LANES), 0) * LANES + lax.broadcasted_iota(
        jnp.int32, (codes // LANES, LANES), 1
    )
    bits = jnp.zeros_like(code)
    used = jnp.int32(0)
    for task in range(tasks):
        bits = bits | jnp.where((code >> task) & 1 == 1, one << y[task], one << x[task])
        used = used | (one << y[task]) | (one << x[task])
    best = jnp.min(popcount(bits) * codes + code) & (codes - 1)
    cover = jnp.int32(0)
    for task in range(tasks):
        cover = cover | (one << jnp.where((best >> task) & 1 == 1, y[task], x[task]))
    place = jnp.int32(0)
    sizes = []
    for group in (cover, used & ~cover, ~used):
        for tile in range(tiles):
            member = (group >> tile) & 1 == 1

            @pl.when(member)
            def _():
                plan_ref[first["order"] + place] = jnp.int32(tile)
                work[4 * tasks + tile] = place

            place = place + member.astype(jnp.int32)
        sizes.append(place)
    plan_ref[first["size"]] = jnp.maximum(sizes[0], (sizes[1] + 1) // 2)
    for task in range(tasks):
        swap = (best >> task) & 1 == 0
        plan_ref[first["local"] + task] = work[4 * tasks + jnp.where(swap, y[task], x[task])]
        plan_ref[first["spread"] + task] = work[4 * tasks + jnp.where(swap, x[task], y[task])]
        plan_ref[first["amp"] + task] = work[task * 4 + 2]
        plan_ref[first["out"] + task] = work[task * 4 + 3]
        plan_ref[first["swap"] + task] = swap.astype(jnp.int32)


def make_plan(tasks, tiles, task_list, counts):
    fields, length = plan_layout(tasks, tiles)
    most = task_list.shape[0] // counts.shape[0]
    plan = pl.pallas_call(
        functools.partial(plan_kernel, tasks, tiles, most),
        out_shape=jax.ShapeDtypeStruct((length,), jnp.int32),
        in_specs=[pl.BlockSpec(memory_space=pltpu.SMEM)] * 2,
        out_specs=pl.BlockSpec(memory_space=pltpu.SMEM),
        scratch_shapes=[pltpu.SMEM((4 * tasks + tiles,), jnp.int32)],
        name="plan",
    )(task_list, counts)
    return plan, {name: plan[at : at + size] for name, (at, size) in fields.items()}


def collect_kernel(plan, rows_ref, *outs):
    depth = outs[0].shape[2]
    for part, out in enumerate(outs):
        out[...] = rows_ref[:, :, part * depth : (part + 1) * depth]


def collect(first, slots, parts, plan, chol):
    _, rows, depth = chol.shape
    chunk = (1, rows, depth // parts)
    return pl.pallas_call(
        collect_kernel,
        out_shape=[jax.ShapeDtypeStruct((slots, *chunk[1:]), chol.dtype)] * parts,
        grid_spec=pltpu.PrefetchScalarGridSpec(
            num_scalar_prefetch=1,
            grid=(slots,),
            in_specs=[pl.BlockSpec((1, rows, depth), lambda slot, plan: (plan[first + slot], 0, 0))],
            out_specs=[pl.BlockSpec(chunk, lambda slot, plan: (slot, 0, 0))] * parts,
        ),
        compiler_params=pltpu.CompilerParams(vmem_limit_bytes=VMEM),
        name="collect",
    )(plan, chol)


def swap_fours(blocks):
    group = lax.broadcasted_iota(jnp.int32, blocks[0].shape, 1) // VB
    for bit in (1, 2):
        right = (group & bit) != 0
        shift = bit * VB
        moved = list(blocks)
        for low in range(4):
            if low & bit:
                continue
            high = low | bit
            moved[low] = jnp.where(right, pltpu.roll(blocks[high], shift, 1), blocks[low])
            moved[high] = jnp.where(right, blocks[high], pltpu.roll(blocks[low], LANES - shift, 1))
        blocks = moved
    return blocks


BLOCKS = 10
ACROSS = (((1,), (1,)), ((), ()))


def row_fetch(first, slots, plan, sources, local, spread, sems):
    own_a, own_b, sib_a, sib_b, fed_a, fed_b, sfed_a, sfed_b, mid_a, mid_b = sources
    rows = own_a.shape[1]
    pairs = ((own_a, own_b), (sib_a, sib_b), (fed_a, fed_b), (sfed_a, sfed_b))
    wide = (own_a, fed_a, mid_a, mid_b)

    def start(task, slot):
        at = plan[first["local"] + task]
        for block, (early, late) in enumerate(pairs):
            target = local.at[slot, pl.ds(block * rows, rows)]

            @pl.when(at < slots)
            def _():
                pltpu.make_async_copy(early.at[at], target, sems.at[slot, block]).start()

            @pl.when(at >= slots)
            def _():
                pltpu.make_async_copy(late.at[at - slots], target, sems.at[slot, block]).start()

        at = plan[first["spread"] + task]
        for block, source in enumerate(wide):
            target = spread.at[slot, pl.ds(block * rows, rows)]
            pltpu.make_async_copy(source.at[at], target, sems.at[slot, len(pairs) + block]).start()

    def wait(slot):
        for which, buffer in enumerate((local, spread)):
            for block in range(len(wide)):
                target = buffer.at[slot, pl.ds(block * rows, rows)]
                sem = sems.at[slot, which * len(wide) + block]
                pltpu.make_async_copy(own_a.at[0], target, sem).wait()

    return start, wait


def streamed(start, wait, task_of):
    step = pl.program_id(0)

    @pl.when(step == 0)
    def _():
        start(task_of(0), 0)

    @pl.when(step + 1 < pl.num_programs(0))
    def _():
        start(task_of(step + 1), lax.rem(step + 1, 2))

    slot = lax.rem(step, 2)
    wait(slot)
    return slot


def partial_kernel(first, slots, plan, *refs):
    *sources, out_ref, local, spread, sems = refs
    start, wait = row_fetch(first, slots, plan, sources, local, spread, sems)
    columns = lax.axis_size("vec")
    column = lax.axis_index("vec")
    task_of = lambda step: (step // columns) * columns + (lax.rem(step, columns) ^ column)
    slot = streamed(start, wait, task_of)
    out_ref[0] = lax.dot_general(local[slot], spread[slot], ACROSS, preferred_element_type=jnp.float32)


def ladder_kernel(first, slots, begin, plan, *refs):
    sources, refs = refs[:BLOCKS], refs[BLOCKS:]
    amp_ref, before_ref, order_ref, *outs, local, spread, amps, integral, sems, amp_sems = refs
    start_rows, wait_rows = row_fetch(first, slots, plan, sources, local, spread, sems)
    step = pl.program_id(0)
    column = lax.axis_index("vec")
    holders, each, amp_rows = amp_ref.shape[1:4]

    def start(task, slot):
        start_rows(task, slot)
        for holder in range(holders):
            target = amps.at[slot, pl.ds(holder * amp_rows, amp_rows)]
            source = amp_ref.at[task // each, holder, lax.rem(task, each)]
            pltpu.make_async_copy(source, target, amp_sems.at[slot, holder]).start()

    def wait(slot):
        wait_rows(slot)
        for holder in range(holders):
            target = amps.at[slot, pl.ds(holder * amp_rows, amp_rows)]
            pltpu.make_async_copy(amp_ref.at[0, 0, 0], target, amp_sems.at[slot, holder]).wait()

    slot = streamed(start, wait, lambda step: begin + (step ^ column))
    products = before_ref[0] + lax.dot_general(
        local[slot], spread[slot], ACROSS, preferred_element_type=jnp.float32
    )
    ordered = jnp.dot(order_ref[...], products.astype(jnp.bfloat16), preferred_element_type=jnp.float32)
    quarter = ordered.shape[0] // 4
    group = ordered.shape[0] // VB
    for high in range(VB // 4):
        for wide_block in range(ordered.shape[1] // LANES):
            lanes = slice(wide_block * LANES, (wide_block + 1) * LANES)
            blocks = [
                ordered[low * quarter + high * group : low * quarter + (high + 1) * group, lanes]
                for low in range(4)
            ]
            for low, block in enumerate(swap_fours(blocks)):
                at = (wide_block * 4 + low) * group
                integral[at : at + group, high * LANES : (high + 1) * LANES] = block.astype(jnp.bfloat16)
    term = lax.dot_general(amps[slot], integral[...], ACROSS, preferred_element_type=jnp.float32)
    for which, out in enumerate(outs):

        @pl.when(step == which)
        def _():
            out[...] = term.astype(jnp.bfloat16)


def row_order(rows):
    new = np.arange(rows)
    group = rows // VB
    low, high, place = new // (rows // 4), new // group % (VB // 4), new % group
    old = place * VB + high * 4 + low
    return (jnp.arange(rows)[None, :] == jnp.asarray(old, jnp.int32)[:, None]).astype(jnp.bfloat16)


ANY = pl.BlockSpec(memory_space=pl.ANY)


def partial_products(first, slots, tasks, plan, blocks):
    rows, depth = blocks[0].shape[1:]
    side = 4 * rows
    return pl.pallas_call(
        functools.partial(partial_kernel, first, slots),
        out_shape=jax.ShapeDtypeStruct((tasks, side, side), jnp.float32),
        grid_spec=pltpu.PrefetchScalarGridSpec(
            num_scalar_prefetch=1,
            grid=(tasks,),
            in_specs=[ANY] * BLOCKS,
            out_specs=pl.BlockSpec((1, side, side), lambda step, plan: (step, 0, 0)),
            scratch_shapes=[
                pltpu.VMEM((2, side, depth), jnp.bfloat16),
                pltpu.VMEM((2, side, depth), jnp.bfloat16),
                pltpu.SemaphoreType.DMA((2, 8)),
            ],
        ),
        compiler_params=pltpu.CompilerParams(vmem_limit_bytes=VMEM),
        cost_estimate=pl.CostEstimate(
            flops=tasks * 2 * side * side * depth,
            bytes_accessed=tasks * 4 * (side * depth + side * side),
            transcendentals=0,
        ),
        name="partial",
    )(plan, *blocks)


def ladder(first, slots, begin, plan, blocks, amps, before, order):
    rows, depth = blocks[0].shape[1:]
    columns = lax.axis_size("vec")
    _, holders, _, amp_rows, pairs = amps.shape
    occupied = holders * amp_rows
    side = 4 * rows
    terms = (side // VB) ** 2
    return pl.pallas_call(
        functools.partial(ladder_kernel, first, slots, begin),
        out_shape=[jax.ShapeDtypeStruct((occupied, terms), jnp.bfloat16)] * columns,
        grid_spec=pltpu.PrefetchScalarGridSpec(
            num_scalar_prefetch=1,
            grid=(columns,),
            in_specs=[ANY] * (BLOCKS + 1)
            + [
                pl.BlockSpec((1, side, side), lambda step, plan: (begin + step, 0, 0)),
                pl.BlockSpec((side, side), lambda step, plan: (0, 0)),
            ],
            out_specs=[pl.BlockSpec((occupied, terms), lambda step, plan: (0, 0))] * columns,
            scratch_shapes=[
                pltpu.VMEM((2, side, depth), jnp.bfloat16),
                pltpu.VMEM((2, side, depth), jnp.bfloat16),
                pltpu.VMEM((2, occupied, pairs), jnp.bfloat16),
                pltpu.VMEM((terms, pairs), jnp.bfloat16),
                pltpu.SemaphoreType.DMA((2, 8)),
                pltpu.SemaphoreType.DMA((2, holders)),
            ],
        ),
        compiler_params=pltpu.CompilerParams(vmem_limit_bytes=VMEM),
        cost_estimate=pl.CostEstimate(
            flops=columns * 2 * (side * side * depth + side**3 + occupied * terms * pairs),
            bytes_accessed=columns * (4 * (side * depth + side * side) + 2 * occupied * pairs),
            transcendentals=0,
        ),
        name="ladder",
    )(plan, *blocks, amps, before, order)


def routes():
    last = CHIPS - 1
    feed = [(0, 1), (last, last - 1)]
    middle = [(1, 2), (2, 1)]
    both = lambda hops: [(a * CORES + c, b * CORES + c) for a, b in hops for c in range(CORES)]
    sibling = [(a * CORES + c, a * CORES + 1 - c) for a in range(CHIPS) for c in range(CORES)]
    return both(feed), both(middle), sibling


def swap_columns(array, bit, columns):
    return lax.ppermute(array, "vec", perm=[(column, column ^ bit) for column in range(columns)])


def gathered_amps(amplitudes, named):
    each = named["amp"].shape[0] // lax.axis_size("vec")
    column = lax.axis_index("vec")
    part = lambda name: lax.dynamic_slice_in_dim(named[name], column * each, each)
    mine = jnp.take(amplitudes, part("amp"), axis=0, mode="clip")
    turned = mine.reshape(*mine.shape[:2], VB, VB).swapaxes(2, 3).reshape(mine.shape)
    mine = jnp.where(part("swap")[:, None, None] == 1, turned, mine)
    line = lax.all_gather(mine, "amp", axis=0, tiled=False)
    return lax.all_gather(line, "vec", axis=0, tiled=False)


def products(first, slots, tiles, chol, amplitudes, plan, named):
    feed, middle, sibling = routes()
    send = functools.partial(lax.ppermute, axis_name="amp")
    start = first["order"]
    own_a = collect(start, slots, PARTS, plan, chol)
    fed_a = [send(rows, perm=feed) for rows in own_a]
    mid_a = [send(rows, perm=middle) for rows in own_a]
    own_b = collect(start + slots, min(2 * slots, tiles) - slots, PARTS, plan, chol)
    amps = gathered_amps(amplitudes, named)
    sib_a = [send(rows, perm=sibling) for rows in own_a]
    sib_b = [send(rows, perm=sibling) for rows in own_b]
    own_b, fed_a = lax.optimization_barrier((own_b, fed_a))
    mid_b = [send(rows, perm=middle) for rows in fed_a]
    fed_b = [send(rows, perm=feed) for rows in own_b]
    sfed_a = [send(rows, perm=sibling) for rows in fed_a]
    sfed_b = [send(rows, perm=sibling) for rows in fed_b]
    chunks = list(zip(own_a, own_b, sib_a, sib_b, fed_a, fed_b, sfed_a, sfed_b, mid_a, mid_b))
    columns = lax.axis_size("vec")
    tasks = named["amp"].shape[0]
    before = partial_products(first, slots, tasks, plan, chunks[0])
    order = row_order(4 * chol.shape[1])
    halves = []
    for begin in range(0, tasks, columns):
        terms = ladder(first, slots, begin, plan, chunks[1], amps, before, order)
        arrived = [terms[0]] + [swap_columns(terms[bit], bit, columns) for bit in range(1, columns)]
        halves.append(sum(term.astype(jnp.float32) for term in arrived).astype(jnp.bfloat16))
    return jnp.stack(halves)


def target_columns():
    worker, wide, fine, low = np.meshgrid(
        np.arange(2 * CORES), np.arange(CHIPS), np.arange(4), np.arange(4 * VB // 8), indexing="ij"
    )
    core = worker % CORES
    chip = 1 + worker // CORES
    near = np.where(chip == 1, 0, CHIPS - 1)
    far = np.where(chip == 1, 2, 1)
    end = np.where(chip == 1, CHIPS - 1, 0)
    each = VB // (CHIPS * CORES)
    block = low // each
    local_chip = np.where(block < 2, chip, near)
    local_core = np.where(block % 2 == 0, core, 1 - core)
    local = (local_chip * CORES + local_core) * each + low % each
    spread_chip = np.choose(wide, [chip, near, far, end])
    spread = (spread_chip * CORES + core) * each + fine
    return local.reshape(-1), spread.reshape(-1)


def scatter_terms(terms, named, tiles):
    columns = lax.axis_size("vec")
    column = lax.axis_index("vec")
    owners = lax.axis_size("amp")
    halves, rows, width = terms.shape
    each = rows // owners
    mine = terms.reshape(halves, owners, each, width).swapaxes(0, 1)
    mine = lax.all_to_all(mine, "amp", split_axis=0, concat_axis=0, tiled=True)
    mine = mine[CORES : CORES * (CHIPS - 1)].transpose(1, 2, 0, 3).reshape(halves * each, PAIRS)
    local, spread = target_columns()
    canonical = jnp.arange(PAIRS, dtype=jnp.int32)[None, :]
    straight = (jnp.asarray(local * VB + spread, jnp.int32)[:, None] == canonical).astype(jnp.bfloat16)
    turned = (jnp.asarray(spread * VB + local, jnp.int32)[:, None] == canonical).astype(jnp.bfloat16)
    dot = functools.partial(jnp.dot, preferred_element_type=jnp.float32)
    straight, turned = dot(mine, straight), dot(mine, turned)
    swap = named["swap"].reshape(halves, columns)
    out = named["out"].reshape(halves, columns)
    swapped = jnp.repeat(lax.dynamic_index_in_dim(swap, column, 1), each, axis=0) == 1
    placed = jnp.where(swapped, turned, straight).astype(jnp.bfloat16).reshape(halves, each, PAIRS)
    held = tiles // columns
    here = column * held + jnp.arange(held, dtype=jnp.int32)
    total = jnp.zeros((held, each, PAIRS), jnp.float32)
    for bit in range(columns):
        arrived = placed if bit == 0 else swap_columns(placed, bit, columns)
        targets = lax.dynamic_index_in_dim(out, column ^ bit, 1, keepdims=False)
        for half in range(halves):
            named_here = (here == targets[half])[:, None, None]
            total = total + jnp.where(named_here, arrived[half].astype(jnp.float32)[None], 0.0)
    return total.astype(jnp.bfloat16)


def line_local(chol, amplitudes, task_list, counts):
    tasks = lax.axis_size("amp")
    tiles = chol.shape[0]
    plan, named = make_plan(tasks, tiles, task_list, counts)
    first = {name: place[0] for name, place in plan_layout(tasks, tiles)[0].items()}
    sizes = [tasks // 2, tasks // 2 + 1, tasks // 2 + 2, tasks]
    branch = functools.reduce(
        lambda total, size: total + (named["size"][0] > size).astype(jnp.int32), sizes[:-1], jnp.int32(0)
    )
    run = lambda slots: lambda: products(first, slots, tiles, chol, amplitudes, plan, named)
    terms = lax.switch(branch, [run(slots) for slots in sizes])
    return scatter_terms(terms, named, tiles)


def integral_tile(x_rows, y_rows):
    products = lax.dot_general(
        x_rows, y_rows, (((1,), (1,)), ((), ())), preferred_element_type=jnp.float32
    )
    return (
        products.reshape(VB, VB, VB, VB).transpose(0, 2, 1, 3).reshape(PAIRS, PAIRS).astype(jnp.bfloat16)
    )


def task_term(x_rows, y_rows, amp_rows):
    products = lax.dot_general(
        amp_rows, integral_tile(x_rows, y_rows), (((1,), (1,)), ((), ())), preferred_element_type=jnp.float32
    )
    return products.astype(jnp.bfloat16)


def spread_local(chol, amplitudes, task_list, counts):
    owners = lax.axis_size("amp")
    most = task_list.shape[0] // owners
    rank = jnp.arange(owners, dtype=jnp.int32)[:, None]
    offsets = jnp.cumsum(counts) - counts
    inside = (rank >= offsets) & (rank < offsets + counts)
    starts = jnp.arange(owners, dtype=jnp.int32) * most
    fields = task_list[jnp.sum(jnp.where(inside, starts + rank - offsets, 0), axis=1)]
    trade = functools.partial(lax.all_to_all, axis_name="amp", tiled=True)
    fetch = lambda array, which: trade(jnp.take(array, which, axis=0), split_axis=0, concat_axis=0).reshape(
        -1, array.shape[2]
    )
    term = task_term(fetch(chol, fields[:, 0]), fetch(chol, fields[:, 1]), fetch(amplitudes, fields[:, 2]))
    returned = trade(term.reshape(owners, -1, PAIRS), split_axis=0, concat_axis=0)
    tiles = amplitudes.shape[0]
    chosen = (jnp.arange(tiles, dtype=jnp.int32)[:, None] == fields[:, 3][None, :]).astype(jnp.bfloat16)
    summed = jnp.dot(chosen, returned.reshape(owners, -1), preferred_element_type=jnp.float32)
    summed = summed.reshape(tiles, -1, PAIRS)
    return lax.psum_scatter(summed, "vec", scatter_dimension=0, tiled=True).astype(jnp.bfloat16)


def solution(mesh):
    placed = (P(None, "amp", "vec"), P(None, "amp", None), P(), P())
    local = line_local if mesh.shape["amp"] == CHIPS * CORES else spread_local
    return jax.shard_map(
        local, mesh=mesh, in_specs=placed, out_specs=P("vec", "amp", None), check_vma=False
    )
```

```python
import functools

import jax
import jax.numpy as jnp
import numpy as np
from jax import lax
from jax.experimental import pallas as pl
from jax.experimental.pallas import tpu as pltpu
from jax.sharding import PartitionSpec as P

VB = 32
PAIRS = VB * VB
CORES = 2
CHIPS = 4
LANES = 128
VMEM = 60 * 1024 * 1024


def plan_layout(tasks, tiles):
    fields = {}
    at = 0
    for name, size in (("order", tiles), ("local", tasks), ("spread", tasks), ("amp", tasks),
                       ("out", tasks), ("swap", tasks), ("size", 1)):
        fields[name] = (at, size)
        at += size
    return fields, at


def popcount(bits):
    bits = bits - ((bits >> 1) & 0x55555555)
    bits = (bits & 0x33333333) + ((bits >> 2) & 0x33333333)
    bits = (bits + (bits >> 4)) & 0x0F0F0F0F
    return (bits + (bits >> 8) + (bits >> 16) + (bits >> 24)) & 0xFF


def plan_kernel(tasks, tiles, most, task_ref, count_ref, plan_ref, work):
    fields, _ = plan_layout(tasks, tiles)
    first = {name: place[0] for name, place in fields.items()}
    at = jnp.int32(0)
    for owner in range(count_ref.shape[0]):
        for entry in range(most):
            live = entry < count_ref[owner]

            @pl.when(live)
            def _():
                for column in range(4):
                    work[at * 4 + column] = task_ref[owner * most + entry, column]

            at = at + live.astype(jnp.int32)
    x = [work[task * 4] for task in range(tasks)]
    y = [work[task * 4 + 1] for task in range(tasks)]
    one = jnp.int32(1)
    codes = 1 << tasks
    code = lax.broadcasted_iota(jnp.int32, (codes // LANES, LANES), 0) * LANES + lax.broadcasted_iota(
        jnp.int32, (codes // LANES, LANES), 1
    )
    bits = jnp.zeros_like(code)
    used = jnp.int32(0)
    for task in range(tasks):
        bits = bits | jnp.where((code >> task) & 1 == 1, one << y[task], one << x[task])
        used = used | (one << y[task]) | (one << x[task])
    best = jnp.min(popcount(bits) * codes + code) & (codes - 1)
    cover = jnp.int32(0)
    for task in range(tasks):
        cover = cover | (one << jnp.where((best >> task) & 1 == 1, y[task], x[task]))
    place = jnp.int32(0)
    sizes = []
    for group in (cover, used & ~cover, ~used):
        for tile in range(tiles):
            member = (group >> tile) & 1 == 1

            @pl.when(member)
            def _():
                plan_ref[first["order"] + place] = jnp.int32(tile)
                work[4 * tasks + tile] = place

            place = place + member.astype(jnp.int32)
        sizes.append(place)
    plan_ref[first["size"]] = jnp.maximum(sizes[0], (sizes[1] + 1) // 2)
    for task in range(tasks):
        swap = (best >> task) & 1 == 0
        plan_ref[first["local"] + task] = work[4 * tasks + jnp.where(swap, y[task], x[task])]
        plan_ref[first["spread"] + task] = work[4 * tasks + jnp.where(swap, x[task], y[task])]
        plan_ref[first["amp"] + task] = work[task * 4 + 2]
        plan_ref[first["out"] + task] = work[task * 4 + 3]
        plan_ref[first["swap"] + task] = swap.astype(jnp.int32)


def make_plan(tasks, tiles, task_list, counts):
    fields, length = plan_layout(tasks, tiles)
    most = task_list.shape[0] // counts.shape[0]
    plan = pl.pallas_call(
        functools.partial(plan_kernel, tasks, tiles, most),
        out_shape=jax.ShapeDtypeStruct((length,), jnp.int32),
        in_specs=[pl.BlockSpec(memory_space=pltpu.SMEM)] * 2,
        out_specs=pl.BlockSpec(memory_space=pltpu.SMEM),
        scratch_shapes=[pltpu.SMEM((4 * tasks + tiles,), jnp.int32)],
        name="plan",
    )(task_list, counts)
    return plan, {name: plan[at : at + size] for name, (at, size) in fields.items()}


def collect_kernel(plan, rows_ref, out_ref):
    out_ref[...] = rows_ref[...]


def collect(first, slots, plan, chol):
    _, rows, depth = chol.shape
    return pl.pallas_call(
        collect_kernel,
        out_shape=jax.ShapeDtypeStruct((slots, rows, depth), chol.dtype),
        grid_spec=pltpu.PrefetchScalarGridSpec(
            num_scalar_prefetch=1,
            grid=(slots,),
            in_specs=[pl.BlockSpec((1, rows, depth), lambda slot, plan: (plan[first + slot], 0, 0))],
            out_specs=pl.BlockSpec((1, rows, depth), lambda slot, plan: (slot, 0, 0)),
        ),
        compiler_params=pltpu.CompilerParams(vmem_limit_bytes=VMEM),
        name="collect",
    )(plan, chol)


def swap_fours(blocks):
    group = lax.broadcasted_iota(jnp.int32, blocks[0].shape, 1) // VB
    for bit in (1, 2):
        right = (group & bit) != 0
        shift = bit * VB
        moved = list(blocks)
        for low in range(4):
            if low & bit:
                continue
            high = low | bit
            moved[low] = jnp.where(right, pltpu.roll(blocks[high], shift, 1), blocks[low])
            moved[high] = jnp.where(right, blocks[high], pltpu.roll(blocks[low], LANES - shift, 1))
        blocks = moved
    return blocks


ACROSS = (((1,), (1,)), ((), ()))
SOURCES = 10


def ladder_kernel(first, plan, *refs):
    sources, refs = refs[:SOURCES], refs[SOURCES:]
    amp_ref, order_ref, *outs, own, sib, fed, sfed, mid_a, mid_b, amps, integral, sems = refs
    slots = mid_a.shape[0]
    copies = []
    for which, held in enumerate((own, sib, fed, sfed)):
        early, late = sources[2 * which : 2 * which + 2]
        copies.append((early, held.at[pl.ds(0, slots)]))
        copies.append((late, held.at[pl.ds(slots, late.shape[0])]))
    copies += [(sources[8], mid_a), (sources[9], mid_b), (amp_ref, amps)]
    copies = [pltpu.make_async_copy(*pair, sems.at[at]) for at, pair in enumerate(copies)]
    for copy in copies:
        copy.start()
    for copy in copies:
        copy.wait()

    column = lax.axis_index("vec")
    columns = len(outs)
    each = amps.shape[2]
    pairs = amps.shape[4]
    for step in range(columns):

        def one(half, carry):
            task = half * columns + (step ^ column)
            at = plan[first["local"] + task]
            to = plan[first["spread"] + task]
            local = jnp.concatenate([held[at] for held in (own, sib, fed, sfed)])
            spread = jnp.concatenate([held[to] for held in (own, fed, mid_a, mid_b)])
            products = lax.dot_general(local, spread, ACROSS, preferred_element_type=jnp.float32)
            ordered = jnp.dot(
                order_ref[...], products.astype(jnp.bfloat16), preferred_element_type=jnp.float32
            )
            quarter = ordered.shape[0] // 4
            group = ordered.shape[0] // VB
            for high in range(VB // 4):
                for wide in range(ordered.shape[1] // LANES):
                    lanes = slice(wide * LANES, (wide + 1) * LANES)
                    begins = [low * quarter + high * group for low in range(4)]
                    blocks = swap_fours([ordered[begin : begin + group, lanes] for begin in begins])
                    for low, block in enumerate(blocks):
                        to_rows = slice((wide * 4 + low) * group, (wide * 4 + low + 1) * group)
                        integral[to_rows, high * LANES : (high + 1) * LANES] = block.astype(jnp.bfloat16)
            rows = amps[task // each, :, lax.rem(task, each)].reshape(-1, pairs)
            term = lax.dot_general(rows, integral[...], ACROSS, preferred_element_type=jnp.float32)
            outs[step][half] = term.astype(jnp.bfloat16)
            return carry

        lax.fori_loop(0, outs[step].shape[0], one, 0)


def row_order(rows):
    new = np.arange(rows)
    group = rows // VB
    low, high, place = new // (rows // 4), new // group % (VB // 4), new % group
    old = place * VB + high * 4 + low
    return (jnp.arange(rows)[None, :] == jnp.asarray(old, jnp.int32)[:, None]).astype(jnp.bfloat16)


def ladder(first, plan, blocks, amps, order):
    rows, depth = blocks[0].shape[1:]
    slots = blocks[0].shape[0]
    held = slots + blocks[1].shape[0]
    columns, holders, each, amp_rows, pairs = amps.shape
    occupied = holders * amp_rows
    side = 4 * rows
    terms = (side // VB) ** 2
    tasks = columns * each
    whole = pl.BlockSpec(memory_space=pltpu.VMEM)
    return pl.pallas_call(
        functools.partial(ladder_kernel, first),
        out_shape=[jax.ShapeDtypeStruct((each, occupied, terms), jnp.bfloat16)] * columns,
        in_specs=[pl.BlockSpec(memory_space=pltpu.SMEM)]
        + [pl.BlockSpec(memory_space=pl.ANY)] * (SOURCES + 1)
        + [whole],
        out_specs=[whole] * columns,
        scratch_shapes=[pltpu.VMEM((held, rows, depth), jnp.bfloat16)] * 4
        + [pltpu.VMEM((slots, rows, depth), jnp.bfloat16)] * 2
        + [
            pltpu.VMEM(amps.shape, jnp.bfloat16),
            pltpu.VMEM((terms, pairs), jnp.bfloat16),
            pltpu.SemaphoreType.DMA((SOURCES + 1,)),
        ],
        compiler_params=pltpu.CompilerParams(vmem_limit_bytes=VMEM),
        cost_estimate=pl.CostEstimate(
            flops=tasks * 2 * (side * side * depth + side**3 + occupied * terms * pairs),
            bytes_accessed=2 * rows * depth * (4 * held + 2 * slots) + 2 * tasks * occupied * pairs,
            transcendentals=0,
        ),
        name="ladder",
    )(plan, *blocks, amps, order)


def routes():
    last = CHIPS - 1
    feed = [(0, 1), (last, last - 1)]
    middle = [(1, 2), (2, 1)]
    both = lambda hops: [(a * CORES + c, b * CORES + c) for a, b in hops for c in range(CORES)]
    sibling = [(a * CORES + c, a * CORES + 1 - c) for a in range(CHIPS) for c in range(CORES)]
    return both(feed), both(middle), sibling


def swap_columns(array, bit, columns):
    return lax.ppermute(array, "vec", perm=[(column, column ^ bit) for column in range(columns)])


def column_amps(amplitudes, named):
    each = named["amp"].shape[0] // lax.axis_size("vec")
    column = lax.axis_index("vec")
    part = lambda name: lax.dynamic_slice_in_dim(named[name], column * each, each)
    mine = jnp.take(amplitudes, part("amp"), axis=0, mode="clip")
    turned = mine.reshape(*mine.shape[:2], VB, VB).swapaxes(2, 3).reshape(mine.shape)
    return jnp.where(part("swap")[:, None, None] == 1, turned, mine)


def products(first, slots, tiles, chol, amplitudes, plan, named):
    feed, middle, sibling = routes()
    send = functools.partial(lax.ppermute, axis_name="amp")
    gather = functools.partial(lax.all_gather, axis=0, tiled=False)
    start = first["order"]
    own_a = collect(start, slots, plan, chol)
    fed_a = send(own_a, perm=feed)
    mid_a = send(own_a, perm=middle)
    own_b = collect(start + slots, min(2 * slots, tiles) - slots, plan, chol)
    amps = gather(column_amps(amplitudes, named), "amp")
    sib_a = send(own_a, perm=sibling)
    sib_b = send(own_b, perm=sibling)
    own_b, fed_a, mid_a, sib_a, sib_b, amps = lax.optimization_barrier(
        (own_b, fed_a, mid_a, sib_a, sib_b, amps)
    )
    mid_b = send(fed_a, perm=middle)
    fed_b = send(own_b, perm=feed)
    sfed_a = send(fed_a, perm=sibling)
    amps = gather(amps, "vec")
    sfed_b = send(fed_b, perm=sibling)
    blocks = (own_a, own_b, sib_a, sib_b, fed_a, fed_b, sfed_a, sfed_b, mid_a, mid_b)
    columns = lax.axis_size("vec")
    terms = ladder(first, plan, blocks, amps, row_order(4 * chol.shape[1]))
    arrived = [terms[0]] + [swap_columns(terms[bit], bit, columns) for bit in range(1, columns)]
    return sum(term.astype(jnp.float32) for term in arrived).astype(jnp.bfloat16)


def target_columns():
    worker, wide, fine, low = np.meshgrid(
        np.arange(2 * CORES), np.arange(CHIPS), np.arange(4), np.arange(4 * VB // 8), indexing="ij"
    )
    core = worker % CORES
    chip = 1 + worker // CORES
    near = np.where(chip == 1, 0, CHIPS - 1)
    far = np.where(chip == 1, 2, 1)
    end = np.where(chip == 1, CHIPS - 1, 0)
    each = VB // (CHIPS * CORES)
    block = low // each
    local_chip = np.where(block < 2, chip, near)
    local_core = np.where(block % 2 == 0, core, 1 - core)
    local = (local_chip * CORES + local_core) * each + low % each
    spread_chip = np.choose(wide, [chip, near, far, end])
    spread = (spread_chip * CORES + core) * each + fine
    return local.reshape(-1), spread.reshape(-1)


def scatter_terms(terms, named, tiles):
    columns = lax.axis_size("vec")
    column = lax.axis_index("vec")
    owners = lax.axis_size("amp")
    halves, rows, width = terms.shape
    each = rows // owners
    mine = terms.reshape(halves, owners, each, width).swapaxes(0, 1)
    mine = lax.all_to_all(mine, "amp", split_axis=0, concat_axis=0, tiled=True)
    mine = mine[CORES : CORES * (CHIPS - 1)].transpose(1, 2, 0, 3).reshape(halves * each, PAIRS)
    local, spread = target_columns()
    canonical = jnp.arange(PAIRS, dtype=jnp.int32)[None, :]
    straight = (jnp.asarray(local * VB + spread, jnp.int32)[:, None] == canonical).astype(jnp.bfloat16)
    turned = (jnp.asarray(spread * VB + local, jnp.int32)[:, None] == canonical).astype(jnp.bfloat16)
    dot = functools.partial(jnp.dot, preferred_element_type=jnp.float32)
    straight, turned = dot(mine, straight), dot(mine, turned)
    swap = named["swap"].reshape(halves, columns)
    out = named["out"].reshape(halves, columns)
    swapped = jnp.repeat(lax.dynamic_index_in_dim(swap, column, 1), each, axis=0) == 1
    placed = jnp.where(swapped, turned, straight).astype(jnp.bfloat16).reshape(halves, each, PAIRS)
    held = tiles // columns
    here = column * held + jnp.arange(held, dtype=jnp.int32)
    total = jnp.zeros((held, each, PAIRS), jnp.float32)
    for bit in range(columns):
        arrived = placed if bit == 0 else swap_columns(placed, bit, columns)
        targets = lax.dynamic_index_in_dim(out, column ^ bit, 1, keepdims=False)
        for half in range(halves):
            named_here = (here == targets[half])[:, None, None]
            total = total + jnp.where(named_here, arrived[half].astype(jnp.float32)[None], 0.0)
    return total.astype(jnp.bfloat16)


def line_local(chol, amplitudes, task_list, counts):
    tasks = lax.axis_size("amp")
    tiles = chol.shape[0]
    plan, named = make_plan(tasks, tiles, task_list, counts)
    first = {name: place[0] for name, place in plan_layout(tasks, tiles)[0].items()}
    sizes = [tasks // 2, tasks // 2 + 1, tasks // 2 + 2, tasks]
    branch = functools.reduce(
        lambda total, size: total + (named["size"][0] > size).astype(jnp.int32), sizes[:-1], jnp.int32(0)
    )
    run = lambda slots: lambda: products(first, slots, tiles, chol, amplitudes, plan, named)
    terms = lax.switch(branch, [run(slots) for slots in sizes])
    return scatter_terms(terms, named, tiles)


def integral_tile(x_rows, y_rows):
    products = lax.dot_general(
        x_rows, y_rows, (((1,), (1,)), ((), ())), preferred_element_type=jnp.float32
    )
    return (
        products.reshape(VB, VB, VB, VB).transpose(0, 2, 1, 3).reshape(PAIRS, PAIRS).astype(jnp.bfloat16)
    )


def task_term(x_rows, y_rows, amp_rows):
    products = lax.dot_general(
        amp_rows, integral_tile(x_rows, y_rows), (((1,), (1,)), ((), ())), preferred_element_type=jnp.float32
    )
    return products.astype(jnp.bfloat16)


def spread_local(chol, amplitudes, task_list, counts):
    owners = lax.axis_size("amp")
    most = task_list.shape[0] // owners
    rank = jnp.arange(owners, dtype=jnp.int32)[:, None]
    offsets = jnp.cumsum(counts) - counts
    inside = (rank >= offsets) & (rank < offsets + counts)
    starts = jnp.arange(owners, dtype=jnp.int32) * most
    fields = task_list[jnp.sum(jnp.where(inside, starts + rank - offsets, 0), axis=1)]
    trade = functools.partial(lax.all_to_all, axis_name="amp", tiled=True)
    fetch = lambda array, which: trade(jnp.take(array, which, axis=0), split_axis=0, concat_axis=0).reshape(
        -1, array.shape[2]
    )
    term = task_term(fetch(chol, fields[:, 0]), fetch(chol, fields[:, 1]), fetch(amplitudes, fields[:, 2]))
    returned = trade(term.reshape(owners, -1, PAIRS), split_axis=0, concat_axis=0)
    tiles = amplitudes.shape[0]
    chosen = (jnp.arange(tiles, dtype=jnp.int32)[:, None] == fields[:, 3][None, :]).astype(jnp.bfloat16)
    summed = jnp.dot(chosen, returned.reshape(owners, -1), preferred_element_type=jnp.float32)
    summed = summed.reshape(tiles, -1, PAIRS)
    return lax.psum_scatter(summed, "vec", scatter_dimension=0, tiled=True).astype(jnp.bfloat16)


def solution(mesh):
    placed = (P(None, "amp", "vec"), P(None, "amp", None), P(), P())
    local = line_local if mesh.shape["amp"] == CHIPS * CORES else spread_local
    return jax.shard_map(
        local, mesh=mesh, in_specs=placed, out_specs=P("vec", "amp", None), check_vma=False
    )
```

```python
import functools

import jax
import jax.numpy as jnp
import numpy as np
from jax import lax
from jax.experimental import pallas as pl
from jax.experimental.pallas import tpu as pltpu
from jax.sharding import PartitionSpec as P

VB = 32
PAIRS = VB * VB
CORES = 2
CHIPS = 4
LANES = 128
VMEM = 60 * 1024 * 1024
SMALL_VMEM = 20 * 1024 * 1024


def plan_layout(tasks, tiles):
    fields = {}
    at = 0
    for name, size in (("order", tiles), ("local", tasks), ("spread", tasks), ("amp", tasks),
                       ("out", tasks), ("swap", tasks), ("size", 1)):
        fields[name] = (at, size)
        at += size
    return fields, at


def popcount(bits):
    bits = bits - ((bits >> 1) & 0x55555555)
    bits = (bits & 0x33333333) + ((bits >> 2) & 0x33333333)
    bits = (bits + (bits >> 4)) & 0x0F0F0F0F
    return (bits + (bits >> 8) + (bits >> 16) + (bits >> 24)) & 0xFF


def plan_kernel(tasks, tiles, most, task_ref, count_ref, plan_ref, work):
    fields, _ = plan_layout(tasks, tiles)
    first = {name: place[0] for name, place in fields.items()}
    at = jnp.int32(0)
    for owner in range(count_ref.shape[0]):
        for entry in range(most):
            live = entry < count_ref[owner]

            @pl.when(live)
            def _():
                for column in range(4):
                    work[at * 4 + column] = task_ref[owner * most + entry, column]

            at = at + live.astype(jnp.int32)
    x = [work[task * 4] for task in range(tasks)]
    y = [work[task * 4 + 1] for task in range(tasks)]
    one = jnp.int32(1)
    codes = 1 << tasks
    code = lax.broadcasted_iota(jnp.int32, (codes // LANES, LANES), 0) * LANES + lax.broadcasted_iota(
        jnp.int32, (codes // LANES, LANES), 1
    )
    bits = jnp.zeros_like(code)
    used = jnp.int32(0)
    for task in range(tasks):
        bits = bits | jnp.where((code >> task) & 1 == 1, one << y[task], one << x[task])
        used = used | (one << y[task]) | (one << x[task])
    best = jnp.min(popcount(bits) * codes + code) & (codes - 1)
    cover = jnp.int32(0)
    for task in range(tasks):
        cover = cover | (one << jnp.where((best >> task) & 1 == 1, y[task], x[task]))
    place = jnp.int32(0)
    sizes = []
    for group in (cover, used & ~cover, ~used):
        for tile in range(tiles):
            member = (group >> tile) & 1 == 1

            @pl.when(member)
            def _():
                plan_ref[first["order"] + place] = jnp.int32(tile)
                work[4 * tasks + tile] = place

            place = place + member.astype(jnp.int32)
        sizes.append(place)
    plan_ref[first["size"]] = jnp.maximum(sizes[0], (sizes[1] + 1) // 2)
    for task in range(tasks):
        swap = (best >> task) & 1 == 0
        plan_ref[first["local"] + task] = work[4 * tasks + jnp.where(swap, y[task], x[task])]
        plan_ref[first["spread"] + task] = work[4 * tasks + jnp.where(swap, x[task], y[task])]
        plan_ref[first["amp"] + task] = work[task * 4 + 2]
        plan_ref[first["out"] + task] = work[task * 4 + 3]
        plan_ref[first["swap"] + task] = swap.astype(jnp.int32)


def make_plan(tasks, tiles, task_list, counts):
    fields, length = plan_layout(tasks, tiles)
    most = task_list.shape[0] // counts.shape[0]
    plan = pl.pallas_call(
        functools.partial(plan_kernel, tasks, tiles, most),
        out_shape=jax.ShapeDtypeStruct((length,), jnp.int32),
        in_specs=[pl.BlockSpec(memory_space=pltpu.SMEM)] * 2,
        out_specs=pl.BlockSpec(memory_space=pltpu.SMEM),
        scratch_shapes=[pltpu.SMEM((4 * tasks + tiles,), jnp.int32)],
        name="plan",
    )(task_list, counts)
    return plan, {name: plan[at : at + size] for name, (at, size) in fields.items()}


def collect_kernel(first, plan, chol, out, held, sems):
    slots = range(out.shape[0])
    loads = [pltpu.make_async_copy(chol.at[plan[first + at]], held.at[at], sems.at[0, at]) for at in slots]
    stores = [pltpu.make_async_copy(held.at[at], out.at[at], sems.at[1, at]) for at in slots]
    for load in loads:
        load.start()
    for load, store in zip(loads, stores):
        load.wait()
        store.start()
    for store in stores:
        store.wait()


def collect(first, slots, plan, chol):
    shape = (slots, *chol.shape[1:])
    return pl.pallas_call(
        functools.partial(collect_kernel, first),
        out_shape=jax.ShapeDtypeStruct(shape, chol.dtype),
        in_specs=[pl.BlockSpec(memory_space=pltpu.SMEM), pl.BlockSpec(memory_space=pl.ANY)],
        out_specs=pl.BlockSpec(memory_space=pl.ANY),
        scratch_shapes=[pltpu.VMEM(shape, chol.dtype), pltpu.SemaphoreType.DMA((2, slots))],
        compiler_params=pltpu.CompilerParams(vmem_limit_bytes=VMEM),
        name="collect",
    )(plan, chol)


def swap_fours(blocks):
    group = lax.broadcasted_iota(jnp.int32, blocks[0].shape, 1) // VB
    for bit in (1, 2):
        right = (group & bit) != 0
        shift = bit * VB
        moved = list(blocks)
        for low in range(4):
            if low & bit:
                continue
            high = low | bit
            moved[low] = jnp.where(right, pltpu.roll(blocks[high], shift, 1), blocks[low])
            moved[high] = jnp.where(right, blocks[high], pltpu.roll(blocks[low], LANES - shift, 1))
        blocks = moved
    return blocks


ACROSS = (((1,), (1,)), ((), ()))
SOURCES = 10


def ladder_kernel(first, slots, plan, *refs):
    sources, refs = refs[:SOURCES], refs[SOURCES:]
    amp_own, amp_sib, order_ref, *outs, rows, amps, integral, sems = refs
    own_a, own_b, sib_a, sib_b, fed_a, fed_b, sfed_a, sfed_b, mid_a, mid_b = sources
    pairs = ((own_a, own_b), (sib_a, sib_b), (fed_a, fed_b), (sfed_a, sfed_b))
    wide = (own_a, fed_a, mid_a, mid_b)
    each_row = own_a.shape[1]
    each = amp_own.shape[2]
    step = pl.program_id(0)
    columns = len(outs)
    column = lax.axis_index("vec")
    core = lax.rem(lax.axis_index("amp"), CORES)
    task_of = lambda at: (at // columns) * columns + (lax.rem(at, columns) ^ column)
    part = lambda slot, side, block: rows.at[slot, side, pl.ds(block * each_row, each_row)]

    def amp_copies(task, slot):
        return [
            pltpu.make_async_copy(
                source.at[task // each, :, lax.rem(task, each)],
                amps.at[slot, :, holder],
                sems.at[slot, 2 * len(wide) + at],
            )
            for at, (source, holder) in enumerate(((amp_own, core), (amp_sib, 1 - core)))
        ]

    def start(task, slot):
        swap = plan[first["swap"] + task]
        at = plan[first["local"] + task]
        for block, (early, late) in enumerate(pairs):
            target, sem = part(slot, swap, block), sems.at[slot, block]

            @pl.when(at < slots)
            def _():
                pltpu.make_async_copy(early.at[at], target, sem).start()

            @pl.when(at >= slots)
            def _():
                pltpu.make_async_copy(late.at[at - slots], target, sem).start()

        at = plan[first["spread"] + task]
        for block, source in enumerate(wide):
            target, sem = part(slot, 1 - swap, block), sems.at[slot, len(wide) + block]
            pltpu.make_async_copy(source.at[at], target, sem).start()
        for copy in amp_copies(task, slot):
            copy.start()

    def wait(task, slot):
        swap = plan[first["swap"] + task]
        for block in range(len(wide)):
            for side, at in ((swap, block), (1 - swap, len(wide) + block)):
                pltpu.make_async_copy(own_a.at[0], part(slot, side, block), sems.at[slot, at]).wait()
        for copy in amp_copies(task, slot):
            copy.wait()

    @pl.when(step == 0)
    def _():
        start(task_of(0), 0)

    @pl.when(step + 1 < pl.num_programs(0))
    def _():
        start(task_of(step + 1), lax.rem(step + 1, 2))

    slot = lax.rem(step, 2)
    wait(task_of(step), slot)
    products = lax.dot_general(rows[slot, 0], rows[slot, 1], ACROSS, preferred_element_type=jnp.float32)
    ordered = jnp.dot(order_ref[...], products.astype(jnp.bfloat16), preferred_element_type=jnp.float32)
    quarter = ordered.shape[0] // 4
    group = ordered.shape[0] // VB
    for high in range(VB // 4):
        for block in range(ordered.shape[1] // LANES):
            lanes = slice(block * LANES, (block + 1) * LANES)
            begins = [low * quarter + high * group for low in range(4)]
            blocks = swap_fours([ordered[begin : begin + group, lanes] for begin in begins])
            for low, moved in enumerate(blocks):
                to = (block * 4 + low) * group
                integral[to : to + group, high * LANES : (high + 1) * LANES] = moved.astype(jnp.bfloat16)
    mine = amps[slot].reshape(-1, amps.shape[-1])
    term = lax.dot_general(mine, integral[...], ACROSS, preferred_element_type=jnp.float32)
    for bit, out in enumerate(outs):

        @pl.when(lax.rem(step, columns) == bit)
        def _():
            out[0] = term.astype(jnp.bfloat16)


def row_order(rows):
    new = np.arange(rows)
    group = rows // VB
    low, high, place = new // (rows // 4), new // group % (VB // 4), new % group
    old = place * VB + high * 4 + low
    return (jnp.arange(rows)[None, :] == jnp.asarray(old, jnp.int32)[:, None]).astype(jnp.bfloat16)


def ladder(first, plan, blocks, amps, order):
    slots, rows, depth = blocks[0].shape
    columns, chips, each, amp_rows, pairs = amps[0].shape
    occupied = chips * CORES * amp_rows
    side = 4 * rows
    terms = (side // VB) ** 2
    tasks = columns * each
    return pl.pallas_call(
        functools.partial(ladder_kernel, first, slots),
        out_shape=[jax.ShapeDtypeStruct((each, occupied, terms), jnp.bfloat16)] * columns,
        grid_spec=pltpu.PrefetchScalarGridSpec(
            num_scalar_prefetch=1,
            grid=(tasks,),
            in_specs=[pl.BlockSpec(memory_space=pl.ANY)] * (SOURCES + len(amps))
            + [pl.BlockSpec((side, side), lambda step, plan: (0, 0))],
            out_specs=[pl.BlockSpec((1, occupied, terms), lambda step, plan: (step // columns, 0, 0))] * columns,
            scratch_shapes=[
                pltpu.VMEM((2, 2, side, depth), jnp.bfloat16),
                pltpu.VMEM((2, chips, CORES, amp_rows, pairs), jnp.bfloat16),
                pltpu.VMEM((terms, pairs), jnp.bfloat16),
                pltpu.SemaphoreType.DMA((2, 10)),
            ],
        ),
        compiler_params=pltpu.CompilerParams(vmem_limit_bytes=SMALL_VMEM),
        cost_estimate=pl.CostEstimate(
            flops=tasks * 2 * (side * side * depth + side**3 + occupied * terms * pairs),
            bytes_accessed=tasks * 2 * (2 * side * depth + occupied * pairs),
            transcendentals=0,
        ),
        name="ladder",
    )(plan, *blocks, *amps, order)


def routes():
    last = CHIPS - 1
    feed = [(0, 1), (last, last - 1)]
    middle = [(1, 2), (2, 1)]
    both = lambda hops: [(a * CORES + c, b * CORES + c) for a, b in hops for c in range(CORES)]
    sibling = [(a * CORES + c, a * CORES + 1 - c) for a in range(CHIPS) for c in range(CORES)]
    return both(feed), both(middle), sibling


def swap_columns(array, bit, columns):
    return lax.ppermute(array, "vec", perm=[(column, column ^ bit) for column in range(columns)])


def column_amps(amplitudes, named):
    each = named["amp"].shape[0] // lax.axis_size("vec")
    mine = lax.dynamic_slice_in_dim(named["amp"], lax.axis_index("vec") * each, each)
    return jnp.take(amplitudes, mine, axis=0, mode="clip")


def line_amps(near, other):
    upper = lax.axis_index("amp") >= CHIPS * CORES // 2
    return jnp.where(
        upper, jnp.concatenate([other, near[::-1]]), jnp.concatenate([near, other[::-1]])
    )


def products(first, slots, tiles, chol, amplitudes, plan, named):
    feed, middle, sibling = routes()
    send = functools.partial(lax.ppermute, axis_name="amp")
    start = first["order"]
    mine = column_amps(amplitudes, named)
    end = send(mine, perm=feed)
    own_a = collect(start, slots, plan, chol)
    own_a, end, mine, chol = lax.optimization_barrier((own_a, end, mine, chol))
    near = jnp.stack([end, mine])
    other = send(near, perm=middle)
    fed_a = send(own_a, perm=feed)
    mid_a = send(own_a, perm=middle)
    own_b = collect(start + slots, min(2 * slots, tiles) - slots, plan, chol)
    sib_a = send(own_a, perm=sibling)
    sib_b = send(own_b, perm=sibling)
    own_b, fed_a, mid_a, sib_a, sib_b, near, other = lax.optimization_barrier(
        (own_b, fed_a, mid_a, sib_a, sib_b, near, other)
    )
    mid_b = send(fed_a, perm=middle)
    fed_b = send(own_b, perm=feed)
    sfed_a = send(fed_a, perm=sibling)
    amps = lax.all_gather(line_amps(near, other), "vec", axis=0, tiled=False)
    amps = (amps, send(amps, perm=sibling))
    sfed_b = send(fed_b, perm=sibling)
    blocks = (own_a, own_b, sib_a, sib_b, fed_a, fed_b, sfed_a, sfed_b, mid_a, mid_b)
    columns = lax.axis_size("vec")
    terms = ladder(first, plan, blocks, amps, row_order(4 * chol.shape[1]))
    arrived = [terms[0]] + [swap_columns(terms[bit], bit, columns) for bit in range(1, columns)]
    return sum(term.astype(jnp.float32) for term in arrived).astype(jnp.bfloat16)


def target_columns(swap):
    worker, right, left = np.meshgrid(
        np.arange(2 * CORES), np.arange(VB // 2), np.arange(VB // 2), indexing="ij"
    )
    core = worker % CORES
    chip = 1 + worker // CORES
    near = np.where(chip == 1, 0, CHIPS - 1)
    far = np.where(chip == 1, 2, 1)
    end = np.where(chip == 1, CHIPS - 1, 0)
    each = VB // (CHIPS * CORES)

    def local(at):
        block = at // each
        home = np.where(block < 2, chip, near) * CORES + np.where(block % 2 == 0, core, 1 - core)
        return home * each + at % each

    def spread(at):
        return (np.choose(at // each, [chip, near, far, end]) * CORES + core) * each + at % each

    a, b = (spread(left), local(right)) if swap else (local(left), spread(right))
    return (a * VB + b).reshape(-1)


def scatter_terms(terms, named, tiles):
    columns = lax.axis_size("vec")
    column = lax.axis_index("vec")
    owners = lax.axis_size("amp")
    halves, rows, width = terms.shape
    each = rows // owners
    mine = terms.reshape(halves, owners, each, width).swapaxes(0, 1)
    mine = lax.all_to_all(mine, "amp", split_axis=0, concat_axis=0, tiled=True)
    mine = mine[CORES : CORES * (CHIPS - 1)].transpose(1, 2, 0, 3).reshape(halves * each, PAIRS)
    canonical = jnp.arange(PAIRS, dtype=jnp.int32)[None, :]
    one_hot = lambda to: (jnp.asarray(to, jnp.int32)[:, None] == canonical).astype(jnp.bfloat16)
    straight, turned = one_hot(target_columns(False)), one_hot(target_columns(True))
    dot = functools.partial(jnp.dot, preferred_element_type=jnp.float32)
    straight, turned = dot(mine, straight), dot(mine, turned)
    swap = named["swap"].reshape(halves, columns)
    out = named["out"].reshape(halves, columns)
    swapped = jnp.repeat(lax.dynamic_index_in_dim(swap, column, 1), each, axis=0) == 1
    placed = jnp.where(swapped, turned, straight).astype(jnp.bfloat16).reshape(halves, each, PAIRS)
    held = tiles // columns
    here = column * held + jnp.arange(held, dtype=jnp.int32)
    total = jnp.zeros((held, each, PAIRS), jnp.float32)
    for bit in range(columns):
        arrived = placed if bit == 0 else swap_columns(placed, bit, columns)
        targets = lax.dynamic_index_in_dim(out, column ^ bit, 1, keepdims=False)
        for half in range(halves):
            named_here = (here == targets[half])[:, None, None]
            total = total + jnp.where(named_here, arrived[half].astype(jnp.float32)[None], 0.0)
    return total.astype(jnp.bfloat16)


def line_local(chol, amplitudes, task_list, counts):
    tasks = lax.axis_size("amp")
    tiles = chol.shape[0]
    plan, named = make_plan(tasks, tiles, task_list, counts)
    first = {name: place[0] for name, place in plan_layout(tasks, tiles)[0].items()}
    sizes = [tasks // 2, tasks // 2 + 1, tasks // 2 + 2, tasks]
    branch = functools.reduce(
        lambda total, size: total + (named["size"][0] > size).astype(jnp.int32), sizes[:-1], jnp.int32(0)
    )
    run = lambda slots: lambda: products(first, slots, tiles, chol, amplitudes, plan, named)
    terms = lax.switch(branch, [run(slots) for slots in sizes])
    return scatter_terms(terms, named, tiles)


def integral_tile(x_rows, y_rows):
    products = lax.dot_general(
        x_rows, y_rows, (((1,), (1,)), ((), ())), preferred_element_type=jnp.float32
    )
    return (
        products.reshape(VB, VB, VB, VB).transpose(0, 2, 1, 3).reshape(PAIRS, PAIRS).astype(jnp.bfloat16)
    )


def task_term(x_rows, y_rows, amp_rows):
    products = lax.dot_general(
        amp_rows, integral_tile(x_rows, y_rows), (((1,), (1,)), ((), ())), preferred_element_type=jnp.float32
    )
    return products.astype(jnp.bfloat16)


def spread_local(chol, amplitudes, task_list, counts):
    owners = lax.axis_size("amp")
    most = task_list.shape[0] // owners
    rank = jnp.arange(owners, dtype=jnp.int32)[:, None]
    offsets = jnp.cumsum(counts) - counts
    inside = (rank >= offsets) & (rank < offsets + counts)
    starts = jnp.arange(owners, dtype=jnp.int32) * most
    fields = task_list[jnp.sum(jnp.where(inside, starts + rank - offsets, 0), axis=1)]
    trade = functools.partial(lax.all_to_all, axis_name="amp", tiled=True)
    fetch = lambda array, which: trade(jnp.take(array, which, axis=0), split_axis=0, concat_axis=0).reshape(
        -1, array.shape[2]
    )
    term = task_term(fetch(chol, fields[:, 0]), fetch(chol, fields[:, 1]), fetch(amplitudes, fields[:, 2]))
    returned = trade(term.reshape(owners, -1, PAIRS), split_axis=0, concat_axis=0)
    tiles = amplitudes.shape[0]
    chosen = (jnp.arange(tiles, dtype=jnp.int32)[:, None] == fields[:, 3][None, :]).astype(jnp.bfloat16)
    summed = jnp.dot(chosen, returned.reshape(owners, -1), preferred_element_type=jnp.float32)
    summed = summed.reshape(tiles, -1, PAIRS)
    return lax.psum_scatter(summed, "vec", scatter_dimension=0, tiled=True).astype(jnp.bfloat16)


def solution(mesh):
    placed = (P(None, "amp", "vec"), P(None, "amp", None), P(), P())
    local = line_local if mesh.shape["amp"] == CHIPS * CORES else spread_local
    return jax.shard_map(
        local, mesh=mesh, in_specs=placed, out_specs=P("vec", "amp", None), check_vma=False
    )
```

```python
import functools

import jax
import jax.numpy as jnp
import numpy as np
from jax import lax
from jax.experimental import pallas as pl
from jax.experimental.pallas import tpu as pltpu
from jax.sharding import PartitionSpec as P

VB = 32
PAIRS = VB * VB
CORES = 2
CHIPS = 4
LANES = 128
VMEM = 60 * 1024 * 1024
SMALL_VMEM = 14 * 1024 * 1024
SPARE_VMEM = 8 * 1024 * 1024


def plan_layout(tasks, tiles):
    fields = {}
    at = 0
    for name, size in (("order", tiles), ("local", tasks), ("spread", tasks), ("amp", tasks),
                       ("out", tasks), ("swap", tasks), ("size", 1)):
        fields[name] = (at, size)
        at += size
    return fields, at


def popcount(bits):
    bits = bits - ((bits >> 1) & 0x55555555)
    bits = (bits & 0x33333333) + ((bits >> 2) & 0x33333333)
    bits = (bits + (bits >> 4)) & 0x0F0F0F0F
    return (bits + (bits >> 8) + (bits >> 16) + (bits >> 24)) & 0xFF


def plan_kernel(tasks, tiles, most, task_ref, count_ref, plan_ref, work):
    fields, _ = plan_layout(tasks, tiles)
    first = {name: place[0] for name, place in fields.items()}
    at = jnp.int32(0)
    for owner in range(count_ref.shape[0]):
        for entry in range(most):
            live = entry < count_ref[owner]

            @pl.when(live)
            def _():
                for column in range(4):
                    work[at * 4 + column] = task_ref[owner * most + entry, column]

            at = at + live.astype(jnp.int32)
    x = [work[task * 4] for task in range(tasks)]
    y = [work[task * 4 + 1] for task in range(tasks)]
    one = jnp.int32(1)
    codes = 1 << tasks
    code = lax.broadcasted_iota(jnp.int32, (codes // LANES, LANES), 0) * LANES + lax.broadcasted_iota(
        jnp.int32, (codes // LANES, LANES), 1
    )
    bits = jnp.zeros_like(code)
    used = jnp.int32(0)
    for task in range(tasks):
        bits = bits | jnp.where((code >> task) & 1 == 1, one << y[task], one << x[task])
        used = used | (one << y[task]) | (one << x[task])
    best = jnp.min(popcount(bits) * codes + code) & (codes - 1)
    cover = jnp.int32(0)
    for task in range(tasks):
        cover = cover | (one << jnp.where((best >> task) & 1 == 1, y[task], x[task]))
    place = jnp.int32(0)
    sizes = []
    for group in (cover, used & ~cover, ~used):
        for tile in range(tiles):
            member = (group >> tile) & 1 == 1

            @pl.when(member)
            def _():
                plan_ref[first["order"] + place] = jnp.int32(tile)
                work[4 * tasks + tile] = place

            place = place + member.astype(jnp.int32)
        sizes.append(place)
    plan_ref[first["size"]] = jnp.maximum(sizes[0], (sizes[1] + 1) // 2)
    for task in range(tasks):
        swap = (best >> task) & 1 == 0
        plan_ref[first["local"] + task] = work[4 * tasks + jnp.where(swap, y[task], x[task])]
        plan_ref[first["spread"] + task] = work[4 * tasks + jnp.where(swap, x[task], y[task])]
        plan_ref[first["amp"] + task] = work[task * 4 + 2]
        plan_ref[first["out"] + task] = work[task * 4 + 3]
        plan_ref[first["swap"] + task] = swap.astype(jnp.int32)


def make_plan(tasks, tiles, task_list, counts):
    fields, length = plan_layout(tasks, tiles)
    most = task_list.shape[0] // counts.shape[0]
    plan = pl.pallas_call(
        functools.partial(plan_kernel, tasks, tiles, most),
        out_shape=jax.ShapeDtypeStruct((length,), jnp.int32),
        in_specs=[pl.BlockSpec(memory_space=pltpu.SMEM)] * 2,
        out_specs=pl.BlockSpec(memory_space=pltpu.SMEM),
        scratch_shapes=[pltpu.SMEM((4 * tasks + tiles,), jnp.int32)],
        name="plan",
    )(task_list, counts)
    return plan, {name: plan[at : at + size] for name, (at, size) in fields.items()}


def collect_kernel(first, plan, chol, out, held, sems):
    slots = range(out.shape[0])
    loads = [pltpu.make_async_copy(chol.at[plan[first + at]], held.at[at], sems.at[0, at]) for at in slots]
    stores = [pltpu.make_async_copy(held.at[at], out.at[at], sems.at[1, at]) for at in slots]
    for load in loads:
        load.start()
    for load, store in zip(loads, stores):
        load.wait()
        store.start()
    for store in stores:
        store.wait()


def collect(first, slots, plan, chol):
    shape = (slots, *chol.shape[1:])
    return pl.pallas_call(
        functools.partial(collect_kernel, first),
        out_shape=jax.ShapeDtypeStruct(shape, chol.dtype),
        in_specs=[pl.BlockSpec(memory_space=pltpu.SMEM), pl.BlockSpec(memory_space=pl.ANY)],
        out_specs=pl.BlockSpec(memory_space=pl.ANY),
        scratch_shapes=[pltpu.VMEM(shape, chol.dtype), pltpu.SemaphoreType.DMA((2, slots))],
        compiler_params=pltpu.CompilerParams(vmem_limit_bytes=VMEM),
        name="collect",
    )(plan, chol)


def stage_kernel(*refs):
    *pairs, sems = refs
    half = len(pairs) // 2
    copies = [
        pltpu.make_async_copy(source, out, sems.at[at])
        for at, (source, out) in enumerate(zip(pairs[:half], pairs[half:]))
    ]
    for copy in copies:
        copy.start()
    for copy in copies:
        copy.wait()


def stage(*arrays):
    out = pl.pallas_call(
        stage_kernel,
        out_shape=[pltpu.VMEM(array.shape, array.dtype) for array in arrays],
        in_specs=[pl.BlockSpec(memory_space=pl.ANY)] * len(arrays),
        out_specs=[pl.BlockSpec(memory_space=pltpu.VMEM)] * len(arrays),
        scratch_shapes=[pltpu.SemaphoreType.DMA((len(arrays),))],
        compiler_params=pltpu.CompilerParams(vmem_limit_bytes=SPARE_VMEM),
        cost_estimate=pl.CostEstimate(
            flops=0, bytes_accessed=4 * sum(array.size for array in arrays), transcendentals=0
        ),
        name="stage",
    )(*arrays)
    return list(out)


def swap_fours(blocks):
    group = lax.broadcasted_iota(jnp.int32, blocks[0].shape, 1) // VB
    for bit in (1, 2):
        right = (group & bit) != 0
        shift = bit * VB
        moved = list(blocks)
        for low in range(4):
            if low & bit:
                continue
            high = low | bit
            moved[low] = jnp.where(right, pltpu.roll(blocks[high], shift, 1), blocks[low])
            moved[high] = jnp.where(right, blocks[high], pltpu.roll(blocks[low], LANES - shift, 1))
        blocks = moved
    return blocks


ACROSS = (((1,), (1,)), ((), ()))
SOURCES = 10


def ladder_kernel(first, resident, bits, plan, *refs):
    sources, refs = refs[:SOURCES], refs[SOURCES:]
    amp_own, amp_sib, order_ref, *outs, rows, integral, sems = refs
    own_a, own_b, sib_a, sib_b, fed_a, fed_b, sfed_a, sfed_b, mid_a, mid_b = sources
    pairs = ((own_a, own_b), (sib_a, sib_b), (fed_a, fed_b), (sfed_a, sfed_b))
    wide = (own_a, fed_a, mid_a, mid_b)
    slots, each_row, _ = own_a.shape
    columns, _, each, _, width = amp_own.shape
    column = lax.axis_index("vec")
    odd = lax.rem(lax.axis_index("amp"), CORES) == 1
    dot = functools.partial(lax.dot_general, preferred_element_type=jnp.float32)

    def fill(source, at, side, here, sem):
        if resident:
            rows[side, here] = source[at]
        else:
            pltpu.make_async_copy(source.at[at], rows.at[side, here], sems.at[sem]).start()

    def one(at_step, carry):
        which, half = at_step // each, lax.rem(at_step, each)
        bit = bits[0] if len(bits) == 1 else jnp.where(which == 0, *bits)
        task = half * columns + (column ^ bit)
        swap = plan[first["swap"] + task]
        at = plan[first["local"] + task]
        to = plan[first["spread"] + task]
        for block, (early, late) in enumerate(pairs):
            here = pl.ds(block * each_row, each_row)
            fill(wide[block], to, 1 - swap, here, len(pairs) + block)

            @pl.when(at < slots)
            def _():
                fill(early, at, swap, here, block)

            @pl.when(at >= slots)
            def _():
                fill(late, at - slots, swap, here, block)

        if not resident:
            for block in range(len(pairs)):
                here = pl.ds(block * each_row, each_row)
                for side, sem in ((swap, block), (1 - swap, len(pairs) + block)):
                    pltpu.make_async_copy(own_a.at[0], rows.at[side, here], sems.at[sem]).wait()

        products = dot(rows[0], rows[1], ACROSS).astype(jnp.bfloat16)
        ordered = jnp.dot(order_ref[...], products, preferred_element_type=jnp.float32)
        quarter = ordered.shape[0] // 4
        group = ordered.shape[0] // VB
        for high in range(VB // 4):
            for block in range(ordered.shape[1] // LANES):
                lanes = slice(block * LANES, (block + 1) * LANES)
                begins = [low * quarter + high * group for low in range(4)]
                blocks = swap_fours([ordered[begin : begin + group, lanes] for begin in begins])
                for low, moved in enumerate(blocks):
                    to_row = (block * 4 + low) * group
                    integral[to_row : to_row + group, high * LANES : (high + 1) * LANES] = moved.astype(
                        jnp.bfloat16
                    )
        mine = [amp[task // each, :, lax.rem(task, each)] for amp in (amp_own, amp_sib)]
        even = [jnp.where(odd, mine[1 - core], mine[core]) for core in range(CORES)]
        amps = jnp.stack(even, axis=1).reshape(-1, width)
        term = dot(amps, integral[...], ACROSS).astype(jnp.bfloat16)
        for to_out, out in enumerate(outs):

            @pl.when(which == to_out)
            def _():
                out[half] = term

        return carry

    lax.fori_loop(0, len(bits) * each, one, None)


def row_order(rows):
    new = np.arange(rows)
    group = rows // VB
    low, high, place = new // (rows // 4), new // group % (VB // 4), new % group
    old = place * VB + high * 4 + low
    return (jnp.arange(rows)[None, :] == jnp.asarray(old, jnp.int32)[:, None]).astype(jnp.bfloat16)


def ladder(first, bits, resident, plan, blocks, amps, order):
    _, rows, depth = blocks[0].shape
    columns, chips, each, amp_rows, pairs = amps[0].shape
    occupied = chips * CORES * amp_rows
    side = 4 * rows
    terms = (side // VB) ** 2
    tasks = len(bits) * each
    whole = pl.BlockSpec(memory_space=pltpu.VMEM)
    source = whole if resident else pl.BlockSpec(memory_space=pl.ANY)
    return pl.pallas_call(
        functools.partial(ladder_kernel, first, resident, bits),
        out_shape=[jax.ShapeDtypeStruct((each, occupied, terms), jnp.bfloat16)] * len(bits),
        in_specs=[pl.BlockSpec(memory_space=pltpu.SMEM)] + [source] * SOURCES + [whole] * (len(amps) + 1),
        out_specs=[whole] * len(bits),
        scratch_shapes=[
            pltpu.VMEM((2, side, depth), jnp.bfloat16),
            pltpu.VMEM((terms, pairs), jnp.bfloat16),
            pltpu.SemaphoreType.DMA((8,)),
        ],
        compiler_params=pltpu.CompilerParams(vmem_limit_bytes=SMALL_VMEM),
        cost_estimate=pl.CostEstimate(
            flops=tasks * 2 * (side * side * depth + side**3 + occupied * terms * pairs),
            bytes_accessed=tasks * 2 * occupied * terms,
            transcendentals=0,
        ),
        name="ladder",
    )(plan, *blocks, *amps, order)


def routes():
    last = CHIPS - 1
    feed = [(0, 1), (last, last - 1)]
    middle = [(1, 2), (2, 1)]
    both = lambda hops: [(a * CORES + c, b * CORES + c) for a, b in hops for c in range(CORES)]
    sibling = [(a * CORES + c, a * CORES + 1 - c) for a in range(CHIPS) for c in range(CORES)]
    return both(feed), both(middle), sibling


def swap_columns(array, bit, columns):
    return lax.ppermute(array, "vec", perm=[(column, column ^ bit) for column in range(columns)])


def column_amps(amplitudes, named):
    each = named["amp"].shape[0] // lax.axis_size("vec")
    mine = lax.dynamic_slice_in_dim(named["amp"], lax.axis_index("vec") * each, each)
    return jnp.take(amplitudes, mine, axis=0, mode="clip")


def line_amps(near, other):
    upper = lax.axis_index("amp") >= CHIPS * CORES // 2
    return jnp.where(
        upper, jnp.concatenate([other, near[::-1]]), jnp.concatenate([near, other[::-1]])
    )


def products(first, slots, tiles, chol, amplitudes, plan, named):
    feed, middle, sibling = routes()
    send = functools.partial(lax.ppermute, axis_name="amp")
    start = first["order"]
    mine = column_amps(amplitudes, named)
    end = send(mine, perm=feed)
    own_a = collect(start, slots, plan, chol)
    own_a, end, mine, chol = lax.optimization_barrier((own_a, end, mine, chol))
    near = jnp.stack([end, mine])
    other = send(near, perm=middle)
    fed_a = send(own_a, perm=feed)
    mid_a = send(own_a, perm=middle)
    own_b = collect(start + slots, min(2 * slots, tiles) - slots, plan, chol)
    sib_a = send(own_a, perm=sibling)
    sib_b = send(own_b, perm=sibling)
    own_b, fed_a, mid_a, sib_a, sib_b, near, other = lax.optimization_barrier(
        (own_b, fed_a, mid_a, sib_a, sib_b, near, other)
    )
    mid_b = send(fed_a, perm=middle)
    fed_b = send(own_b, perm=feed)
    sfed_a = send(fed_a, perm=sibling)
    amps = lax.all_gather(line_amps(near, other), "vec", axis=0, tiled=False)
    amps = (amps, send(amps, perm=sibling))
    sfed_b = send(fed_b, perm=sibling)
    held = 2 * (10 * own_a.size + 2 * amps[0].size)
    resident = held + SMALL_VMEM < VMEM - SPARE_VMEM
    if resident:
        own_a, own_b, sib_a, sib_b, fed_a, mid_a = stage(own_a, own_b, sib_a, sib_b, fed_a, mid_a)
        (sfed_a,) = stage(sfed_a)
        (fed_b,) = stage(fed_b)
        (mid_b,) = stage(mid_b)
        (sfed_b,) = stage(sfed_b)
    blocks = (own_a, own_b, sib_a, sib_b, fed_a, fed_b, sfed_a, sfed_b, mid_a, mid_b)
    columns = lax.axis_size("vec")
    order = row_order(4 * chol.shape[1])
    bits = list(range(columns))
    calls = [bits[: 0 : -2], bits[2 : 0 : -2], bits[:1]]
    arrived = []
    for call in calls:
        for bit, term in zip(call, ladder(first, call, resident, plan, blocks, amps, order)):
            arrived.append(swap_columns(term, bit, columns) if bit else term)
    return sum(term.astype(jnp.float32) for term in arrived).astype(jnp.bfloat16)


def target_columns(swap):
    worker, right, left = np.meshgrid(
        np.arange(2 * CORES), np.arange(VB // 2), np.arange(VB // 2), indexing="ij"
    )
    core = worker % CORES
    chip = 1 + worker // CORES
    near = np.where(chip == 1, 0, CHIPS - 1)
    far = np.where(chip == 1, 2, 1)
    end = np.where(chip == 1, CHIPS - 1, 0)
    each = VB // (CHIPS * CORES)

    def local(at):
        block = at // each
        home = np.where(block < 2, chip, near) * CORES + np.where(block % 2 == 0, core, 1 - core)
        return home * each + at % each

    def spread(at):
        return (np.choose(at // each, [chip, near, far, end]) * CORES + core) * each + at % each

    a, b = (spread(left), local(right)) if swap else (local(left), spread(right))
    return (a * VB + b).reshape(-1)


def scatter_terms(terms, named, tiles):
    columns = lax.axis_size("vec")
    column = lax.axis_index("vec")
    owners = lax.axis_size("amp")
    halves, rows, width = terms.shape
    each = rows // owners
    mine = terms.reshape(halves, owners, each, width).swapaxes(0, 1)
    mine = lax.all_to_all(mine, "amp", split_axis=0, concat_axis=0, tiled=True)
    mine = mine[CORES : CORES * (CHIPS - 1)].transpose(1, 2, 0, 3).reshape(halves * each, PAIRS)
    canonical = jnp.arange(PAIRS, dtype=jnp.int32)[None, :]
    one_hot = lambda to: (jnp.asarray(to, jnp.int32)[:, None] == canonical).astype(jnp.bfloat16)
    straight, turned = one_hot(target_columns(False)), one_hot(target_columns(True))
    dot = functools.partial(jnp.dot, preferred_element_type=jnp.float32)
    straight, turned = dot(mine, straight), dot(mine, turned)
    swap = named["swap"].reshape(halves, columns)
    out = named["out"].reshape(halves, columns)
    swapped = jnp.repeat(lax.dynamic_index_in_dim(swap, column, 1), each, axis=0) == 1
    placed = jnp.where(swapped, turned, straight).astype(jnp.bfloat16).reshape(halves, each, PAIRS)
    held = tiles // columns
    here = column * held + jnp.arange(held, dtype=jnp.int32)
    total = jnp.zeros((held, each, PAIRS), jnp.float32)
    for bit in range(columns):
        arrived = placed if bit == 0 else swap_columns(placed, bit, columns)
        targets = lax.dynamic_index_in_dim(out, column ^ bit, 1, keepdims=False)
        for half in range(halves):
            named_here = (here == targets[half])[:, None, None]
            total = total + jnp.where(named_here, arrived[half].astype(jnp.float32)[None], 0.0)
    return total.astype(jnp.bfloat16)


def line_local(chol, amplitudes, task_list, counts):
    tasks = lax.axis_size("amp")
    tiles = chol.shape[0]
    plan, named = make_plan(tasks, tiles, task_list, counts)
    first = {name: place[0] for name, place in plan_layout(tasks, tiles)[0].items()}
    sizes = [tasks // 2, tasks // 2 + 1, tasks // 2 + 2, tasks]
    branch = functools.reduce(
        lambda total, size: total + (named["size"][0] > size).astype(jnp.int32), sizes[:-1], jnp.int32(0)
    )
    run = lambda slots: lambda: products(first, slots, tiles, chol, amplitudes, plan, named)
    terms = lax.switch(branch, [run(slots) for slots in sizes])
    return scatter_terms(terms, named, tiles)


def integral_tile(x_rows, y_rows):
    products = lax.dot_general(
        x_rows, y_rows, (((1,), (1,)), ((), ())), preferred_element_type=jnp.float32
    )
    return (
        products.reshape(VB, VB, VB, VB).transpose(0, 2, 1, 3).reshape(PAIRS, PAIRS).astype(jnp.bfloat16)
    )


def task_term(x_rows, y_rows, amp_rows):
    products = lax.dot_general(
        amp_rows, integral_tile(x_rows, y_rows), (((1,), (1,)), ((), ())), preferred_element_type=jnp.float32
    )
    return products.astype(jnp.bfloat16)


def spread_local(chol, amplitudes, task_list, counts):
    owners = lax.axis_size("amp")
    most = task_list.shape[0] // owners
    rank = jnp.arange(owners, dtype=jnp.int32)[:, None]
    offsets = jnp.cumsum(counts) - counts
    inside = (rank >= offsets) & (rank < offsets + counts)
    starts = jnp.arange(owners, dtype=jnp.int32) * most
    fields = task_list[jnp.sum(jnp.where(inside, starts + rank - offsets, 0), axis=1)]
    trade = functools.partial(lax.all_to_all, axis_name="amp", tiled=True)
    fetch = lambda array, which: trade(jnp.take(array, which, axis=0), split_axis=0, concat_axis=0).reshape(
        -1, array.shape[2]
    )
    term = task_term(fetch(chol, fields[:, 0]), fetch(chol, fields[:, 1]), fetch(amplitudes, fields[:, 2]))
    returned = trade(term.reshape(owners, -1, PAIRS), split_axis=0, concat_axis=0)
    tiles = amplitudes.shape[0]
    chosen = (jnp.arange(tiles, dtype=jnp.int32)[:, None] == fields[:, 3][None, :]).astype(jnp.bfloat16)
    summed = jnp.dot(chosen, returned.reshape(owners, -1), preferred_element_type=jnp.float32)
    summed = summed.reshape(tiles, -1, PAIRS)
    return lax.psum_scatter(summed, "vec", scatter_dimension=0, tiled=True).astype(jnp.bfloat16)


def solution(mesh):
    placed = (P(None, "amp", "vec"), P(None, "amp", None), P(), P())
    local = line_local if mesh.shape["amp"] == CHIPS * CORES else spread_local
    return jax.shard_map(
        local, mesh=mesh, in_specs=placed, out_specs=P("vec", "amp", None), check_vma=False
    )
```

```python
import functools

import jax
import jax.numpy as jnp
import numpy as np
from jax import lax
from jax.experimental import pallas as pl
from jax.experimental.pallas import tpu as pltpu
from jax.sharding import PartitionSpec as P

VB = 32
PAIRS = VB * VB
CORES = 2
CHIPS = 4
LANES = 128
VMEM = 60 * 1024 * 1024
SMALL_VMEM = 20 * 1024 * 1024


def plan_layout(tasks, tiles):
    fields = {}
    at = 0
    for name, size in (("order", tiles), ("local", tasks), ("spread", tasks), ("amp", tasks),
                       ("out", tasks), ("swap", tasks)):
        fields[name] = (at, size)
        at += size
    return fields, at


def popcount(bits):
    bits = bits - ((bits >> 1) & 0x55555555)
    bits = (bits & 0x33333333) + ((bits >> 2) & 0x33333333)
    bits = (bits + (bits >> 4)) & 0x0F0F0F0F
    return (bits + (bits >> 8) + (bits >> 16) + (bits >> 24)) & 0xFF


def plan_kernel(tasks, tiles, most, classes, task_ref, count_ref, plan_ref, size_ref, work):
    fields, _ = plan_layout(tasks, tiles)
    first = {name: place[0] for name, place in fields.items()}
    at = jnp.int32(0)
    for owner in range(count_ref.shape[0]):
        for entry in range(most):
            live = entry < count_ref[owner]

            @pl.when(live)
            def _():
                for column in range(4):
                    work[at * 4 + column] = task_ref[column, owner * most + entry]

            at = at + live.astype(jnp.int32)
    x = [work[task * 4] for task in range(tasks)]
    y = [work[task * 4 + 1] for task in range(tasks)]
    one = jnp.int32(1)
    codes = 1 << tasks
    code = lax.broadcasted_iota(jnp.int32, (codes // LANES, LANES), 0) * LANES + lax.broadcasted_iota(
        jnp.int32, (codes // LANES, LANES), 1
    )
    bits = jnp.zeros_like(code)
    used = jnp.int32(0)
    for task in range(tasks):
        bits = bits | jnp.where((code >> task) & 1 == 1, one << y[task], one << x[task])
        used = used | (one << y[task]) | (one << x[task])
    best = jnp.min(popcount(bits) * codes + code) & (codes - 1)
    cover = jnp.int32(0)
    for task in range(tasks):
        cover = cover | (one << jnp.where((best >> task) & 1 == 1, y[task], x[task]))
    place = jnp.int32(0)
    sizes = []
    for group in (cover, used & ~cover, ~used):
        for tile in range(tiles):
            member = (group >> tile) & 1 == 1

            @pl.when(member)
            def _():
                plan_ref[first["order"] + place] = jnp.int32(tile)
                work[4 * tasks + tile] = place

            place = place + member.astype(jnp.int32)
        sizes.append(place)
    size = jnp.maximum(sizes[0], (sizes[1] + 1) // 2)
    size_ref[0] = sum((size > limit).astype(jnp.int32) for limit in classes[:-1])
    for task in range(tasks):
        swap = (best >> task) & 1 == 0
        plan_ref[first["local"] + task] = work[4 * tasks + jnp.where(swap, y[task], x[task])]
        plan_ref[first["spread"] + task] = work[4 * tasks + jnp.where(swap, x[task], y[task])]
        plan_ref[first["amp"] + task] = work[task * 4 + 2]
        plan_ref[first["out"] + task] = work[task * 4 + 3]
        plan_ref[first["swap"] + task] = swap.astype(jnp.int32)


def make_plan(tasks, tiles, classes, task_list, counts):
    fields, length = plan_layout(tasks, tiles)
    most = task_list.shape[0] // counts.shape[0]
    smem = pl.BlockSpec(memory_space=pltpu.SMEM)
    plan, size = pl.pallas_call(
        functools.partial(plan_kernel, tasks, tiles, most, classes),
        out_shape=[jax.ShapeDtypeStruct((length,), jnp.int32), jax.ShapeDtypeStruct((1,), jnp.int32)],
        in_specs=[smem] * 2,
        out_specs=[smem] * 2,
        scratch_shapes=[pltpu.SMEM((4 * tasks + tiles,), jnp.int32)],
        name="plan",
    )(task_list.T, counts)
    return plan, {name: plan[at : at + held] for name, (at, held) in fields.items()}, size[0]


def collect_kernel(lists, plan, *refs):
    sources, refs = refs[: len(lists)], refs[len(lists) :]
    outs, refs = refs[: len(lists)], refs[len(lists) :]
    *held, sems = refs
    moves = []
    for (first, each), source, out, slot in zip(lists, sources, outs, held):
        begin = lax.axis_index("vec") * each + first
        moves += [(source.at[plan[begin + at]], slot.at[at], out.at[at]) for at in range(out.shape[0])]
    loads = [pltpu.make_async_copy(move[0], move[1], sems.at[0, at]) for at, move in enumerate(moves)]
    stores = [pltpu.make_async_copy(move[1], move[2], sems.at[1, at]) for at, move in enumerate(moves)]
    for load in loads:
        load.start()
    for load, store in zip(loads, stores):
        load.wait()
        store.start()
    for store in stores:
        store.wait()


def collect(plan, *wanted):
    shapes = [(count, *array.shape[1:]) for _, _, count, array in wanted]
    total = sum(shape[0] for shape in shapes)
    any_spec = pl.BlockSpec(memory_space=pl.ANY)
    return pl.pallas_call(
        functools.partial(collect_kernel, [want[:2] for want in wanted]),
        out_shape=[jax.ShapeDtypeStruct(shape, jnp.bfloat16) for shape in shapes],
        in_specs=[pl.BlockSpec(memory_space=pltpu.SMEM)] + [any_spec] * len(wanted),
        out_specs=[any_spec] * len(wanted),
        scratch_shapes=[pltpu.VMEM(shape, jnp.bfloat16) for shape in shapes]
        + [pltpu.SemaphoreType.DMA((2, total))],
        compiler_params=pltpu.CompilerParams(vmem_limit_bytes=VMEM),
        name="collect",
    )(plan, *[want[3] for want in wanted])


def swap_fours(blocks):
    group = lax.broadcasted_iota(jnp.int32, blocks[0].shape, 1) // VB
    for bit in (1, 2):
        right = (group & bit) != 0
        shift = bit * VB
        moved = list(blocks)
        for low in range(4):
            if low & bit:
                continue
            high = low | bit
            moved[low] = jnp.where(right, pltpu.roll(blocks[high], shift, 1), blocks[low])
            moved[high] = jnp.where(right, blocks[high], pltpu.roll(blocks[low], LANES - shift, 1))
        blocks = moved
    return blocks


ACROSS = (((1,), (1,)), ((), ()))
SOURCES = 10


def ladder_kernel(first, bits, plan, *refs):
    sources, refs = refs[:SOURCES], refs[SOURCES:]
    amp_own, amp_sib, *outs, rows, amps, products, integral, sems = refs
    own_a, own_b, sib_a, sib_b, fed_a, fed_b, sfed_a, sfed_b, mid_a, mid_b = sources
    pairs = ((own_a, own_b), (sib_a, sib_b), (fed_a, fed_b), (sfed_a, sfed_b))
    wide = (own_a, fed_a, mid_a, mid_b)
    slots, each_row, _ = own_a.shape
    each = amp_own.shape[2]
    step = pl.program_id(0)
    columns = amp_own.shape[0]
    column = lax.axis_index("vec")
    core = lax.rem(lax.axis_index("amp"), CORES)
    bit_of = lambda at: jnp.where(at // each == 0, *bits)
    task_of = lambda at: lax.rem(at, each) * columns + (bit_of(at) ^ column)
    part = lambda slot, side, block: rows.at[slot, side, pl.ds(block * each_row, each_row)]

    def amp_copies(task, slot):
        return [
            pltpu.make_async_copy(
                source.at[task // each, :, lax.rem(task, each)],
                amps.at[slot, :, holder],
                sems.at[slot, 2 * len(wide) + at],
            )
            for at, (source, holder) in enumerate(((amp_own, core), (amp_sib, 1 - core)))
        ]

    def start(task, slot):
        swap = plan[first["swap"] + task]
        at = plan[first["local"] + task]
        for block, (early, late) in enumerate(pairs):
            target, sem = part(slot, swap, block), sems.at[slot, block]

            @pl.when(at < slots)
            def _():
                pltpu.make_async_copy(early.at[at], target, sem).start()

            @pl.when(at >= slots)
            def _():
                pltpu.make_async_copy(late.at[at - slots], target, sem).start()

        at = plan[first["spread"] + task]
        for block, source in enumerate(wide):
            target, sem = part(slot, 1 - swap, block), sems.at[slot, len(wide) + block]
            pltpu.make_async_copy(source.at[at], target, sem).start()
        for copy in amp_copies(task, slot):
            copy.start()

    def wait(task, slot):
        swap = plan[first["swap"] + task]
        for block in range(len(wide)):
            for side, at in ((swap, block), (1 - swap, len(wide) + block)):
                pltpu.make_async_copy(own_a.at[0], part(slot, side, block), sems.at[slot, at]).wait()
        for copy in amp_copies(task, slot):
            copy.wait()

    @pl.when(step == 0)
    def _():
        start(task_of(0), 0)

    @pl.when(step + 1 < pl.num_programs(0))
    def _():
        start(task_of(step + 1), lax.rem(step + 1, 2))

    slot = lax.rem(step, 2)
    wait(task_of(step), slot)
    whole_products = lax.dot_general(
        rows[slot, 0], rows[slot, 1], ACROSS, preferred_element_type=jnp.float32
    )
    for block in range(products.shape[0]):
        products[block] = whole_products[:, block * LANES : (block + 1) * LANES]
    group = products.shape[1] // VB
    for high in range(VB // 4):
        for block in range(products.shape[0]):
            blocks = [products[block, pl.ds(high * 4 + low, group, VB)] for low in range(4)]
            for low, moved in enumerate(swap_fours(blocks)):
                to = (block * 4 + low) * group
                integral[to : to + group, high * LANES : (high + 1) * LANES] = moved.astype(jnp.bfloat16)
    mine = amps[slot].reshape(-1, amps.shape[-1])
    term = lax.dot_general(mine, integral[...], ACROSS, preferred_element_type=jnp.float32)
    for which, out in enumerate(outs):

        @pl.when(step // each == which)
        def _():
            out[0] = term.astype(jnp.bfloat16)


def ladder(first, bits, plan, blocks, amps):
    _, rows, depth = blocks[0].shape
    columns, chips, each, amp_rows, pairs = amps[0].shape
    occupied = chips * CORES * amp_rows
    side = 4 * rows
    terms = (side // VB) ** 2
    tasks = len(bits) * each

    def out_spec(which):
        half = lambda step: jnp.clip(step - which * each, 0, each - 1)
        return pl.BlockSpec((1, occupied, terms), lambda step, plan: (half(step), 0, 0))

    return pl.pallas_call(
        functools.partial(ladder_kernel, first, bits),
        out_shape=[jax.ShapeDtypeStruct((each, occupied, terms), jnp.bfloat16)] * len(bits),
        grid_spec=pltpu.PrefetchScalarGridSpec(
            num_scalar_prefetch=1,
            grid=(tasks,),
            in_specs=[pl.BlockSpec(memory_space=pl.ANY)] * (SOURCES + len(amps)),
            out_specs=[out_spec(which) for which in range(len(bits))],
            scratch_shapes=[
                pltpu.VMEM((2, 2, side, depth), jnp.bfloat16),
                pltpu.VMEM((2, chips, CORES, amp_rows, pairs), jnp.bfloat16),
                pltpu.VMEM((side // LANES, side, LANES), jnp.float32),
                pltpu.VMEM((terms, pairs), jnp.bfloat16),
                pltpu.SemaphoreType.DMA((2, 10)),
            ],
        ),
        compiler_params=pltpu.CompilerParams(vmem_limit_bytes=SMALL_VMEM),
        cost_estimate=pl.CostEstimate(
            flops=tasks * 2 * (side * side * depth + occupied * terms * pairs),
            bytes_accessed=tasks * 2 * (2 * side * depth + occupied * pairs),
            transcendentals=0,
        ),
        name="ladder",
    )(plan, *blocks, *amps)


def routes():
    last = CHIPS - 1
    feed = [(0, 1), (last, last - 1)]
    middle = [(1, 2), (2, 1)]
    both = lambda hops: [(a * CORES + c, b * CORES + c) for a, b in hops for c in range(CORES)]
    sibling = [(a * CORES + c, a * CORES + 1 - c) for a in range(CHIPS) for c in range(CORES)]
    return both(feed), both(middle), sibling


def swap_columns(array, bit, columns):
    return lax.ppermute(array, "vec", perm=[(column, column ^ bit) for column in range(columns)])


def line_amps(near, other):
    upper = lax.axis_index("amp") >= CHIPS * CORES // 2
    return jnp.where(
        upper, jnp.concatenate([other, near[::-1]]), jnp.concatenate([near, other[::-1]])
    )


def products(first, slots, tiles, chol, amplitudes, plan, each):
    feed, middle, sibling = routes()
    send = functools.partial(lax.ppermute, axis_name="amp")
    start = first["order"]
    listed = min(2 * slots, tiles)
    (mine,) = collect(plan, (first["amp"], each, each, amplitudes))
    end = send(mine, perm=feed)
    (own_a,) = collect(plan, (start, 0, slots, chol))
    own_a, end, mine, chol = lax.optimization_barrier((own_a, end, mine, chol))
    fed_a = send(own_a, perm=feed)
    mid_a = send(own_a, perm=middle)
    (own_b,) = collect(plan, (start + slots, 0, listed - slots, chol))
    sib_a = send(own_a, perm=sibling)
    sib_b = send(own_b, perm=sibling)
    near = jnp.stack([end, mine])
    other = send(near, perm=middle)
    own_b, fed_a, mid_a, sib_a, sib_b, near, other = lax.optimization_barrier(
        (own_b, fed_a, mid_a, sib_a, sib_b, near, other)
    )
    mid_b = send(fed_a, perm=middle)
    fed_b = send(own_b, perm=feed)
    sfed_a = send(fed_a, perm=sibling)
    amps = lax.all_gather(line_amps(near, other), "vec", axis=0, tiled=False)
    amps = (amps, send(amps, perm=sibling))
    sfed_b = send(fed_b, perm=sibling)
    blocks = (own_a, own_b, sib_a, sib_b, fed_a, fed_b, sfed_a, sfed_b, mid_a, mid_b)
    columns = lax.axis_size("vec")
    arrived = []
    for call in ([3, 1], [2, 0]):
        for bit, term in zip(call, ladder(first, call, plan, blocks, amps)):
            arrived.append(swap_columns(term, bit, columns) if bit else term)
    return sum(term.astype(jnp.float32) for term in arrived).astype(jnp.bfloat16)


def target_columns(swap):
    worker, right, left = np.meshgrid(
        np.arange(2 * CORES), np.arange(VB // 2), np.arange(VB // 2), indexing="ij"
    )
    core = worker % CORES
    chip = 1 + worker // CORES
    near = np.where(chip == 1, 0, CHIPS - 1)
    far = np.where(chip == 1, 2, 1)
    end = np.where(chip == 1, CHIPS - 1, 0)
    each = VB // (CHIPS * CORES)

    def local(at):
        block = at // each
        home = np.where(block < 2, chip, near) * CORES + np.where(block % 2 == 0, core, 1 - core)
        return home * each + at % each

    def spread(at):
        return (np.choose(at // each, [chip, near, far, end]) * CORES + core) * each + at % each

    a, b = (spread(left), local(right)) if swap else (local(left), spread(right))
    return (a * VB + b).reshape(-1)


def scatter_terms(terms, named, tiles):
    columns = lax.axis_size("vec")
    column = lax.axis_index("vec")
    owners = lax.axis_size("amp")
    halves, rows, width = terms.shape
    each = rows // owners
    mine = terms.reshape(halves, owners, each, width).swapaxes(0, 1)
    mine = lax.all_to_all(mine, "amp", split_axis=0, concat_axis=0, tiled=True)
    mine = mine[CORES : CORES * (CHIPS - 1)].transpose(1, 2, 0, 3).reshape(halves * each, PAIRS)
    canonical = jnp.arange(PAIRS, dtype=jnp.int32)[None, :]
    one_hot = lambda to: (jnp.asarray(to, jnp.int32)[:, None] == canonical).astype(jnp.bfloat16)
    straight, turned = one_hot(target_columns(False)), one_hot(target_columns(True))
    dot = functools.partial(jnp.dot, preferred_element_type=jnp.float32)
    straight, turned = dot(mine, straight), dot(mine, turned)
    swap = named["swap"].reshape(halves, columns)
    out = named["out"].reshape(halves, columns)
    swapped = jnp.repeat(lax.dynamic_index_in_dim(swap, column, 1), each, axis=0) == 1
    placed = jnp.where(swapped, turned, straight).astype(jnp.bfloat16).reshape(halves, each, PAIRS)
    held = tiles // columns
    here = column * held + jnp.arange(held, dtype=jnp.int32)
    total = jnp.zeros((held, each, PAIRS), jnp.float32)
    for bit in range(columns):
        arrived = placed if bit == 0 else swap_columns(placed, bit, columns)
        targets = lax.dynamic_index_in_dim(out, column ^ bit, 1, keepdims=False)
        for half in range(halves):
            named_here = (here == targets[half])[:, None, None]
            total = total + jnp.where(named_here, arrived[half].astype(jnp.float32)[None], 0.0)
    return total.astype(jnp.bfloat16)


def line_local(chol, amplitudes, task_list, counts):
    tasks = lax.axis_size("amp")
    tiles = chol.shape[0]
    each = tasks // lax.axis_size("vec")
    classes = [tasks // 2, tasks // 2 + 1, tasks // 2 + 2, tasks]
    plan, named, branch = make_plan(tasks, tiles, classes, task_list, counts)
    first = {name: place[0] for name, place in plan_layout(tasks, tiles)[0].items()}
    run = lambda slots: lambda: products(first, slots, tiles, chol, amplitudes, plan, each)
    terms = lax.switch(branch, [run(slots) for slots in classes])
    return scatter_terms(terms, named, tiles)


def integral_tile(x_rows, y_rows):
    products = lax.dot_general(
        x_rows, y_rows, (((1,), (1,)), ((), ())), preferred_element_type=jnp.float32
    )
    return (
        products.reshape(VB, VB, VB, VB).transpose(0, 2, 1, 3).reshape(PAIRS, PAIRS).astype(jnp.bfloat16)
    )


def task_term(x_rows, y_rows, amp_rows):
    products = lax.dot_general(
        amp_rows, integral_tile(x_rows, y_rows), (((1,), (1,)), ((), ())), preferred_element_type=jnp.float32
    )
    return products.astype(jnp.bfloat16)


def spread_local(chol, amplitudes, task_list, counts):
    owners = lax.axis_size("amp")
    most = task_list.shape[0] // owners
    rank = jnp.arange(owners, dtype=jnp.int32)[:, None]
    offsets = jnp.cumsum(counts) - counts
    inside = (rank >= offsets) & (rank < offsets + counts)
    starts = jnp.arange(owners, dtype=jnp.int32) * most
    fields = task_list[jnp.sum(jnp.where(inside, starts + rank - offsets, 0), axis=1)]
    trade = functools.partial(lax.all_to_all, axis_name="amp", tiled=True)
    fetch = lambda array, which: trade(jnp.take(array, which, axis=0), split_axis=0, concat_axis=0).reshape(
        -1, array.shape[2]
    )
    term = task_term(fetch(chol, fields[:, 0]), fetch(chol, fields[:, 1]), fetch(amplitudes, fields[:, 2]))
    returned = trade(term.reshape(owners, -1, PAIRS), split_axis=0, concat_axis=0)
    tiles = amplitudes.shape[0]
    chosen = (jnp.arange(tiles, dtype=jnp.int32)[:, None] == fields[:, 3][None, :]).astype(jnp.bfloat16)
    summed = jnp.dot(chosen, returned.reshape(owners, -1), preferred_element_type=jnp.float32)
    summed = summed.reshape(tiles, -1, PAIRS)
    return lax.psum_scatter(summed, "vec", scatter_dimension=0, tiled=True).astype(jnp.bfloat16)


def solution(mesh):
    placed = (P(None, "amp", "vec"), P(None, "amp", None), P(), P())
    local = line_local if mesh.shape["amp"] == CHIPS * CORES else spread_local
    return jax.shard_map(
        local, mesh=mesh, in_specs=placed, out_specs=P("vec", "amp", None), check_vma=False
    )
```

```python
import functools

import jax
import jax.numpy as jnp
import numpy as np
from jax import lax
from jax.experimental import pallas as pl
from jax.experimental.pallas import tpu as pltpu
from jax.sharding import PartitionSpec as P

VB = 32
PAIRS = VB * VB
CORES = 2
CHIPS = 4
LANES = 128
VMEM = 60 * 1024 * 1024


def plan_layout(tasks, tiles):
    fields = {}
    at = 0
    for name, size in (("order", tiles), ("local", tasks), ("spread", tasks), ("amp", tasks),
                       ("out", tasks), ("swap", tasks)):
        fields[name] = (at, size)
        at += size
    return fields, at


def popcount(bits):
    bits = bits - ((bits >> 1) & 0x55555555)
    bits = (bits & 0x33333333) + ((bits >> 2) & 0x33333333)
    bits = (bits + (bits >> 4)) & 0x0F0F0F0F
    return (bits + (bits >> 8) + (bits >> 16) + (bits >> 24)) & 0xFF


def plan_kernel(tasks, tiles, most, classes, task_ref, count_ref, plan_ref, size_ref, work):
    fields, _ = plan_layout(tasks, tiles)
    first = {name: place[0] for name, place in fields.items()}
    at = jnp.int32(0)
    for owner in range(count_ref.shape[0]):
        for entry in range(most):
            live = entry < count_ref[owner]

            @pl.when(live)
            def _():
                for column in range(4):
                    work[at * 4 + column] = task_ref[column, owner * most + entry]

            at = at + live.astype(jnp.int32)
    x = [work[task * 4] for task in range(tasks)]
    y = [work[task * 4 + 1] for task in range(tasks)]
    one = jnp.int32(1)
    codes = 1 << tasks
    code = lax.broadcasted_iota(jnp.int32, (codes // LANES, LANES), 0) * LANES + lax.broadcasted_iota(
        jnp.int32, (codes // LANES, LANES), 1
    )
    bits = jnp.zeros_like(code)
    used = jnp.int32(0)
    for task in range(tasks):
        bits = bits | jnp.where((code >> task) & 1 == 1, one << y[task], one << x[task])
        used = used | (one << y[task]) | (one << x[task])
    best = jnp.min(popcount(bits) * codes + code) & (codes - 1)
    cover = jnp.int32(0)
    for task in range(tasks):
        cover = cover | (one << jnp.where((best >> task) & 1 == 1, y[task], x[task]))
    place = jnp.int32(0)
    sizes = []
    for group in (cover, used & ~cover, ~used):
        for tile in range(tiles):
            member = (group >> tile) & 1 == 1

            @pl.when(member)
            def _():
                plan_ref[first["order"] + place] = jnp.int32(tile)
                work[4 * tasks + tile] = place

            place = place + member.astype(jnp.int32)
        sizes.append(place)
    size = jnp.maximum(sizes[0], (sizes[1] + 1) // 2)
    size_ref[0] = sum((size > limit).astype(jnp.int32) for limit in classes[:-1])
    for task in range(tasks):
        swap = (best >> task) & 1 == 0
        plan_ref[first["local"] + task] = work[4 * tasks + jnp.where(swap, y[task], x[task])]
        plan_ref[first["spread"] + task] = work[4 * tasks + jnp.where(swap, x[task], y[task])]
        plan_ref[first["amp"] + task] = work[task * 4 + 2]
        plan_ref[first["out"] + task] = work[task * 4 + 3]
        plan_ref[first["swap"] + task] = swap.astype(jnp.int32)


def make_plan(tasks, tiles, classes, task_list, counts):
    fields, length = plan_layout(tasks, tiles)
    most = task_list.shape[0] // counts.shape[0]
    smem = pl.BlockSpec(memory_space=pltpu.SMEM)
    plan, size = pl.pallas_call(
        functools.partial(plan_kernel, tasks, tiles, most, classes),
        out_shape=[jax.ShapeDtypeStruct((length,), jnp.int32), jax.ShapeDtypeStruct((1,), jnp.int32)],
        in_specs=[smem] * 2,
        out_specs=[smem] * 2,
        scratch_shapes=[pltpu.SMEM((4 * tasks + tiles,), jnp.int32)],
        name="plan",
    )(task_list.T, counts)
    return plan, {name: plan[at : at + held] for name, (at, held) in fields.items()}, size[0]


def collect_kernel(lists, plan, *refs):
    sources, refs = refs[: len(lists)], refs[len(lists) :]
    outs, refs = refs[: len(lists)], refs[len(lists) :]
    *held, sems = refs
    moves = []
    for (first, each), source, out, slot in zip(lists, sources, outs, held):
        begin = lax.axis_index("vec") * each + first
        moves += [(source.at[plan[begin + at]], slot.at[at], out.at[at]) for at in range(out.shape[0])]
    loads = [pltpu.make_async_copy(move[0], move[1], sems.at[0, at]) for at, move in enumerate(moves)]
    stores = [pltpu.make_async_copy(move[1], move[2], sems.at[1, at]) for at, move in enumerate(moves)]
    for load in loads:
        load.start()
    for load, store in zip(loads, stores):
        load.wait()
        store.start()
    for store in stores:
        store.wait()


def collect(plan, *wanted):
    shapes = [(count, *array.shape[1:]) for _, _, count, array in wanted]
    total = sum(shape[0] for shape in shapes)
    any_spec = pl.BlockSpec(memory_space=pl.ANY)
    return pl.pallas_call(
        functools.partial(collect_kernel, [want[:2] for want in wanted]),
        out_shape=[jax.ShapeDtypeStruct(shape, jnp.bfloat16) for shape in shapes],
        in_specs=[pl.BlockSpec(memory_space=pltpu.SMEM)] + [any_spec] * len(wanted),
        out_specs=[any_spec] * len(wanted),
        scratch_shapes=[pltpu.VMEM(shape, jnp.bfloat16) for shape in shapes]
        + [pltpu.SemaphoreType.DMA((2, total))],
        compiler_params=pltpu.CompilerParams(vmem_limit_bytes=VMEM),
        name="collect",
    )(plan, *[want[3] for want in wanted])


def swap_fours(blocks):
    group = lax.broadcasted_iota(jnp.int32, blocks[0].shape, 1) // VB
    for bit in (1, 2):
        right = (group & bit) != 0
        shift = bit * VB
        moved = list(blocks)
        for low in range(4):
            if low & bit:
                continue
            high = low | bit
            moved[low] = jnp.where(right, pltpu.roll(blocks[high], shift, 1), blocks[low])
            moved[high] = jnp.where(right, blocks[high], pltpu.roll(blocks[low], LANES - shift, 1))
        blocks = moved
    return blocks


ACROSS = (((1,), (1,)), ((), ()))
SOURCES = 10


def ladder_kernel(first, bits, plan, *refs):
    sources, refs = refs[:SOURCES], refs[SOURCES:]
    amp_own, amp_sib, *outs, rows, amps, products, integral, sems = refs
    own_a, own_b, sib_a, sib_b, fed_a, fed_b, sfed_a, sfed_b, mid_a, mid_b = sources
    pairs = ((own_a, own_b), (sib_a, sib_b), (fed_a, fed_b), (sfed_a, sfed_b))
    wide = (own_a, fed_a, mid_a, mid_b)
    slots, each_row, _ = own_a.shape
    each = amp_own.shape[2]
    step = pl.program_id(0)
    columns = amp_own.shape[0]
    column = lax.axis_index("vec")
    core = lax.rem(lax.axis_index("amp"), CORES)
    bit_of = lambda at: jnp.where(at // each == 0, *bits)
    task_of = lambda at: lax.rem(at, each) * columns + (bit_of(at) ^ column)
    part = lambda slot, side, block: rows.at[slot, side, pl.ds(block * each_row, each_row)]

    def amp_copies(task, slot):
        return [
            pltpu.make_async_copy(
                source.at[task // each, :, lax.rem(task, each)],
                amps.at[slot, :, holder],
                sems.at[slot, 2 * len(wide) + at],
            )
            for at, (source, holder) in enumerate(((amp_own, core), (amp_sib, 1 - core)))
        ]

    def start(task, slot):
        swap = plan[first["swap"] + task]
        at = plan[first["local"] + task]
        for block, (early, late) in enumerate(pairs):
            target, sem = part(slot, swap, block), sems.at[slot, block]

            @pl.when(at < slots)
            def _():
                pltpu.make_async_copy(early.at[at], target, sem).start()

            @pl.when(at >= slots)
            def _():
                pltpu.make_async_copy(late.at[at - slots], target, sem).start()

        at = plan[first["spread"] + task]
        for block, source in enumerate(wide):
            target, sem = part(slot, 1 - swap, block), sems.at[slot, len(wide) + block]
            pltpu.make_async_copy(source.at[at], target, sem).start()
        for copy in amp_copies(task, slot):
            copy.start()

    def wait(task, slot):
        swap = plan[first["swap"] + task]
        for block in range(len(wide)):
            for side, at in ((swap, block), (1 - swap, len(wide) + block)):
                pltpu.make_async_copy(own_a.at[0], part(slot, side, block), sems.at[slot, at]).wait()
        for copy in amp_copies(task, slot):
            copy.wait()

    @pl.when(step == 0)
    def _():
        start(task_of(0), 0)

    @pl.when(step + 1 < pl.num_programs(0))
    def _():
        start(task_of(step + 1), lax.rem(step + 1, 2))

    slot = lax.rem(step, 2)
    wait(task_of(step), slot)
    whole_products = lax.dot_general(
        rows[slot, 0], rows[slot, 1], ACROSS, preferred_element_type=jnp.float32
    )
    for block in range(products.shape[0]):
        products[block] = whole_products[:, block * LANES : (block + 1) * LANES]
    group = products.shape[1] // VB
    for high in range(VB // 4):
        for block in range(products.shape[0]):
            starts = [high * 4 + low for low in range(4)]
            blocks = [products[block, pl.ds(start, group, VB)].astype(jnp.bfloat16) for start in starts]
            for low, moved in enumerate(swap_fours(blocks)):
                to = (block * 4 + low) * group
                integral[to : to + group, high * LANES : (high + 1) * LANES] = moved
    upper = lax.axis_index("amp") >= CHIPS * CORES // 2
    order = [jnp.where(upper, CHIPS - 1 - chip, chip) for chip in range(CHIPS)]
    mine = jnp.concatenate([amps[slot, chip] for chip in order]).reshape(-1, amps.shape[-1])
    term = lax.dot_general(mine, integral[...], ACROSS, preferred_element_type=jnp.float32)
    for which, out in enumerate(outs):

        @pl.when(step // each == which)
        def _():
            out[0] = term.astype(jnp.bfloat16)


def ladder(first, bits, plan, blocks, amps):
    _, rows, depth = blocks[0].shape
    columns, chips, each, amp_rows, pairs = amps[0].shape
    occupied = chips * CORES * amp_rows
    side = 4 * rows
    terms = (side // VB) ** 2
    tasks = len(bits) * each

    def out_spec(which):
        half = lambda step: jnp.clip(step - which * each, 0, each - 1)
        return pl.BlockSpec((1, occupied, terms), lambda step, plan: (half(step), 0, 0))

    return pl.pallas_call(
        functools.partial(ladder_kernel, first, bits),
        out_shape=[jax.ShapeDtypeStruct((each, occupied, terms), jnp.bfloat16)] * len(bits),
        grid_spec=pltpu.PrefetchScalarGridSpec(
            num_scalar_prefetch=1,
            grid=(tasks,),
            in_specs=[pl.BlockSpec(memory_space=pl.ANY)] * (SOURCES + len(amps)),
            out_specs=[out_spec(which) for which in range(len(bits))],
            scratch_shapes=[
                pltpu.VMEM((2, 2, side, depth), jnp.bfloat16),
                pltpu.VMEM((2, chips, CORES, amp_rows, pairs), jnp.bfloat16),
                pltpu.VMEM((side // LANES, side, LANES), jnp.float32),
                pltpu.VMEM((terms, pairs), jnp.bfloat16),
                pltpu.SemaphoreType.DMA((2, 10)),
            ],
        ),
        compiler_params=pltpu.CompilerParams(vmem_limit_bytes=VMEM),
        cost_estimate=pl.CostEstimate(
            flops=tasks * 6 * (side * side * depth + occupied * terms * pairs),
            bytes_accessed=tasks * 2 * (2 * side * depth + occupied * pairs),
            transcendentals=0,
        ),
        name="ladder",
    )(plan, *blocks, *amps)


def routes():
    last = CHIPS - 1
    feed = [(0, 1), (last, last - 1)]
    middle = [(1, 2), (2, 1)]
    both = lambda hops: [(a * CORES + c, b * CORES + c) for a, b in hops for c in range(CORES)]
    sibling = [(a * CORES + c, a * CORES + 1 - c) for a in range(CHIPS) for c in range(CORES)]
    return both(feed), both(middle), sibling


def swap_columns(array, bit, columns):
    return lax.ppermute(array, "vec", perm=[(column, column ^ bit) for column in range(columns)])


def products(first, slots, tiles, chol, amplitudes, plan, each):
    feed, middle, sibling = routes()
    send = functools.partial(lax.ppermute, axis_name="amp")
    start = first["order"]
    listed = min(2 * slots, tiles)
    (mine,) = collect(plan, (first["amp"], each, each, amplitudes))
    end = send(mine, perm=feed)
    (own_a,) = collect(plan, (start, 0, slots, chol))
    own_a, end, mine, chol = lax.optimization_barrier((own_a, end, mine, chol))
    fed_a = send(own_a, perm=feed)
    mid_a = send(own_a, perm=middle)
    (own_b,) = collect(plan, (start + slots, 0, listed - slots, chol))
    sib_a = send(own_a, perm=sibling)
    sib_b = send(own_b, perm=sibling)
    other = send(jnp.stack([mine, end]), perm=middle)
    near = jnp.stack([end, mine])
    own_b, fed_a, mid_a, sib_a, sib_b, near, other = lax.optimization_barrier(
        (own_b, fed_a, mid_a, sib_a, sib_b, near, other)
    )
    mid_b = send(fed_a, perm=middle)
    fed_b = send(own_b, perm=feed)
    sfed_a = send(fed_a, perm=sibling)
    amps = lax.all_gather(jnp.concatenate([near, other]), "vec", axis=0, tiled=False)
    amps = (amps, send(amps, perm=sibling))
    sfed_b = send(fed_b, perm=sibling)
    blocks = (own_a, own_b, sib_a, sib_b, fed_a, fed_b, sfed_a, sfed_b, mid_a, mid_b)
    columns = lax.axis_size("vec")
    arrived = []
    for call in ([3, 1], [2, 0]):
        for bit, term in zip(call, ladder(first, call, plan, blocks, amps)):
            arrived.append(swap_columns(term, bit, columns) if bit else term)
    return sum(term.astype(jnp.float32) for term in arrived).astype(jnp.bfloat16)


def target_columns(swap):
    worker, right, left = np.meshgrid(
        np.arange(2 * CORES), np.arange(VB // 2), np.arange(VB // 2), indexing="ij"
    )
    core = worker % CORES
    chip = 1 + worker // CORES
    near = np.where(chip == 1, 0, CHIPS - 1)
    far = np.where(chip == 1, 2, 1)
    end = np.where(chip == 1, CHIPS - 1, 0)
    each = VB // (CHIPS * CORES)

    def local(at):
        block = at // each
        home = np.where(block < 2, chip, near) * CORES + np.where(block % 2 == 0, core, 1 - core)
        return home * each + at % each

    def spread(at):
        return (np.choose(at // each, [chip, near, far, end]) * CORES + core) * each + at % each

    a, b = (spread(left), local(right)) if swap else (local(left), spread(right))
    return (a * VB + b).reshape(-1)


def scatter_terms(terms, named, tiles):
    columns = lax.axis_size("vec")
    column = lax.axis_index("vec")
    owners = lax.axis_size("amp")
    halves, rows, width = terms.shape
    each = rows // owners
    mine = terms.reshape(halves, owners, each, width).swapaxes(0, 1)
    mine = lax.all_to_all(mine, "amp", split_axis=0, concat_axis=0, tiled=True)
    mine = mine[CORES : CORES * (CHIPS - 1)].transpose(1, 2, 0, 3).reshape(halves * each, PAIRS)
    canonical = jnp.arange(PAIRS, dtype=jnp.int32)[None, :]
    one_hot = lambda to: (jnp.asarray(to, jnp.int32)[:, None] == canonical).astype(jnp.bfloat16)
    straight, turned = one_hot(target_columns(False)), one_hot(target_columns(True))
    dot = functools.partial(jnp.dot, preferred_element_type=jnp.float32)
    straight, turned = dot(mine, straight), dot(mine, turned)
    swap = named["swap"].reshape(halves, columns)
    out = named["out"].reshape(halves, columns)
    swapped = jnp.repeat(lax.dynamic_index_in_dim(swap, column, 1), each, axis=0) == 1
    placed = jnp.where(swapped, turned, straight).astype(jnp.bfloat16).reshape(halves, each, PAIRS)
    held = tiles // columns
    here = column * held + jnp.arange(held, dtype=jnp.int32)
    total = jnp.zeros((held, each, PAIRS), jnp.float32)
    for bit in range(columns):
        arrived = placed if bit == 0 else swap_columns(placed, bit, columns)
        targets = lax.dynamic_index_in_dim(out, column ^ bit, 1, keepdims=False)
        for half in range(halves):
            named_here = (here == targets[half])[:, None, None]
            total = total + jnp.where(named_here, arrived[half].astype(jnp.float32)[None], 0.0)
    return total.astype(jnp.bfloat16)


def line_local(chol, amplitudes, task_list, counts):
    tasks = lax.axis_size("amp")
    tiles = chol.shape[0]
    each = tasks // lax.axis_size("vec")
    classes = [tasks // 2, tasks // 2 + 1, tasks // 2 + 2, tasks]
    plan, named, branch = make_plan(tasks, tiles, classes, task_list, counts)
    first = {name: place[0] for name, place in plan_layout(tasks, tiles)[0].items()}
    run = lambda slots: lambda: products(first, slots, tiles, chol, amplitudes, plan, each)
    terms = lax.switch(branch, [run(slots) for slots in classes])
    return scatter_terms(terms, named, tiles)


def integral_tile(x_rows, y_rows):
    products = lax.dot_general(
        x_rows, y_rows, (((1,), (1,)), ((), ())), preferred_element_type=jnp.float32
    )
    return (
        products.reshape(VB, VB, VB, VB).transpose(0, 2, 1, 3).reshape(PAIRS, PAIRS).astype(jnp.bfloat16)
    )


def task_term(x_rows, y_rows, amp_rows):
    products = lax.dot_general(
        amp_rows, integral_tile(x_rows, y_rows), (((1,), (1,)), ((), ())), preferred_element_type=jnp.float32
    )
    return products.astype(jnp.bfloat16)


def spread_local(chol, amplitudes, task_list, counts):
    owners = lax.axis_size("amp")
    most = task_list.shape[0] // owners
    rank = jnp.arange(owners, dtype=jnp.int32)[:, None]
    offsets = jnp.cumsum(counts) - counts
    inside = (rank >= offsets) & (rank < offsets + counts)
    starts = jnp.arange(owners, dtype=jnp.int32) * most
    fields = task_list[jnp.sum(jnp.where(inside, starts + rank - offsets, 0), axis=1)]
    trade = functools.partial(lax.all_to_all, axis_name="amp", tiled=True)
    fetch = lambda array, which: trade(jnp.take(array, which, axis=0), split_axis=0, concat_axis=0).reshape(
        -1, array.shape[2]
    )
    term = task_term(fetch(chol, fields[:, 0]), fetch(chol, fields[:, 1]), fetch(amplitudes, fields[:, 2]))
    returned = trade(term.reshape(owners, -1, PAIRS), split_axis=0, concat_axis=0)
    tiles = amplitudes.shape[0]
    chosen = (jnp.arange(tiles, dtype=jnp.int32)[:, None] == fields[:, 3][None, :]).astype(jnp.bfloat16)
    summed = jnp.dot(chosen, returned.reshape(owners, -1), preferred_element_type=jnp.float32)
    summed = summed.reshape(tiles, -1, PAIRS)
    return lax.psum_scatter(summed, "vec", scatter_dimension=0, tiled=True).astype(jnp.bfloat16)


def solution(mesh):
    placed = (P(None, "amp", "vec"), P(None, "amp", None), P(), P())
    local = line_local if mesh.shape["amp"] == CHIPS * CORES else spread_local
    return jax.shard_map(
        local, mesh=mesh, in_specs=placed, out_specs=P("vec", "amp", None), check_vma=False
    )
```

```python
import functools

import jax
import jax.numpy as jnp
import numpy as np
from jax import lax
from jax.experimental import pallas as pl
from jax.experimental.pallas import tpu as pltpu
from jax.sharding import PartitionSpec as P

VB = 32
PAIRS = VB * VB
CORES = 2
CHIPS = 4
LANES = 128
VMEM = 60 * 1024 * 1024


def plan_layout(tasks, tiles):
    fields = {}
    at = 0
    for name, size in (("order", tiles), ("local", tasks), ("spread", tasks), ("amp", tasks),
                       ("out", tasks), ("swap", tasks)):
        fields[name] = (at, size)
        at += size
    return fields, at


def popcount(bits):
    bits = bits - ((bits >> 1) & 0x55555555)
    bits = (bits & 0x33333333) + ((bits >> 2) & 0x33333333)
    bits = (bits + (bits >> 4)) & 0x0F0F0F0F
    return (bits + (bits >> 8) + (bits >> 16) + (bits >> 24)) & 0xFF


def plan_kernel(tasks, tiles, most, classes, task_ref, count_ref, plan_ref, size_ref, work):
    fields, _ = plan_layout(tasks, tiles)
    first = {name: place[0] for name, place in fields.items()}
    at = jnp.int32(0)
    for owner in range(count_ref.shape[0]):
        for entry in range(most):
            live = entry < count_ref[owner]

            @pl.when(live)
            def _():
                for column in range(4):
                    work[at * 4 + column] = task_ref[column, owner * most + entry]

            at = at + live.astype(jnp.int32)
    x = [work[task * 4] for task in range(tasks)]
    y = [work[task * 4 + 1] for task in range(tasks)]
    one = jnp.int32(1)
    codes = 1 << tasks
    code = lax.broadcasted_iota(jnp.int32, (codes // LANES, LANES), 0) * LANES + lax.broadcasted_iota(
        jnp.int32, (codes // LANES, LANES), 1
    )
    bits = jnp.zeros_like(code)
    used = jnp.int32(0)
    for task in range(tasks):
        bits = bits | jnp.where((code >> task) & 1 == 1, one << y[task], one << x[task])
        used = used | (one << y[task]) | (one << x[task])
    best = jnp.min(popcount(bits) * codes + code) & (codes - 1)
    cover = jnp.int32(0)
    for task in range(tasks):
        cover = cover | (one << jnp.where((best >> task) & 1 == 1, y[task], x[task]))
    place = jnp.int32(0)
    sizes = []
    for group in (cover, used & ~cover, ~used):
        for tile in range(tiles):
            member = (group >> tile) & 1 == 1

            @pl.when(member)
            def _():
                plan_ref[first["order"] + place] = jnp.int32(tile)
                work[4 * tasks + tile] = place

            place = place + member.astype(jnp.int32)
        sizes.append(place)
    fits = jnp.int32(len(classes) - 1)
    for at, (spread, listed) in reversed(list(enumerate(classes[:-1]))):
        fits = jnp.where((sizes[0] <= spread) & (sizes[1] <= listed), at, fits)
    size_ref[0] = fits
    for task in range(tasks):
        swap = (best >> task) & 1 == 0
        plan_ref[first["local"] + task] = work[4 * tasks + jnp.where(swap, y[task], x[task])]
        plan_ref[first["spread"] + task] = work[4 * tasks + jnp.where(swap, x[task], y[task])]
        plan_ref[first["amp"] + task] = work[task * 4 + 2]
        plan_ref[first["out"] + task] = work[task * 4 + 3]
        plan_ref[first["swap"] + task] = swap.astype(jnp.int32)


def make_plan(tasks, tiles, classes, task_list, counts):
    fields, length = plan_layout(tasks, tiles)
    most = task_list.shape[0] // counts.shape[0]
    smem = pl.BlockSpec(memory_space=pltpu.SMEM)
    plan, size = pl.pallas_call(
        functools.partial(plan_kernel, tasks, tiles, most, classes),
        out_shape=[jax.ShapeDtypeStruct((length,), jnp.int32), jax.ShapeDtypeStruct((1,), jnp.int32)],
        in_specs=[smem] * 2,
        out_specs=[smem] * 2,
        scratch_shapes=[pltpu.SMEM((4 * tasks + tiles,), jnp.int32)],
        name="plan",
    )(task_list.T, counts)
    return plan, {name: plan[at : at + held] for name, (at, held) in fields.items()}, size[0]


def collect_kernel(lists, plan, *refs):
    sources, refs = refs[: len(lists)], refs[len(lists) :]
    outs, refs = refs[: len(lists)], refs[len(lists) :]
    *held, sems = refs
    moves = []
    for (first, each), source, out, slot in zip(lists, sources, outs, held):
        begin = lax.axis_index("vec") * each + first
        moves += [(source.at[plan[begin + at]], slot.at[at], out.at[at]) for at in range(out.shape[0])]
    loads = [pltpu.make_async_copy(move[0], move[1], sems.at[0, at]) for at, move in enumerate(moves)]
    stores = [pltpu.make_async_copy(move[1], move[2], sems.at[1, at]) for at, move in enumerate(moves)]
    for load in loads:
        load.start()
    for load, store in zip(loads, stores):
        load.wait()
        store.start()
    for store in stores:
        store.wait()


def collect(plan, *wanted):
    shapes = [(count, *array.shape[1:]) for _, _, count, array in wanted]
    total = sum(shape[0] for shape in shapes)
    any_spec = pl.BlockSpec(memory_space=pl.ANY)
    return pl.pallas_call(
        functools.partial(collect_kernel, [want[:2] for want in wanted]),
        out_shape=[jax.ShapeDtypeStruct(shape, jnp.bfloat16) for shape in shapes],
        in_specs=[pl.BlockSpec(memory_space=pltpu.SMEM)] + [any_spec] * len(wanted),
        out_specs=[any_spec] * len(wanted),
        scratch_shapes=[pltpu.VMEM(shape, jnp.bfloat16) for shape in shapes]
        + [pltpu.SemaphoreType.DMA((2, total))],
        compiler_params=pltpu.CompilerParams(vmem_limit_bytes=VMEM),
        name="collect",
    )(plan, *[want[3] for want in wanted])


def swap_fours(blocks):
    group = lax.broadcasted_iota(jnp.int32, blocks[0].shape, 1) // VB
    for bit in (1, 2):
        right = (group & bit) != 0
        shift = bit * VB
        moved = list(blocks)
        for low in range(4):
            if low & bit:
                continue
            high = low | bit
            moved[low] = jnp.where(right, pltpu.roll(blocks[high], shift, 1), blocks[low])
            moved[high] = jnp.where(right, blocks[high], pltpu.roll(blocks[low], LANES - shift, 1))
        blocks = moved
    return blocks


ACROSS = (((1,), (1,)), ((), ()))
SOURCES = 10


def ladder_kernel(first, bits, plan, *refs):
    sources, refs = refs[:SOURCES], refs[SOURCES:]
    amp_own, amp_sib, *outs, rows, amps, products, integral, sems = refs
    own_a, own_b, sib_a, sib_b, fed_a, fed_b, sfed_a, sfed_b, mid_a, mid_b = sources
    pairs = ((own_a, own_b), (sib_a, sib_b), (fed_a, fed_b), (sfed_a, sfed_b))
    wide = (own_a, fed_a, mid_a, mid_b)
    slots, each_row, _ = own_a.shape
    each = amp_own.shape[2]
    step = pl.program_id(0)
    columns = amp_own.shape[0]
    column = lax.axis_index("vec")
    core = lax.rem(lax.axis_index("amp"), CORES)
    bit_of = lambda at: jnp.where(at // each == 0, *bits)
    task_of = lambda at: lax.rem(at, each) * columns + (bit_of(at) ^ column)
    part = lambda slot, side, block: rows.at[slot, side, pl.ds(block * each_row, each_row)]

    def amp_copies(task, slot):
        return [
            pltpu.make_async_copy(
                source.at[task // each, :, lax.rem(task, each)],
                amps.at[slot, :, holder],
                sems.at[slot, 2 * len(wide) + at],
            )
            for at, (source, holder) in enumerate(((amp_own, core), (amp_sib, 1 - core)))
        ]

    def start(task, slot):
        swap = plan[first["swap"] + task]
        at = plan[first["local"] + task]
        for block, (early, late) in enumerate(pairs):
            target, sem = part(slot, swap, block), sems.at[slot, block]

            @pl.when(at < slots)
            def _():
                pltpu.make_async_copy(early.at[at], target, sem).start()

            @pl.when(at >= slots)
            def _():
                pltpu.make_async_copy(late.at[at - slots], target, sem).start()

        at = plan[first["spread"] + task]
        for block, source in enumerate(wide):
            target, sem = part(slot, 1 - swap, block), sems.at[slot, len(wide) + block]
            pltpu.make_async_copy(source.at[at], target, sem).start()
        for copy in amp_copies(task, slot):
            copy.start()

    def wait(task, slot):
        swap = plan[first["swap"] + task]
        for block in range(len(wide)):
            for side, at in ((swap, block), (1 - swap, len(wide) + block)):
                pltpu.make_async_copy(own_a.at[0], part(slot, side, block), sems.at[slot, at]).wait()
        for copy in amp_copies(task, slot):
            copy.wait()

    @pl.when(step == 0)
    def _():
        start(task_of(0), 0)

    @pl.when(step + 1 < pl.num_programs(0))
    def _():
        start(task_of(step + 1), lax.rem(step + 1, 2))

    slot = lax.rem(step, 2)
    wait(task_of(step), slot)
    wide_rows = 2 * LANES

    def multiply(part, carry):
        right = rows[slot, 1, pl.ds(pl.multiple_of(part * wide_rows, wide_rows), wide_rows)]
        both = lax.dot_general(rows[slot, 0], right, ACROSS, preferred_element_type=jnp.float32)
        products[2 * part] = both[:, :LANES]
        products[2 * part + 1] = both[:, LANES:]
        return carry

    lax.fori_loop(0, products.shape[0] // 2, multiply, 0)
    group = products.shape[1] // VB

    def transpose(high, carry):
        lanes = pl.ds(pl.multiple_of(high * LANES, LANES), LANES)
        for block in range(products.shape[0]):
            starts = [high * 4 + low for low in range(4)]
            blocks = [products[block, pl.ds(at, group, VB)].astype(jnp.bfloat16) for at in starts]
            for low, moved in enumerate(swap_fours(blocks)):
                to = (block * 4 + low) * group
                integral[to : to + group, lanes] = moved
        return carry

    lax.fori_loop(0, VB // 4, transpose, 0)
    upper = lax.axis_index("amp") >= CHIPS * CORES // 2
    order = [jnp.where(upper, CHIPS - 1 - chip, chip) for chip in range(CHIPS)]
    mine = jnp.concatenate([amps[slot, chip] for chip in order]).reshape(-1, amps.shape[-1])
    term = lax.dot_general(mine, integral[...], ACROSS, preferred_element_type=jnp.float32)
    for which, out in enumerate(outs):

        @pl.when(step // each == which)
        def _():
            out[0] = term.astype(jnp.bfloat16)


def ladder(first, bits, plan, blocks, amps):
    _, rows, depth = blocks[0].shape
    columns, chips, each, amp_rows, pairs = amps[0].shape
    occupied = chips * CORES * amp_rows
    side = 4 * rows
    terms = (side // VB) ** 2
    tasks = len(bits) * each

    def out_spec(which):
        half = lambda step: jnp.clip(step - which * each, 0, each - 1)
        return pl.BlockSpec((1, occupied, terms), lambda step, plan: (half(step), 0, 0))

    return pl.pallas_call(
        functools.partial(ladder_kernel, first, bits),
        out_shape=[jax.ShapeDtypeStruct((each, occupied, terms), jnp.bfloat16)] * len(bits),
        grid_spec=pltpu.PrefetchScalarGridSpec(
            num_scalar_prefetch=1,
            grid=(tasks,),
            in_specs=[pl.BlockSpec(memory_space=pl.ANY)] * (SOURCES + len(amps)),
            out_specs=[out_spec(which) for which in range(len(bits))],
            scratch_shapes=[
                pltpu.VMEM((2, 2, side, depth), jnp.bfloat16),
                pltpu.VMEM((2, chips, CORES, amp_rows, pairs), jnp.bfloat16),
                pltpu.VMEM((side // LANES, side, LANES), jnp.float32),
                pltpu.VMEM((terms, pairs), jnp.bfloat16),
                pltpu.SemaphoreType.DMA((2, 10)),
            ],
        ),
        compiler_params=pltpu.CompilerParams(vmem_limit_bytes=VMEM),
        cost_estimate=pl.CostEstimate(
            flops=tasks * 6 * (side * side * depth + occupied * terms * pairs),
            bytes_accessed=tasks * 2 * (2 * side * depth + occupied * pairs),
            transcendentals=0,
        ),
        name="ladder",
    )(plan, *blocks, *amps)


def routes():
    last = CHIPS - 1
    feed = [(0, 1), (last, last - 1)]
    middle = [(1, 2), (2, 1)]
    both = lambda hops: [(a * CORES + c, b * CORES + c) for a, b in hops for c in range(CORES)]
    sibling = [(a * CORES + c, a * CORES + 1 - c) for a in range(CHIPS) for c in range(CORES)]
    return both(feed), both(middle), sibling


def swap_columns(array, bit, columns):
    return lax.ppermute(array, "vec", perm=[(column, column ^ bit) for column in range(columns)])


def products(first, slots, listed, chol, amplitudes, plan, each):
    feed, middle, sibling = routes()
    send = functools.partial(lax.ppermute, axis_name="amp")
    start = first["order"]
    (mine,) = collect(plan, (first["amp"], each, each, amplitudes))
    end = send(mine, perm=feed)
    over = send(mine, perm=middle)
    (own_a,) = collect(plan, (start, 0, slots, chol))
    own_a, end, over, mine, chol = lax.optimization_barrier((own_a, end, over, mine, chol))
    fed_a = send(own_a, perm=feed)
    mid_a = send(own_a, perm=middle)
    (own_b,) = collect(plan, (start + slots, 0, listed - slots, chol))
    sib_a = send(own_a, perm=sibling)
    sib_b = send(own_b, perm=sibling)
    far = send(end, perm=middle)
    line = jnp.stack([end, mine, over])
    own_b, fed_a, mid_a, sib_a, sib_b, line, far = lax.optimization_barrier(
        (own_b, fed_a, mid_a, sib_a, sib_b, line, far)
    )
    mid_b = send(fed_a, perm=middle)
    fed_b = send(own_b, perm=feed)
    sfed_a = send(fed_a, perm=sibling)
    amps = lax.all_gather(jnp.concatenate([line, far[None]]), "vec", axis=0, tiled=False)
    amps = (amps, send(amps, perm=sibling))
    if listed > 2 * slots:
        fed_b, mid_b = lax.optimization_barrier((fed_b, mid_b))
    sfed_b = send(fed_b, perm=sibling)
    blocks = (own_a, own_b, sib_a, sib_b, fed_a, fed_b, sfed_a, sfed_b, mid_a, mid_b)
    columns = lax.axis_size("vec")
    arrived = []
    for call in ([3, 1], [2, 0]):
        for bit, term in zip(call, ladder(first, call, plan, blocks, amps)):
            arrived.append(swap_columns(term, bit, columns) if bit else term)
    return sum(term.astype(jnp.float32) for term in arrived).astype(jnp.bfloat16)


def target_columns(swap):
    worker, right, left = np.meshgrid(
        np.arange(2 * CORES), np.arange(VB // 2), np.arange(VB // 2), indexing="ij"
    )
    core = worker % CORES
    chip = 1 + worker // CORES
    near = np.where(chip == 1, 0, CHIPS - 1)
    far = np.where(chip == 1, 2, 1)
    end = np.where(chip == 1, CHIPS - 1, 0)
    each = VB // (CHIPS * CORES)

    def local(at):
        block = at // each
        home = np.where(block < 2, chip, near) * CORES + np.where(block % 2 == 0, core, 1 - core)
        return home * each + at % each

    def spread(at):
        return (np.choose(at // each, [chip, near, far, end]) * CORES + core) * each + at % each

    a, b = (spread(left), local(right)) if swap else (local(left), spread(right))
    return (a * VB + b).reshape(-1)


def scatter_terms(terms, named, tiles):
    columns = lax.axis_size("vec")
    column = lax.axis_index("vec")
    owners = lax.axis_size("amp")
    halves, rows, width = terms.shape
    each = rows // owners
    mine = terms.reshape(halves, owners, each, width).swapaxes(0, 1)
    mine = lax.all_to_all(mine, "amp", split_axis=0, concat_axis=0, tiled=True)
    mine = mine[CORES : CORES * (CHIPS - 1)].transpose(1, 2, 0, 3).reshape(halves * each, PAIRS)
    canonical = jnp.arange(PAIRS, dtype=jnp.int32)[None, :]
    one_hot = lambda to: (jnp.asarray(to, jnp.int32)[:, None] == canonical).astype(jnp.bfloat16)
    straight, turned = one_hot(target_columns(False)), one_hot(target_columns(True))
    dot = functools.partial(jnp.dot, preferred_element_type=jnp.float32)
    straight, turned = dot(mine, straight), dot(mine, turned)
    swap = named["swap"].reshape(halves, columns)
    out = named["out"].reshape(halves, columns)
    swapped = jnp.repeat(lax.dynamic_index_in_dim(swap, column, 1), each, axis=0) == 1
    placed = jnp.where(swapped, turned, straight).astype(jnp.bfloat16).reshape(halves, each, PAIRS)
    held = tiles // columns
    here = column * held + jnp.arange(held, dtype=jnp.int32)
    total = jnp.zeros((held, each, PAIRS), jnp.float32)
    for bit in range(columns):
        arrived = placed if bit == 0 else swap_columns(placed, bit, columns)
        targets = lax.dynamic_index_in_dim(out, column ^ bit, 1, keepdims=False)
        for half in range(halves):
            named_here = (here == targets[half])[:, None, None]
            total = total + jnp.where(named_here, arrived[half].astype(jnp.float32)[None], 0.0)
    return total.astype(jnp.bfloat16)


def line_local(chol, amplitudes, task_list, counts):
    tasks = lax.axis_size("amp")
    tiles = chol.shape[0]
    each = tasks // lax.axis_size("vec")
    half = tasks // 2
    classes = [(half, tasks + 1), (half + 1, tasks + 2), (half + 1, tasks + 3), (half + 2, tasks + 4)]
    classes.append((tasks, min(2 * tasks, tiles)))
    plan, named, branch = make_plan(tasks, tiles, classes, task_list, counts)
    first = {name: place[0] for name, place in plan_layout(tasks, tiles)[0].items()}
    run = lambda slots, listed: lambda: products(first, slots, listed, chol, amplitudes, plan, each)
    terms = lax.switch(branch, [run(*sizes) for sizes in classes])
    return scatter_terms(terms, named, tiles)


def integral_tile(x_rows, y_rows):
    products = lax.dot_general(
        x_rows, y_rows, (((1,), (1,)), ((), ())), preferred_element_type=jnp.float32
    )
    return (
        products.reshape(VB, VB, VB, VB).transpose(0, 2, 1, 3).reshape(PAIRS, PAIRS).astype(jnp.bfloat16)
    )


def task_term(x_rows, y_rows, amp_rows):
    products = lax.dot_general(
        amp_rows, integral_tile(x_rows, y_rows), (((1,), (1,)), ((), ())), preferred_element_type=jnp.float32
    )
    return products.astype(jnp.bfloat16)


def spread_local(chol, amplitudes, task_list, counts):
    owners = lax.axis_size("amp")
    most = task_list.shape[0] // owners
    rank = jnp.arange(owners, dtype=jnp.int32)[:, None]
    offsets = jnp.cumsum(counts) - counts
    inside = (rank >= offsets) & (rank < offsets + counts)
    starts = jnp.arange(owners, dtype=jnp.int32) * most
    fields = task_list[jnp.sum(jnp.where(inside, starts + rank - offsets, 0), axis=1)]
    trade = functools.partial(lax.all_to_all, axis_name="amp", tiled=True)
    fetch = lambda array, which: trade(jnp.take(array, which, axis=0), split_axis=0, concat_axis=0).reshape(
        -1, array.shape[2]
    )
    term = task_term(fetch(chol, fields[:, 0]), fetch(chol, fields[:, 1]), fetch(amplitudes, fields[:, 2]))
    returned = trade(term.reshape(owners, -1, PAIRS), split_axis=0, concat_axis=0)
    tiles = amplitudes.shape[0]
    chosen = (jnp.arange(tiles, dtype=jnp.int32)[:, None] == fields[:, 3][None, :]).astype(jnp.bfloat16)
    summed = jnp.dot(chosen, returned.reshape(owners, -1), preferred_element_type=jnp.float32)
    summed = summed.reshape(tiles, -1, PAIRS)
    return lax.psum_scatter(summed, "vec", scatter_dimension=0, tiled=True).astype(jnp.bfloat16)


def solution(mesh):
    placed = (P(None, "amp", "vec"), P(None, "amp", None), P(), P())
    local = line_local if mesh.shape["amp"] == CHIPS * CORES else spread_local
    return jax.shard_map(
        local, mesh=mesh, in_specs=placed, out_specs=P("vec", "amp", None), check_vma=False
    )
```

```python
import functools

import jax
import jax.numpy as jnp
import numpy as np
from jax import lax
from jax.experimental import pallas as pl
from jax.experimental.pallas import tpu as pltpu
from jax.sharding import PartitionSpec as P

VB = 32
PAIRS = VB * VB
CORES = 2
CHIPS = 4
LANES = 128
VMEM = 60 * 1024 * 1024


def plan_layout(tasks, tiles):
    fields = {}
    at = 0
    for name, size in (("order", tiles), ("local", tasks), ("spread", tasks), ("amp", tasks),
                       ("out", tasks), ("swap", tasks)):
        fields[name] = (at, size)
        at += size
    return fields, at


def popcount(bits):
    bits = bits - ((bits >> 1) & 0x55555555)
    bits = (bits & 0x33333333) + ((bits >> 2) & 0x33333333)
    bits = (bits + (bits >> 4)) & 0x0F0F0F0F
    return (bits + (bits >> 8) + (bits >> 16) + (bits >> 24)) & 0xFF


def plan_kernel(tasks, tiles, most, classes, task_ref, count_ref, plan_ref, size_ref, work):
    fields, _ = plan_layout(tasks, tiles)
    first = {name: place[0] for name, place in fields.items()}
    at = jnp.int32(0)
    for owner in range(count_ref.shape[0]):
        for entry in range(most):
            live = entry < count_ref[owner]

            @pl.when(live)
            def _():
                for column in range(4):
                    work[at * 4 + column] = task_ref[column, owner * most + entry]

            at = at + live.astype(jnp.int32)
    x = [work[task * 4] for task in range(tasks)]
    y = [work[task * 4 + 1] for task in range(tasks)]
    one = jnp.int32(1)
    codes = 1 << tasks
    code = lax.broadcasted_iota(jnp.int32, (codes // LANES, LANES), 0) * LANES + lax.broadcasted_iota(
        jnp.int32, (codes // LANES, LANES), 1
    )
    bits = jnp.zeros_like(code)
    used = jnp.int32(0)
    for task in range(tasks):
        bits = bits | jnp.where((code >> task) & 1 == 1, one << y[task], one << x[task])
        used = used | (one << y[task]) | (one << x[task])
    best = jnp.min(popcount(bits) * codes + code) & (codes - 1)
    cover = jnp.int32(0)
    for task in range(tasks):
        cover = cover | (one << jnp.where((best >> task) & 1 == 1, y[task], x[task]))
    place = jnp.int32(0)
    sizes = []
    for group in (cover, used & ~cover, ~used):
        for tile in range(tiles):
            member = (group >> tile) & 1 == 1

            @pl.when(member)
            def _():
                plan_ref[first["order"] + place] = jnp.int32(tile)
                work[4 * tasks + tile] = place

            place = place + member.astype(jnp.int32)
        sizes.append(place)
    fits = jnp.int32(len(classes) - 1)
    for at, (spread, listed) in sorted(enumerate(classes), key=lambda entry: -sum(entry[1])):
        fits = jnp.where((sizes[0] <= spread) & (sizes[1] <= listed), at, fits)
    size_ref[0] = fits
    for task in range(tasks):
        swap = (best >> task) & 1 == 0
        plan_ref[first["local"] + task] = work[4 * tasks + jnp.where(swap, y[task], x[task])]
        plan_ref[first["spread"] + task] = work[4 * tasks + jnp.where(swap, x[task], y[task])]
        plan_ref[first["amp"] + task] = work[task * 4 + 2]
        plan_ref[first["out"] + task] = work[task * 4 + 3]
        plan_ref[first["swap"] + task] = swap.astype(jnp.int32)


def make_plan(tasks, tiles, classes, task_list, counts):
    fields, length = plan_layout(tasks, tiles)
    most = task_list.shape[0] // counts.shape[0]
    smem = pl.BlockSpec(memory_space=pltpu.SMEM)
    plan, size = pl.pallas_call(
        functools.partial(plan_kernel, tasks, tiles, most, classes),
        out_shape=[jax.ShapeDtypeStruct((length,), jnp.int32), jax.ShapeDtypeStruct((1,), jnp.int32)],
        in_specs=[smem] * 2,
        out_specs=[smem] * 2,
        scratch_shapes=[pltpu.SMEM((4 * tasks + tiles,), jnp.int32)],
        name="plan",
    )(task_list.T, counts)
    return plan, {name: plan[at : at + held] for name, (at, held) in fields.items()}, size[0]


def collect_kernel(lists, plan, *refs):
    sources, refs = refs[: len(lists)], refs[len(lists) :]
    outs, refs = refs[: len(lists)], refs[len(lists) :]
    *held, sems = refs
    moves = []
    for (first, each), source, out, slot in zip(lists, sources, outs, held):
        begin = lax.axis_index("vec") * each + first
        moves += [(source.at[plan[begin + at]], slot.at[at], out.at[at]) for at in range(out.shape[0])]
    loads = [pltpu.make_async_copy(move[0], move[1], sems.at[0, at]) for at, move in enumerate(moves)]
    stores = [pltpu.make_async_copy(move[1], move[2], sems.at[1, at]) for at, move in enumerate(moves)]
    for load in loads:
        load.start()
    for load, store in zip(loads, stores):
        load.wait()
        store.start()
    for store in stores:
        store.wait()


def collect(plan, *wanted):
    shapes = [(count, *array.shape[1:]) for _, _, count, array in wanted]
    total = sum(shape[0] for shape in shapes)
    any_spec = pl.BlockSpec(memory_space=pl.ANY)
    return pl.pallas_call(
        functools.partial(collect_kernel, [want[:2] for want in wanted]),
        out_shape=[jax.ShapeDtypeStruct(shape, jnp.bfloat16) for shape in shapes],
        in_specs=[pl.BlockSpec(memory_space=pltpu.SMEM)] + [any_spec] * len(wanted),
        out_specs=[any_spec] * len(wanted),
        scratch_shapes=[pltpu.VMEM(shape, jnp.bfloat16) for shape in shapes]
        + [pltpu.SemaphoreType.DMA((2, total))],
        compiler_params=pltpu.CompilerParams(vmem_limit_bytes=VMEM),
        name="collect",
    )(plan, *[want[3] for want in wanted])


def swap_fours(blocks):
    group = lax.broadcasted_iota(jnp.int32, blocks[0].shape, 1) // VB
    for bit in (1, 2):
        right = (group & bit) != 0
        shift = bit * VB
        moved = list(blocks)
        for low in range(4):
            if low & bit:
                continue
            high = low | bit
            moved[low] = jnp.where(right, pltpu.roll(blocks[high], shift, 1), blocks[low])
            moved[high] = jnp.where(right, blocks[high], pltpu.roll(blocks[low], LANES - shift, 1))
        blocks = moved
    return blocks


ACROSS = (((1,), (1,)), ((), ()))
SOURCES = 10


def ladder_kernel(first, bits, plan, *refs):
    sources, refs = refs[:SOURCES], refs[SOURCES:]
    amp_own, amp_sib, *outs, rows, amps, products, integral, sems = refs
    own_a, own_b, sib_a, sib_b, fed_a, fed_b, sfed_a, sfed_b, mid_a, mid_b = sources
    pairs = ((own_a, own_b), (sib_a, sib_b), (fed_a, fed_b), (sfed_a, sfed_b))
    wide = (own_a, fed_a, mid_a, mid_b)
    slots, each_row, _ = own_a.shape
    each = amp_own.shape[2]
    step = pl.program_id(0)
    columns = amp_own.shape[0]
    column = lax.axis_index("vec")
    core = lax.rem(lax.axis_index("amp"), CORES)
    bit_of = lambda at: sum(jnp.where(at // each == which, bit, 0) for which, bit in enumerate(bits))
    task_of = lambda at: lax.rem(at, each) * columns + (bit_of(at) ^ column)
    part = lambda slot, side, block: rows.at[slot, side, pl.ds(block * each_row, each_row)]

    def amp_copies(task, slot):
        return [
            pltpu.make_async_copy(
                source.at[task // each, :, lax.rem(task, each)],
                amps.at[slot, :, holder],
                sems.at[slot, 2 * len(wide) + at],
            )
            for at, (source, holder) in enumerate(((amp_own, core), (amp_sib, 1 - core)))
        ]

    def start(task, slot):
        swap = plan[first["swap"] + task]
        at = plan[first["local"] + task]
        for block, (early, late) in enumerate(pairs):
            target, sem = part(slot, swap, block), sems.at[slot, block]

            @pl.when(at < slots)
            def _():
                pltpu.make_async_copy(early.at[at], target, sem).start()

            @pl.when(at >= slots)
            def _():
                pltpu.make_async_copy(late.at[at - slots], target, sem).start()

        at = plan[first["spread"] + task]
        for block, source in enumerate(wide):
            target, sem = part(slot, 1 - swap, block), sems.at[slot, len(wide) + block]
            pltpu.make_async_copy(source.at[at], target, sem).start()
        for copy in amp_copies(task, slot):
            copy.start()

    def wait(task, slot):
        swap = plan[first["swap"] + task]
        for block in range(len(wide)):
            for side, at in ((swap, block), (1 - swap, len(wide) + block)):
                pltpu.make_async_copy(own_a.at[0], part(slot, side, block), sems.at[slot, at]).wait()
        for copy in amp_copies(task, slot):
            copy.wait()

    @pl.when(step == 0)
    def _():
        start(task_of(0), 0)

    @pl.when(step + 1 < pl.num_programs(0))
    def _():
        start(task_of(step + 1), lax.rem(step + 1, 2))

    slot = lax.rem(step, 2)
    wait(task_of(step), slot)
    whole_products = lax.dot_general(
        rows[slot, 0], rows[slot, 1], ACROSS, preferred_element_type=jnp.float32
    )
    for block in range(products.shape[0]):
        products[block] = whole_products[:, block * LANES : (block + 1) * LANES]
    group = products.shape[1] // VB
    for high in range(VB // 4):
        for block in range(products.shape[0]):
            starts = [high * 4 + low for low in range(4)]
            blocks = [products[block, pl.ds(at, group, VB)].astype(jnp.bfloat16) for at in starts]
            for low, moved in enumerate(swap_fours(blocks)):
                to = (block * 4 + low) * group
                integral[to : to + group, high * LANES : (high + 1) * LANES] = moved
    upper = lax.axis_index("amp") >= CHIPS * CORES // 2
    order = [jnp.where(upper, CHIPS - 1 - chip, chip) for chip in range(CHIPS)]
    mine = jnp.concatenate([amps[slot, chip] for chip in order]).reshape(-1, amps.shape[-1])
    term = lax.dot_general(mine, integral[...], ACROSS, preferred_element_type=jnp.float32)
    for which, out in enumerate(outs):

        @pl.when(step // each == which)
        def _():
            out[0] = term.astype(jnp.bfloat16)


def ladder(first, bits, plan, blocks, amps):
    _, rows, depth = blocks[0].shape
    columns, chips, each, amp_rows, pairs = amps[0].shape
    occupied = chips * CORES * amp_rows
    side = 4 * rows
    terms = (side // VB) ** 2
    tasks = len(bits) * each

    def out_spec(which):
        half = lambda step: jnp.clip(step - which * each, 0, each - 1)
        return pl.BlockSpec((1, occupied, terms), lambda step, plan: (half(step), 0, 0))

    return pl.pallas_call(
        functools.partial(ladder_kernel, first, bits),
        out_shape=[jax.ShapeDtypeStruct((each, occupied, terms), jnp.bfloat16)] * len(bits),
        grid_spec=pltpu.PrefetchScalarGridSpec(
            num_scalar_prefetch=1,
            grid=(tasks,),
            in_specs=[pl.BlockSpec(memory_space=pl.ANY)] * (SOURCES + len(amps)),
            out_specs=[out_spec(which) for which in range(len(bits))],
            scratch_shapes=[
                pltpu.VMEM((2, 2, side, depth), jnp.bfloat16),
                pltpu.VMEM((2, chips, CORES, amp_rows, pairs), jnp.bfloat16),
                pltpu.VMEM((side // LANES, side, LANES), jnp.float32),
                pltpu.VMEM((terms, pairs), jnp.bfloat16),
                pltpu.SemaphoreType.DMA((2, 10)),
            ],
        ),
        compiler_params=pltpu.CompilerParams(vmem_limit_bytes=VMEM),
        cost_estimate=pl.CostEstimate(
            flops=tasks * 6 * (side * side * depth + occupied * terms * pairs),
            bytes_accessed=tasks * 2 * (2 * side * depth + occupied * pairs),
            transcendentals=0,
        ),
        name="ladder",
    )(plan, *blocks, *amps)


def routes():
    last = CHIPS - 1
    feed = [(0, 1), (last, last - 1)]
    middle = [(1, 2), (2, 1)]
    both = lambda hops: [(a * CORES + c, b * CORES + c) for a, b in hops for c in range(CORES)]
    sibling = [(a * CORES + c, a * CORES + 1 - c) for a in range(CHIPS) for c in range(CORES)]
    return both(feed), both(middle), sibling


def swap_columns(array, bit, columns):
    return lax.ppermute(array, "vec", perm=[(column, column ^ bit) for column in range(columns)])


def products(first, slots, listed, chol, amplitudes, plan, each):
    feed, middle, sibling = routes()
    send = functools.partial(lax.ppermute, axis_name="amp")
    start = first["order"]
    (mine,) = collect(plan, (first["amp"], each, each, amplitudes))
    end = send(mine, perm=feed)
    over = send(mine, perm=middle)
    (own_a,) = collect(plan, (start, 0, slots, chol))
    own_a, end, over, mine, chol = lax.optimization_barrier((own_a, end, over, mine, chol))
    fed_a = send(own_a, perm=feed)
    mid_a = send(own_a, perm=middle)
    (own_b,) = collect(plan, (start + slots, 0, listed - slots, chol))
    sib_a = send(own_a, perm=sibling)
    sib_b = send(own_b, perm=sibling)
    far = send(end, perm=middle)
    line = jnp.stack([end, mine, over])
    own_b, fed_a, mid_a, sib_a, sib_b, line, far = lax.optimization_barrier(
        (own_b, fed_a, mid_a, sib_a, sib_b, line, far)
    )
    mid_b = send(fed_a, perm=middle)
    fed_b = send(own_b, perm=feed)
    sfed_a = send(fed_a, perm=sibling)
    amps = lax.all_gather(jnp.concatenate([line, far[None]]), "vec", axis=0, tiled=False)
    amps = (amps, send(amps, perm=sibling))
    fed_b, mid_b, amps = lax.optimization_barrier((fed_b, mid_b, amps))
    sfed_b = send(fed_b, perm=sibling)
    blocks = (own_a, own_b, sib_a, sib_b, fed_a, fed_b, sfed_a, sfed_b, mid_a, mid_b)
    columns = lax.axis_size("vec")
    terms = ladder(first, list(range(columns)), plan, blocks, amps)
    arrived = [swap_columns(term, bit, columns) if bit else term for bit, term in enumerate(terms)]
    return sum(term.astype(jnp.float32) for term in arrived).astype(jnp.bfloat16)


def target_columns(swap):
    worker, right, left = np.meshgrid(
        np.arange(2 * CORES), np.arange(VB // 2), np.arange(VB // 2), indexing="ij"
    )
    core = worker % CORES
    chip = 1 + worker // CORES
    near = np.where(chip == 1, 0, CHIPS - 1)
    far = np.where(chip == 1, 2, 1)
    end = np.where(chip == 1, CHIPS - 1, 0)
    each = VB // (CHIPS * CORES)

    def local(at):
        block = at // each
        home = np.where(block < 2, chip, near) * CORES + np.where(block % 2 == 0, core, 1 - core)
        return home * each + at % each

    def spread(at):
        return (np.choose(at // each, [chip, near, far, end]) * CORES + core) * each + at % each

    a, b = (spread(left), local(right)) if swap else (local(left), spread(right))
    return (a * VB + b).reshape(-1)


def scatter_terms(terms, named, tiles):
    columns = lax.axis_size("vec")
    column = lax.axis_index("vec")
    owners = lax.axis_size("amp")
    halves, rows, width = terms.shape
    each = rows // owners
    mine = terms.reshape(halves, owners, each, width).swapaxes(0, 1)
    mine = lax.all_to_all(mine, "amp", split_axis=0, concat_axis=0, tiled=True)
    mine = mine[CORES : CORES * (CHIPS - 1)].transpose(1, 2, 0, 3).reshape(halves * each, PAIRS)
    canonical = jnp.arange(PAIRS, dtype=jnp.int32)[None, :]
    one_hot = lambda to: (jnp.asarray(to, jnp.int32)[:, None] == canonical).astype(jnp.bfloat16)
    straight, turned = one_hot(target_columns(False)), one_hot(target_columns(True))
    dot = functools.partial(jnp.dot, preferred_element_type=jnp.float32)
    straight, turned = dot(mine, straight), dot(mine, turned)
    swap = named["swap"].reshape(halves, columns)
    out = named["out"].reshape(halves, columns)
    swapped = jnp.repeat(lax.dynamic_index_in_dim(swap, column, 1), each, axis=0) == 1
    placed = jnp.where(swapped, turned, straight).astype(jnp.bfloat16).reshape(halves, each, PAIRS)
    held = tiles // columns
    here = column * held + jnp.arange(held, dtype=jnp.int32)
    total = jnp.zeros((held, each, PAIRS), jnp.float32)
    for bit in range(columns):
        arrived = placed if bit == 0 else swap_columns(placed, bit, columns)
        targets = lax.dynamic_index_in_dim(out, column ^ bit, 1, keepdims=False)
        for half in range(halves):
            named_here = (here == targets[half])[:, None, None]
            total = total + jnp.where(named_here, arrived[half].astype(jnp.float32)[None], 0.0)
    return total.astype(jnp.bfloat16)


def line_local(chol, amplitudes, task_list, counts):
    tasks = lax.axis_size("amp")
    tiles = chol.shape[0]
    each = tasks // lax.axis_size("vec")
    half = tasks // 2
    classes = [(half + 1, tasks + 3), (half + 1, tasks + 2), (half, tasks + 1), (half + 2, tasks + 4)]
    classes.append((tasks, min(2 * tasks, tiles)))
    plan, named, branch = make_plan(tasks, tiles, classes, task_list, counts)
    first = {name: place[0] for name, place in plan_layout(tasks, tiles)[0].items()}
    run = lambda slots, listed: lambda: products(first, slots, listed, chol, amplitudes, plan, each)
    terms = lax.switch(branch, [run(*sizes) for sizes in classes])
    return scatter_terms(terms, named, tiles)


def integral_tile(x_rows, y_rows):
    products = lax.dot_general(
        x_rows, y_rows, (((1,), (1,)), ((), ())), preferred_element_type=jnp.float32
    )
    return (
        products.reshape(VB, VB, VB, VB).transpose(0, 2, 1, 3).reshape(PAIRS, PAIRS).astype(jnp.bfloat16)
    )


def task_term(x_rows, y_rows, amp_rows):
    products = lax.dot_general(
        amp_rows, integral_tile(x_rows, y_rows), (((1,), (1,)), ((), ())), preferred_element_type=jnp.float32
    )
    return products.astype(jnp.bfloat16)


def spread_local(chol, amplitudes, task_list, counts):
    owners = lax.axis_size("amp")
    most = task_list.shape[0] // owners
    rank = jnp.arange(owners, dtype=jnp.int32)[:, None]
    offsets = jnp.cumsum(counts) - counts
    inside = (rank >= offsets) & (rank < offsets + counts)
    starts = jnp.arange(owners, dtype=jnp.int32) * most
    fields = task_list[jnp.sum(jnp.where(inside, starts + rank - offsets, 0), axis=1)]
    trade = functools.partial(lax.all_to_all, axis_name="amp", tiled=True)
    fetch = lambda array, which: trade(jnp.take(array, which, axis=0), split_axis=0, concat_axis=0).reshape(
        -1, array.shape[2]
    )
    term = task_term(fetch(chol, fields[:, 0]), fetch(chol, fields[:, 1]), fetch(amplitudes, fields[:, 2]))
    returned = trade(term.reshape(owners, -1, PAIRS), split_axis=0, concat_axis=0)
    tiles = amplitudes.shape[0]
    chosen = (jnp.arange(tiles, dtype=jnp.int32)[:, None] == fields[:, 3][None, :]).astype(jnp.bfloat16)
    summed = jnp.dot(chosen, returned.reshape(owners, -1), preferred_element_type=jnp.float32)
    summed = summed.reshape(tiles, -1, PAIRS)
    return lax.psum_scatter(summed, "vec", scatter_dimension=0, tiled=True).astype(jnp.bfloat16)


def solution(mesh):
    placed = (P(None, "amp", "vec"), P(None, "amp", None), P(), P())
    local = line_local if mesh.shape["amp"] == CHIPS * CORES else spread_local
    return jax.shard_map(
        local, mesh=mesh, in_specs=placed, out_specs=P("vec", "amp", None), check_vma=False
    )
```

```python
import functools

import jax
import jax.numpy as jnp
import numpy as np
from jax import lax
from jax.experimental import pallas as pl
from jax.experimental.pallas import tpu as pltpu
from jax.sharding import PartitionSpec as P

VB = 32
PAIRS = VB * VB
CORES = 2
CHIPS = 4
LANES = 128
VMEM = 60 * 1024 * 1024


def plan_layout(tasks, tiles):
    fields = {}
    at = 0
    for name, size in (("order", tiles), ("local", tasks), ("spread", tasks), ("amp", tasks),
                       ("out", tasks), ("swap", tasks)):
        fields[name] = (at, size)
        at += size
    return fields, at


def popcount(bits):
    bits = bits - ((bits >> 1) & 0x55555555)
    bits = (bits & 0x33333333) + ((bits >> 2) & 0x33333333)
    bits = (bits + (bits >> 4)) & 0x0F0F0F0F
    return (bits + (bits >> 8) + (bits >> 16) + (bits >> 24)) & 0xFF


def plan_kernel(tasks, tiles, most, classes, task_ref, count_ref, plan_ref, size_ref, work):
    fields, _ = plan_layout(tasks, tiles)
    first = {name: place[0] for name, place in fields.items()}
    at = jnp.int32(0)
    for owner in range(count_ref.shape[0]):
        for entry in range(most):
            live = entry < count_ref[owner]

            @pl.when(live)
            def _():
                for column in range(4):
                    work[at * 4 + column] = task_ref[column, owner * most + entry]

            at = at + live.astype(jnp.int32)
    x = [work[task * 4] for task in range(tasks)]
    y = [work[task * 4 + 1] for task in range(tasks)]
    one = jnp.int32(1)
    codes = 1 << tasks
    code = lax.broadcasted_iota(jnp.int32, (codes // LANES, LANES), 0) * LANES + lax.broadcasted_iota(
        jnp.int32, (codes // LANES, LANES), 1
    )
    bits = jnp.zeros_like(code)
    used = jnp.int32(0)
    for task in range(tasks):
        bits = bits | jnp.where((code >> task) & 1 == 1, one << y[task], one << x[task])
        used = used | (one << y[task]) | (one << x[task])
    best = jnp.min(popcount(bits) * codes + code) & (codes - 1)
    cover = jnp.int32(0)
    for task in range(tasks):
        cover = cover | (one << jnp.where((best >> task) & 1 == 1, y[task], x[task]))
    place = jnp.int32(0)
    sizes = []
    for group in (cover, used & ~cover, ~used):
        for tile in range(tiles):
            member = (group >> tile) & 1 == 1

            @pl.when(member)
            def _():
                plan_ref[first["order"] + place] = jnp.int32(tile)
                work[4 * tasks + tile] = place

            place = place + member.astype(jnp.int32)
        sizes.append(place)
    fits = jnp.int32(len(classes) - 1)
    for at, (spread, listed) in sorted(enumerate(classes), key=lambda entry: -sum(entry[1])):
        fits = jnp.where((sizes[0] <= spread) & (sizes[1] <= listed), at, fits)
    size_ref[0] = fits
    for task in range(tasks):
        swap = (best >> task) & 1 == 0
        plan_ref[first["local"] + task] = work[4 * tasks + jnp.where(swap, y[task], x[task])]
        plan_ref[first["spread"] + task] = work[4 * tasks + jnp.where(swap, x[task], y[task])]
        plan_ref[first["amp"] + task] = work[task * 4 + 2]
        plan_ref[first["out"] + task] = work[task * 4 + 3]
        plan_ref[first["swap"] + task] = swap.astype(jnp.int32)


def make_plan(tasks, tiles, classes, task_list, counts):
    fields, length = plan_layout(tasks, tiles)
    most = task_list.shape[0] // counts.shape[0]
    smem = pl.BlockSpec(memory_space=pltpu.SMEM)
    plan, size = pl.pallas_call(
        functools.partial(plan_kernel, tasks, tiles, most, classes),
        out_shape=[jax.ShapeDtypeStruct((length,), jnp.int32), jax.ShapeDtypeStruct((1,), jnp.int32)],
        in_specs=[smem] * 2,
        out_specs=[smem] * 2,
        scratch_shapes=[pltpu.SMEM((4 * tasks + tiles,), jnp.int32)],
        name="plan",
    )(task_list.T, counts)
    return plan, {name: plan[at : at + held] for name, (at, held) in fields.items()}, size[0]


def collect_kernel(lists, plan, *refs):
    sources, refs = refs[: len(lists)], refs[len(lists) :]
    outs, refs = refs[: len(lists)], refs[len(lists) :]
    *held, sems = refs
    moves = []
    for (first, each), source, out, slot in zip(lists, sources, outs, held):
        begin = lax.axis_index("vec") * each + first
        moves += [(source.at[plan[begin + at]], slot.at[at], out.at[at]) for at in range(out.shape[0])]
    loads = [pltpu.make_async_copy(move[0], move[1], sems.at[0, at]) for at, move in enumerate(moves)]
    stores = [pltpu.make_async_copy(move[1], move[2], sems.at[1, at]) for at, move in enumerate(moves)]
    for load in loads:
        load.start()
    for load, store in zip(loads, stores):
        load.wait()
        store.start()
    for store in stores:
        store.wait()


def collect(plan, *wanted):
    shapes = [(count, *array.shape[1:]) for _, _, count, array in wanted]
    total = sum(shape[0] for shape in shapes)
    any_spec = pl.BlockSpec(memory_space=pl.ANY)
    return pl.pallas_call(
        functools.partial(collect_kernel, [want[:2] for want in wanted]),
        out_shape=[jax.ShapeDtypeStruct(shape, jnp.bfloat16) for shape in shapes],
        in_specs=[pl.BlockSpec(memory_space=pltpu.SMEM)] + [any_spec] * len(wanted),
        out_specs=[any_spec] * len(wanted),
        scratch_shapes=[pltpu.VMEM(shape, jnp.bfloat16) for shape in shapes]
        + [pltpu.SemaphoreType.DMA((2, total))],
        compiler_params=pltpu.CompilerParams(vmem_limit_bytes=VMEM),
        name="collect",
    )(plan, *[want[3] for want in wanted])


def swap_fours(blocks):
    group = lax.broadcasted_iota(jnp.int32, blocks[0].shape, 1) // VB
    for bit in (1, 2):
        right = (group & bit) != 0
        shift = bit * VB
        moved = list(blocks)
        for low in range(4):
            if low & bit:
                continue
            high = low | bit
            moved[low] = jnp.where(right, pltpu.roll(blocks[high], shift, 1), blocks[low])
            moved[high] = jnp.where(right, blocks[high], pltpu.roll(blocks[low], LANES - shift, 1))
        blocks = moved
    return blocks


ACROSS = (((1,), (1,)), ((), ()))
SOURCES = 10


def ladder_kernel(first, bits, plan, *refs):
    sources, refs = refs[:SOURCES], refs[SOURCES:]
    amp_own, amp_sib, *outs, rows, amps, products, integral, sems = refs
    own_a, own_b, sib_a, sib_b, fed_a, fed_b, sfed_a, sfed_b, mid_a, mid_b = sources
    pairs = ((own_a, own_b), (sib_a, sib_b), (fed_a, fed_b), (sfed_a, sfed_b))
    wide = (own_a, fed_a, mid_a, mid_b)
    slots, each_row, _ = own_a.shape
    each = amp_own.shape[2]
    step = pl.program_id(0)
    columns = amp_own.shape[0]
    column = lax.axis_index("vec")
    core = lax.rem(lax.axis_index("amp"), CORES)
    bit_of = lambda at: sum(jnp.where(at // each == which, bit, 0) for which, bit in enumerate(bits))
    task_of = lambda at: lax.rem(at, each) * columns + (bit_of(at) ^ column)
    part = lambda slot, side, block: rows.at[slot, side, pl.ds(block * each_row, each_row)]

    def amp_copies(task, slot):
        return [
            pltpu.make_async_copy(
                source.at[task // each, :, lax.rem(task, each)],
                amps.at[slot, :, holder],
                sems.at[slot, 2 * len(wide) + at],
            )
            for at, (source, holder) in enumerate(((amp_own, core), (amp_sib, 1 - core)))
        ]

    def start(task, slot):
        swap = plan[first["swap"] + task]
        at = plan[first["local"] + task]
        for block, (early, late) in enumerate(pairs):
            target, sem = part(slot, swap, block), sems.at[slot, block]

            @pl.when(at < slots)
            def _():
                pltpu.make_async_copy(early.at[at], target, sem).start()

            @pl.when(at >= slots)
            def _():
                pltpu.make_async_copy(late.at[at - slots], target, sem).start()

        at = plan[first["spread"] + task]
        for block, source in enumerate(wide):
            target, sem = part(slot, 1 - swap, block), sems.at[slot, len(wide) + block]
            pltpu.make_async_copy(source.at[at], target, sem).start()
        for copy in amp_copies(task, slot):
            copy.start()

    def wait(task, slot):
        swap = plan[first["swap"] + task]
        for block in range(len(wide)):
            for side, at in ((swap, block), (1 - swap, len(wide) + block)):
                pltpu.make_async_copy(own_a.at[0], part(slot, side, block), sems.at[slot, at]).wait()
        for copy in amp_copies(task, slot):
            copy.wait()

    @pl.when(step == 0)
    def _():
        start(task_of(0), 0)

    @pl.when(step + 1 < pl.num_programs(0))
    def _():
        start(task_of(step + 1), lax.rem(step + 1, 2))

    slot = lax.rem(step, 2)
    wait(task_of(step), slot)
    whole_products = lax.dot_general(
        rows[slot, 0], rows[slot, 1], ACROSS, preferred_element_type=jnp.float32
    )
    for block in range(products.shape[0]):
        products[block] = whole_products[:, block * LANES : (block + 1) * LANES]
    group = products.shape[1] // VB
    for high in range(VB // 4):
        for block in range(products.shape[0]):
            starts = [high * 4 + low for low in range(4)]
            blocks = [products[block, pl.ds(at, group, VB)].astype(jnp.bfloat16) for at in starts]
            for low, moved in enumerate(swap_fours(blocks)):
                to = (block * 4 + low) * group
                integral[to : to + group, high * LANES : (high + 1) * LANES] = moved
    upper = lax.axis_index("amp") >= CHIPS * CORES // 2
    order = [jnp.where(upper, CHIPS - 1 - chip, chip) for chip in range(CHIPS)]
    mine = jnp.concatenate([amps[slot, chip] for chip in order]).reshape(-1, amps.shape[-1])
    term = lax.dot_general(mine, integral[...], ACROSS, preferred_element_type=jnp.float32)
    for which, out in enumerate(outs):

        @pl.when(step // each == which)
        def _():
            out[0] = term.astype(jnp.bfloat16)


def ladder(first, bits, plan, blocks, amps):
    _, rows, depth = blocks[0].shape
    columns, chips, each, amp_rows, pairs = amps[0].shape
    occupied = chips * CORES * amp_rows
    side = 4 * rows
    terms = (side // VB) ** 2
    tasks = len(bits) * each

    def out_spec(which):
        half = lambda step: jnp.clip(step - which * each, 0, each - 1)
        return pl.BlockSpec((1, occupied, terms), lambda step, plan: (half(step), 0, 0))

    return pl.pallas_call(
        functools.partial(ladder_kernel, first, bits),
        out_shape=[jax.ShapeDtypeStruct((each, occupied, terms), jnp.bfloat16)] * len(bits),
        grid_spec=pltpu.PrefetchScalarGridSpec(
            num_scalar_prefetch=1,
            grid=(tasks,),
            in_specs=[pl.BlockSpec(memory_space=pl.ANY)] * (SOURCES + len(amps)),
            out_specs=[out_spec(which) for which in range(len(bits))],
            scratch_shapes=[
                pltpu.VMEM((2, 2, side, depth), jnp.bfloat16),
                pltpu.VMEM((2, chips, CORES, amp_rows, pairs), jnp.bfloat16),
                pltpu.VMEM((side // LANES, side, LANES), jnp.float32),
                pltpu.VMEM((terms, pairs), jnp.bfloat16),
                pltpu.SemaphoreType.DMA((2, 10)),
            ],
        ),
        compiler_params=pltpu.CompilerParams(vmem_limit_bytes=VMEM),
        cost_estimate=pl.CostEstimate(
            flops=tasks * 6 * (side * side * depth + occupied * terms * pairs),
            bytes_accessed=tasks * 2 * (2 * side * depth + occupied * pairs),
            transcendentals=0,
        ),
        name="ladder",
    )(plan, *blocks, *amps)


def routes():
    last = CHIPS - 1
    feed = [(0, 1), (last, last - 1)]
    middle = [(1, 2), (2, 1)]
    both = lambda hops: [(a * CORES + c, b * CORES + c) for a, b in hops for c in range(CORES)]
    sibling = [(a * CORES + c, a * CORES + 1 - c) for a in range(CHIPS) for c in range(CORES)]
    return both(feed), both(middle), sibling


def swap_columns(array, bit, columns):
    return lax.ppermute(array, "vec", perm=[(column, column ^ bit) for column in range(columns)])


def products(first, slots, listed, chol, amplitudes, plan, each):
    feed, middle, sibling = routes()
    send = functools.partial(lax.ppermute, axis_name="amp")
    start = first["order"]
    (mine,) = collect(plan, (first["amp"], each, each, amplitudes))
    end = send(mine, perm=feed)
    over = send(mine, perm=middle)
    (own_a,) = collect(plan, (start, 0, slots, chol))
    own_a, end, over, mine, chol = lax.optimization_barrier((own_a, end, over, mine, chol))
    fed_a = send(own_a, perm=feed)
    mid_a = send(own_a, perm=middle)
    (own_b,) = collect(plan, (start + slots, 0, listed - slots, chol))
    sib_a = send(own_a, perm=sibling)
    far = send(end, perm=middle)
    line = jnp.stack([end, mine, over])
    own_b, fed_a, mid_a, sib_a, line, far = lax.optimization_barrier(
        (own_b, fed_a, mid_a, sib_a, line, far)
    )
    mid_b = send(fed_a, perm=middle)
    fed_b = send(own_b, perm=feed)
    sib_b = send(own_b, perm=sibling)
    sfed_a = send(fed_a, perm=sibling)
    amps = lax.all_gather(jnp.concatenate([line, far[None]]), "vec", axis=0, tiled=False)
    amps = (amps, send(amps, perm=sibling))
    fed_b, mid_b, sib_b, sfed_a, amps = lax.optimization_barrier((fed_b, mid_b, sib_b, sfed_a, amps))
    sfed_b = send(fed_b, perm=sibling)
    blocks = (own_a, own_b, sib_a, sib_b, fed_a, fed_b, sfed_a, sfed_b, mid_a, mid_b)
    columns = lax.axis_size("vec")
    terms = ladder(first, list(range(columns)), plan, blocks, amps)
    arrived = [swap_columns(term, bit, columns) if bit else term for bit, term in enumerate(terms)]
    return sum(term.astype(jnp.float32) for term in arrived).astype(jnp.bfloat16)


def target_columns(swap):
    worker, right, left = np.meshgrid(
        np.arange(2 * CORES), np.arange(VB // 2), np.arange(VB // 2), indexing="ij"
    )
    core = worker % CORES
    chip = 1 + worker // CORES
    near = np.where(chip == 1, 0, CHIPS - 1)
    far = np.where(chip == 1, 2, 1)
    end = np.where(chip == 1, CHIPS - 1, 0)
    each = VB // (CHIPS * CORES)

    def local(at):
        block = at // each
        home = np.where(block < 2, chip, near) * CORES + np.where(block % 2 == 0, core, 1 - core)
        return home * each + at % each

    def spread(at):
        return (np.choose(at // each, [chip, near, far, end]) * CORES + core) * each + at % each

    a, b = (spread(left), local(right)) if swap else (local(left), spread(right))
    return (a * VB + b).reshape(-1)


def scatter_terms(terms, named, tiles):
    columns = lax.axis_size("vec")
    column = lax.axis_index("vec")
    owners = lax.axis_size("amp")
    halves, rows, width = terms.shape
    each = rows // owners
    mine = terms.reshape(halves, owners, each, width).swapaxes(0, 1)
    mine = lax.all_to_all(mine, "amp", split_axis=0, concat_axis=0, tiled=True)
    mine = mine[CORES : CORES * (CHIPS - 1)].transpose(1, 2, 0, 3).reshape(halves * each, PAIRS)
    canonical = jnp.arange(PAIRS, dtype=jnp.int32)[None, :]
    one_hot = lambda to: (jnp.asarray(to, jnp.int32)[:, None] == canonical).astype(jnp.bfloat16)
    straight, turned = one_hot(target_columns(False)), one_hot(target_columns(True))
    dot = functools.partial(jnp.dot, preferred_element_type=jnp.float32)
    straight, turned = dot(mine, straight), dot(mine, turned)
    swap = named["swap"].reshape(halves, columns)
    out = named["out"].reshape(halves, columns)
    swapped = jnp.repeat(lax.dynamic_index_in_dim(swap, column, 1), each, axis=0) == 1
    placed = jnp.where(swapped, turned, straight).astype(jnp.bfloat16).reshape(halves, each, PAIRS)
    held = tiles // columns
    here = column * held + jnp.arange(held, dtype=jnp.int32)
    total = jnp.zeros((held, each, PAIRS), jnp.float32)
    for bit in range(columns):
        arrived = placed if bit == 0 else swap_columns(placed, bit, columns)
        targets = lax.dynamic_index_in_dim(out, column ^ bit, 1, keepdims=False)
        for half in range(halves):
            named_here = (here == targets[half])[:, None, None]
            total = total + jnp.where(named_here, arrived[half].astype(jnp.float32)[None], 0.0)
    return total.astype(jnp.bfloat16)


def line_local(chol, amplitudes, task_list, counts):
    tasks = lax.axis_size("amp")
    tiles = chol.shape[0]
    each = tasks // lax.axis_size("vec")
    half = tasks // 2
    classes = [(half + 1, tasks + 3), (half + 1, tasks + 2), (half, tasks + 1), (half + 2, tasks + 4)]
    classes.append((tasks, min(2 * tasks, tiles)))
    plan, named, branch = make_plan(tasks, tiles, classes, task_list, counts)
    first = {name: place[0] for name, place in plan_layout(tasks, tiles)[0].items()}
    run = lambda slots, listed: lambda: products(first, slots, listed, chol, amplitudes, plan, each)
    terms = lax.switch(branch, [run(*sizes) for sizes in classes])
    return scatter_terms(terms, named, tiles)


def integral_tile(x_rows, y_rows):
    products = lax.dot_general(
        x_rows, y_rows, (((1,), (1,)), ((), ())), preferred_element_type=jnp.float32
    )
    return (
        products.reshape(VB, VB, VB, VB).transpose(0, 2, 1, 3).reshape(PAIRS, PAIRS).astype(jnp.bfloat16)
    )


def task_term(x_rows, y_rows, amp_rows):
    products = lax.dot_general(
        amp_rows, integral_tile(x_rows, y_rows), (((1,), (1,)), ((), ())), preferred_element_type=jnp.float32
    )
    return products.astype(jnp.bfloat16)


def spread_local(chol, amplitudes, task_list, counts):
    owners = lax.axis_size("amp")
    most = task_list.shape[0] // owners
    rank = jnp.arange(owners, dtype=jnp.int32)[:, None]
    offsets = jnp.cumsum(counts) - counts
    inside = (rank >= offsets) & (rank < offsets + counts)
    starts = jnp.arange(owners, dtype=jnp.int32) * most
    fields = task_list[jnp.sum(jnp.where(inside, starts + rank - offsets, 0), axis=1)]
    trade = functools.partial(lax.all_to_all, axis_name="amp", tiled=True)
    fetch = lambda array, which: trade(jnp.take(array, which, axis=0), split_axis=0, concat_axis=0).reshape(
        -1, array.shape[2]
    )
    term = task_term(fetch(chol, fields[:, 0]), fetch(chol, fields[:, 1]), fetch(amplitudes, fields[:, 2]))
    returned = trade(term.reshape(owners, -1, PAIRS), split_axis=0, concat_axis=0)
    tiles = amplitudes.shape[0]
    chosen = (jnp.arange(tiles, dtype=jnp.int32)[:, None] == fields[:, 3][None, :]).astype(jnp.bfloat16)
    summed = jnp.dot(chosen, returned.reshape(owners, -1), preferred_element_type=jnp.float32)
    summed = summed.reshape(tiles, -1, PAIRS)
    return lax.psum_scatter(summed, "vec", scatter_dimension=0, tiled=True).astype(jnp.bfloat16)


def solution(mesh):
    placed = (P(None, "amp", "vec"), P(None, "amp", None), P(), P())
    local = line_local if mesh.shape["amp"] == CHIPS * CORES else spread_local
    return jax.shard_map(
        local, mesh=mesh, in_specs=placed, out_specs=P("vec", "amp", None), check_vma=False
    )
```

```python
import functools

import jax
import jax.numpy as jnp
import numpy as np
from jax import lax
from jax.experimental import pallas as pl
from jax.experimental.pallas import tpu as pltpu
from jax.sharding import PartitionSpec as P

VB = 32
PAIRS = VB * VB
CORES = 2
CHIPS = 4
LANES = 128
VMEM = 60 * 1024 * 1024


def plan_layout(tasks, tiles):
    fields = {}
    at = 0
    for name, size in (("order", tiles), ("local", tasks), ("spread", tasks), ("amp", tasks),
                       ("out", tasks), ("swap", tasks)):
        fields[name] = (at, size)
        at += size
    return fields, at


def popcount(bits):
    bits = bits - ((bits >> 1) & 0x55555555)
    bits = (bits & 0x33333333) + ((bits >> 2) & 0x33333333)
    bits = (bits + (bits >> 4)) & 0x0F0F0F0F
    return (bits + (bits >> 8) + (bits >> 16) + (bits >> 24)) & 0xFF


def plan_kernel(tasks, tiles, most, classes, task_ref, count_ref, plan_ref, size_ref, work):
    fields, _ = plan_layout(tasks, tiles)
    first = {name: place[0] for name, place in fields.items()}
    at = jnp.int32(0)
    for owner in range(count_ref.shape[0]):
        for entry in range(most):
            live = entry < count_ref[owner]

            @pl.when(live)
            def _():
                for column in range(4):
                    work[at * 4 + column] = task_ref[column, owner * most + entry]

            at = at + live.astype(jnp.int32)
    x = [work[task * 4] for task in range(tasks)]
    y = [work[task * 4 + 1] for task in range(tasks)]
    one = jnp.int32(1)
    codes = 1 << tasks
    code = lax.broadcasted_iota(jnp.int32, (codes // LANES, LANES), 0) * LANES + lax.broadcasted_iota(
        jnp.int32, (codes // LANES, LANES), 1
    )
    bits = jnp.zeros_like(code)
    used = jnp.int32(0)
    for task in range(tasks):
        bits = bits | jnp.where((code >> task) & 1 == 1, one << y[task], one << x[task])
        used = used | (one << y[task]) | (one << x[task])
    best = jnp.min(popcount(bits) * codes + code) & (codes - 1)
    cover = jnp.int32(0)
    for task in range(tasks):
        cover = cover | (one << jnp.where((best >> task) & 1 == 1, y[task], x[task]))
    place = jnp.int32(0)
    sizes = []
    for group in (cover, used & ~cover, ~used):
        for tile in range(tiles):
            member = (group >> tile) & 1 == 1

            @pl.when(member)
            def _():
                plan_ref[first["order"] + place] = jnp.int32(tile)
                work[4 * tasks + tile] = place

            place = place + member.astype(jnp.int32)
        sizes.append(place)
    fits = jnp.int32(len(classes) - 1)
    for at, (spread, listed) in sorted(enumerate(classes), key=lambda entry: -sum(entry[1])):
        fits = jnp.where((sizes[0] <= spread) & (sizes[1] <= listed), at, fits)
    size_ref[0] = fits
    for task in range(tasks):
        swap = (best >> task) & 1 == 0
        plan_ref[first["local"] + task] = work[4 * tasks + jnp.where(swap, y[task], x[task])]
        plan_ref[first["spread"] + task] = work[4 * tasks + jnp.where(swap, x[task], y[task])]
        plan_ref[first["amp"] + task] = work[task * 4 + 2]
        plan_ref[first["out"] + task] = work[task * 4 + 3]
        plan_ref[first["swap"] + task] = swap.astype(jnp.int32)


def make_plan(tasks, tiles, classes, task_list, counts):
    fields, length = plan_layout(tasks, tiles)
    most = task_list.shape[0] // counts.shape[0]
    smem = pl.BlockSpec(memory_space=pltpu.SMEM)
    plan, size = pl.pallas_call(
        functools.partial(plan_kernel, tasks, tiles, most, classes),
        out_shape=[jax.ShapeDtypeStruct((length,), jnp.int32), jax.ShapeDtypeStruct((1,), jnp.int32)],
        in_specs=[smem] * 2,
        out_specs=[smem] * 2,
        scratch_shapes=[pltpu.SMEM((4 * tasks + tiles,), jnp.int32)],
        name="plan",
    )(task_list.T, counts)
    return plan, {name: plan[at : at + held] for name, (at, held) in fields.items()}, size[0]


def collect_kernel(lists, plan, *refs):
    sources, refs = refs[: len(lists)], refs[len(lists) :]
    outs, refs = refs[: len(lists)], refs[len(lists) :]
    *held, sems = refs
    moves = []
    for (first, each), source, out, slot in zip(lists, sources, outs, held):
        begin = lax.axis_index("vec") * each + first
        moves += [(source.at[plan[begin + at]], slot.at[at], out.at[at]) for at in range(out.shape[0])]
    loads = [pltpu.make_async_copy(move[0], move[1], sems.at[0, at]) for at, move in enumerate(moves)]
    stores = [pltpu.make_async_copy(move[1], move[2], sems.at[1, at]) for at, move in enumerate(moves)]
    for load in loads:
        load.start()
    for load, store in zip(loads, stores):
        load.wait()
        store.start()
    for store in stores:
        store.wait()


def collect(plan, *wanted):
    shapes = [(count, *array.shape[1:]) for _, _, count, array in wanted]
    total = sum(shape[0] for shape in shapes)
    any_spec = pl.BlockSpec(memory_space=pl.ANY)
    return pl.pallas_call(
        functools.partial(collect_kernel, [want[:2] for want in wanted]),
        out_shape=[jax.ShapeDtypeStruct(shape, jnp.bfloat16) for shape in shapes],
        in_specs=[pl.BlockSpec(memory_space=pltpu.SMEM)] + [any_spec] * len(wanted),
        out_specs=[any_spec] * len(wanted),
        scratch_shapes=[pltpu.VMEM(shape, jnp.bfloat16) for shape in shapes]
        + [pltpu.SemaphoreType.DMA((2, total))],
        compiler_params=pltpu.CompilerParams(vmem_limit_bytes=VMEM),
        name="collect",
    )(plan, *[want[3] for want in wanted])


def swap_fours(blocks):
    group = lax.broadcasted_iota(jnp.int32, blocks[0].shape, 1) // VB
    for bit in (1, 2):
        right = (group & bit) != 0
        shift = bit * VB
        moved = list(blocks)
        for low in range(4):
            if low & bit:
                continue
            high = low | bit
            moved[low] = jnp.where(right, pltpu.roll(blocks[high], shift, 1), blocks[low])
            moved[high] = jnp.where(right, blocks[high], pltpu.roll(blocks[low], LANES - shift, 1))
        blocks = moved
    return blocks


ACROSS = (((1,), (1,)), ((), ()))
SOURCES = 10


def ladder_kernel(first, bits, plan, *refs):
    sources, refs = refs[:SOURCES], refs[SOURCES:]
    amp_own, amp_sib, *outs, rows, amps, products, integral, sems = refs
    own_a, own_b, sib_a, sib_b, fed_a, fed_b, sfed_a, sfed_b, mid_a, mid_b = sources
    pairs = ((own_a, own_b), (sib_a, sib_b), (fed_a, fed_b), (sfed_a, sfed_b))
    wide = (own_a, fed_a, mid_a, mid_b)
    slots, each_row, _ = own_a.shape
    each = amp_own.shape[2]
    step = pl.program_id(0)
    columns = amp_own.shape[0]
    column = lax.axis_index("vec")
    core = lax.rem(lax.axis_index("amp"), CORES)
    bit_of = lambda at: sum(jnp.where(at // each == which, bit, 0) for which, bit in enumerate(bits))
    task_of = lambda at: lax.rem(at, each) * columns + (bit_of(at) ^ column)
    part = lambda slot, side, block: rows.at[slot, side, pl.ds(block * each_row, each_row)]

    def amp_copies(task, slot):
        return [
            pltpu.make_async_copy(
                source.at[task // each, :, lax.rem(task, each)],
                amps.at[slot, :, holder],
                sems.at[slot, 2 * len(wide) + at],
            )
            for at, (source, holder) in enumerate(((amp_own, core), (amp_sib, 1 - core)))
        ]

    def start(task, slot):
        swap = plan[first["swap"] + task]
        at = plan[first["local"] + task]
        for block, (early, late) in enumerate(pairs):
            target, sem = part(slot, swap, block), sems.at[slot, block]

            @pl.when(at < slots)
            def _():
                pltpu.make_async_copy(early.at[at], target, sem).start()

            @pl.when(at >= slots)
            def _():
                pltpu.make_async_copy(late.at[at - slots], target, sem).start()

        at = plan[first["spread"] + task]
        for block, source in enumerate(wide):
            target, sem = part(slot, 1 - swap, block), sems.at[slot, len(wide) + block]
            pltpu.make_async_copy(source.at[at], target, sem).start()
        for copy in amp_copies(task, slot):
            copy.start()

    def wait(task, slot):
        swap = plan[first["swap"] + task]
        for block in range(len(wide)):
            for side, at in ((swap, block), (1 - swap, len(wide) + block)):
                pltpu.make_async_copy(own_a.at[0], part(slot, side, block), sems.at[slot, at]).wait()
        for copy in amp_copies(task, slot):
            copy.wait()

    @pl.when(step == 0)
    def _():
        start(task_of(0), 0)

    @pl.when(step + 1 < pl.num_programs(0))
    def _():
        start(task_of(step + 1), lax.rem(step + 1, 2))

    slot = lax.rem(step, 2)
    wait(task_of(step), slot)
    whole_products = lax.dot_general(
        rows[slot, 0], rows[slot, 1], ACROSS, preferred_element_type=jnp.float32
    )
    for block in range(products.shape[0]):
        products[block] = whole_products[:, block * LANES : (block + 1) * LANES]
    group = products.shape[1] // VB
    for high in range(VB // 4):
        for block in range(products.shape[0]):
            starts = [high * 4 + low for low in range(4)]
            blocks = [products[block, pl.ds(at, group, VB)].astype(jnp.bfloat16) for at in starts]
            for low, moved in enumerate(swap_fours(blocks)):
                to = (block * 4 + low) * group
                integral[to : to + group, high * LANES : (high + 1) * LANES] = moved
    upper = lax.axis_index("amp") >= CHIPS * CORES // 2
    order = [jnp.where(upper, CHIPS - 1 - chip, chip) for chip in range(CHIPS)]
    mine = jnp.concatenate([amps[slot, chip] for chip in order]).reshape(-1, amps.shape[-1])
    term = lax.dot_general(mine, integral[...], ACROSS, preferred_element_type=jnp.float32)
    for which, out in enumerate(outs):

        @pl.when(step // each == which)
        def _():
            out[0] = term.astype(jnp.bfloat16)


def ladder(first, bits, plan, blocks, amps):
    _, rows, depth = blocks[0].shape
    columns, chips, each, amp_rows, pairs = amps[0].shape
    occupied = chips * CORES * amp_rows
    side = 4 * rows
    terms = (side // VB) ** 2
    tasks = len(bits) * each

    def out_spec(which):
        half = lambda step: jnp.clip(step - which * each, 0, each - 1)
        return pl.BlockSpec((1, occupied, terms), lambda step, plan: (half(step), 0, 0))

    return pl.pallas_call(
        functools.partial(ladder_kernel, first, bits),
        out_shape=[jax.ShapeDtypeStruct((each, occupied, terms), jnp.bfloat16)] * len(bits),
        grid_spec=pltpu.PrefetchScalarGridSpec(
            num_scalar_prefetch=1,
            grid=(tasks,),
            in_specs=[pl.BlockSpec(memory_space=pl.ANY)] * (SOURCES + len(amps)),
            out_specs=[out_spec(which) for which in range(len(bits))],
            scratch_shapes=[
                pltpu.VMEM((2, 2, side, depth), jnp.bfloat16),
                pltpu.VMEM((2, chips, CORES, amp_rows, pairs), jnp.bfloat16),
                pltpu.VMEM((side // LANES, side, LANES), jnp.float32),
                pltpu.VMEM((terms, pairs), jnp.bfloat16),
                pltpu.SemaphoreType.DMA((2, 10)),
            ],
        ),
        compiler_params=pltpu.CompilerParams(vmem_limit_bytes=VMEM),
        cost_estimate=pl.CostEstimate(
            flops=tasks * 6 * (side * side * depth + occupied * terms * pairs),
            bytes_accessed=tasks * 2 * (2 * side * depth + occupied * pairs),
            transcendentals=0,
        ),
        name="ladder",
    )(plan, *blocks, *amps)


def routes():
    last = CHIPS - 1
    feed = [(0, 1), (last, last - 1)]
    middle = [(1, 2), (2, 1)]
    both = lambda hops: [(a * CORES + c, b * CORES + c) for a, b in hops for c in range(CORES)]
    sibling = [(a * CORES + c, a * CORES + 1 - c) for a in range(CHIPS) for c in range(CORES)]
    return both(feed), both(middle), sibling


def swap_columns(array, bit, columns):
    return lax.ppermute(array, "vec", perm=[(column, column ^ bit) for column in range(columns)])


def products(first, slots, listed, twice, chol, amplitudes, plan, each):
    feed, middle, sibling = routes()
    send = functools.partial(lax.ppermute, axis_name="amp")
    start = first["order"]
    (mine,) = collect(plan, (first["amp"], each, each, amplitudes))
    end = send(mine, perm=feed)
    (own_a,) = collect(plan, (start, 0, slots, chol))
    own_a, end, mine, chol = lax.optimization_barrier((own_a, end, mine, chol))
    mid_a = send(own_a, perm=middle)
    fed_a = send(own_a, perm=feed)
    (own_b,) = collect(plan, (start + slots, 0, listed - slots, chol))
    sib_a = send(own_a, perm=sibling)
    far = send(jnp.stack([mine, end]), perm=middle)
    line = jnp.stack([end, mine])
    own_b, fed_a, mid_a, sib_a, line, far = lax.optimization_barrier(
        (own_b, fed_a, mid_a, sib_a, line, far)
    )
    mid_b = send(fed_a, perm=middle)
    fed_b = send(own_b, perm=feed)
    sib_b = send(own_b, perm=sibling)
    sfed_a = send(fed_a, perm=sibling)
    amps = lax.all_gather(jnp.concatenate([line, far]), "vec", axis=0, tiled=False)
    amps = (amps, send(amps, perm=sibling))
    fed_b, mid_b, sib_b, sfed_a, amps = lax.optimization_barrier((fed_b, mid_b, sib_b, sfed_a, amps))
    sfed_b = send(fed_b, perm=sibling)
    blocks = (own_a, own_b, sib_a, sib_b, fed_a, fed_b, sfed_a, sfed_b, mid_a, mid_b)
    columns = lax.axis_size("vec")
    away = list(range(columns))[:0:-1]
    arrived = []
    for call in ([away, [0]] if twice else [[*away, 0]]):
        for bit, term in zip(call, ladder(first, call, plan, blocks, amps)):
            arrived.append(swap_columns(term, bit, columns) if bit else term)
    return sum(term.astype(jnp.float32) for term in arrived).astype(jnp.bfloat16)


def target_columns(swap):
    worker, right, left = np.meshgrid(
        np.arange(2 * CORES), np.arange(VB // 2), np.arange(VB // 2), indexing="ij"
    )
    core = worker % CORES
    chip = 1 + worker // CORES
    near = np.where(chip == 1, 0, CHIPS - 1)
    far = np.where(chip == 1, 2, 1)
    end = np.where(chip == 1, CHIPS - 1, 0)
    each = VB // (CHIPS * CORES)

    def local(at):
        block = at // each
        home = np.where(block < 2, chip, near) * CORES + np.where(block % 2 == 0, core, 1 - core)
        return home * each + at % each

    def spread(at):
        return (np.choose(at // each, [chip, near, far, end]) * CORES + core) * each + at % each

    a, b = (spread(left), local(right)) if swap else (local(left), spread(right))
    return (a * VB + b).reshape(-1)


def scatter_terms(terms, named, tiles):
    columns = lax.axis_size("vec")
    column = lax.axis_index("vec")
    owners = lax.axis_size("amp")
    halves, rows, width = terms.shape
    each = rows // owners
    mine = terms.reshape(halves, owners, each, width).swapaxes(0, 1)
    mine = lax.all_to_all(mine, "amp", split_axis=0, concat_axis=0, tiled=True)
    mine = mine[CORES : CORES * (CHIPS - 1)].transpose(1, 2, 0, 3).reshape(halves * each, PAIRS)
    canonical = jnp.arange(PAIRS, dtype=jnp.int32)[None, :]
    one_hot = lambda to: (jnp.asarray(to, jnp.int32)[:, None] == canonical).astype(jnp.bfloat16)
    straight, turned = one_hot(target_columns(False)), one_hot(target_columns(True))
    dot = functools.partial(jnp.dot, preferred_element_type=jnp.float32)
    straight, turned = dot(mine, straight), dot(mine, turned)
    swap = named["swap"].reshape(halves, columns)
    out = named["out"].reshape(halves, columns)
    swapped = jnp.repeat(lax.dynamic_index_in_dim(swap, column, 1), each, axis=0) == 1
    placed = jnp.where(swapped, turned, straight).astype(jnp.bfloat16).reshape(halves, each, PAIRS)
    held = tiles // columns
    here = column * held + jnp.arange(held, dtype=jnp.int32)
    total = jnp.zeros((held, each, PAIRS), jnp.float32)
    for bit in range(columns):
        arrived = placed if bit == 0 else swap_columns(placed, bit, columns)
        targets = lax.dynamic_index_in_dim(out, column ^ bit, 1, keepdims=False)
        for half in range(halves):
            named_here = (here == targets[half])[:, None, None]
            total = total + jnp.where(named_here, arrived[half].astype(jnp.float32)[None], 0.0)
    return total.astype(jnp.bfloat16)


def line_local(chol, amplitudes, task_list, counts):
    tasks = lax.axis_size("amp")
    tiles = chol.shape[0]
    each = tasks // lax.axis_size("vec")
    half = tasks // 2
    classes = [(half + 1, tasks + 3), (half + 1, tasks + 2), (half, tasks + 1), (half + 2, tasks + 4)]
    classes.append((tasks, min(2 * tasks, tiles)))
    plan, named, branch = make_plan(tasks, tiles, classes, task_list, counts)
    first = {name: place[0] for name, place in plan_layout(tasks, tiles)[0].items()}
    def run(slots, listed):
        twice = slots < tasks
        return lambda: products(first, slots, listed, twice, chol, amplitudes, plan, each)

    terms = lax.switch(branch, [run(*sizes) for sizes in classes])
    return scatter_terms(terms, named, tiles)


def integral_tile(x_rows, y_rows):
    products = lax.dot_general(
        x_rows, y_rows, (((1,), (1,)), ((), ())), preferred_element_type=jnp.float32
    )
    return (
        products.reshape(VB, VB, VB, VB).transpose(0, 2, 1, 3).reshape(PAIRS, PAIRS).astype(jnp.bfloat16)
    )


def task_term(x_rows, y_rows, amp_rows):
    products = lax.dot_general(
        amp_rows, integral_tile(x_rows, y_rows), (((1,), (1,)), ((), ())), preferred_element_type=jnp.float32
    )
    return products.astype(jnp.bfloat16)


def spread_local(chol, amplitudes, task_list, counts):
    owners = lax.axis_size("amp")
    most = task_list.shape[0] // owners
    rank = jnp.arange(owners, dtype=jnp.int32)[:, None]
    offsets = jnp.cumsum(counts) - counts
    inside = (rank >= offsets) & (rank < offsets + counts)
    starts = jnp.arange(owners, dtype=jnp.int32) * most
    fields = task_list[jnp.sum(jnp.where(inside, starts + rank - offsets, 0), axis=1)]
    trade = functools.partial(lax.all_to_all, axis_name="amp", tiled=True)
    fetch = lambda array, which: trade(jnp.take(array, which, axis=0), split_axis=0, concat_axis=0).reshape(
        -1, array.shape[2]
    )
    term = task_term(fetch(chol, fields[:, 0]), fetch(chol, fields[:, 1]), fetch(amplitudes, fields[:, 2]))
    returned = trade(term.reshape(owners, -1, PAIRS), split_axis=0, concat_axis=0)
    tiles = amplitudes.shape[0]
    chosen = (jnp.arange(tiles, dtype=jnp.int32)[:, None] == fields[:, 3][None, :]).astype(jnp.bfloat16)
    summed = jnp.dot(chosen, returned.reshape(owners, -1), preferred_element_type=jnp.float32)
    summed = summed.reshape(tiles, -1, PAIRS)
    return lax.psum_scatter(summed, "vec", scatter_dimension=0, tiled=True).astype(jnp.bfloat16)


def solution(mesh):
    placed = (P(None, "amp", "vec"), P(None, "amp", None), P(), P())
    local = line_local if mesh.shape["amp"] == CHIPS * CORES else spread_local
    return jax.shard_map(
        local, mesh=mesh, in_specs=placed, out_specs=P("vec", "amp", None), check_vma=False
    )
```

```python
import functools

import jax
import jax.numpy as jnp
import numpy as np
from jax import lax
from jax.experimental import pallas as pl
from jax.experimental.pallas import tpu as pltpu
from jax.sharding import PartitionSpec as P

VB = 32
PAIRS = VB * VB
CORES = 2
CHIPS = 4
LANES = 128
VMEM = 60 * 1024 * 1024


def plan_layout(tasks, tiles):
    fields = {}
    at = 0
    for name, size in (("order", tiles), ("local", tasks), ("spread", tasks), ("amp", tasks),
                       ("out", tasks), ("swap", tasks)):
        fields[name] = (at, size)
        at += size
    return fields, at


def popcount(bits):
    bits = bits - ((bits >> 1) & 0x55555555)
    bits = (bits & 0x33333333) + ((bits >> 2) & 0x33333333)
    bits = (bits + (bits >> 4)) & 0x0F0F0F0F
    return (bits + (bits >> 8) + (bits >> 16) + (bits >> 24)) & 0xFF


def plan_kernel(tasks, tiles, most, classes, task_ref, count_ref, plan_ref, size_ref, work):
    fields, _ = plan_layout(tasks, tiles)
    first = {name: place[0] for name, place in fields.items()}
    at = jnp.int32(0)
    for owner in range(count_ref.shape[0]):
        for entry in range(most):
            live = entry < count_ref[owner]

            @pl.when(live)
            def _():
                for column in range(4):
                    work[at * 4 + column] = task_ref[column, owner * most + entry]

            at = at + live.astype(jnp.int32)
    x = [work[task * 4] for task in range(tasks)]
    y = [work[task * 4 + 1] for task in range(tasks)]
    one = jnp.int32(1)
    codes = 1 << tasks
    code = lax.broadcasted_iota(jnp.int32, (codes // LANES, LANES), 0) * LANES + lax.broadcasted_iota(
        jnp.int32, (codes // LANES, LANES), 1
    )
    bits = jnp.zeros_like(code)
    used = jnp.int32(0)
    for task in range(tasks):
        bits = bits | jnp.where((code >> task) & 1 == 1, one << y[task], one << x[task])
        used = used | (one << y[task]) | (one << x[task])
    best = jnp.min(popcount(bits) * codes + code) & (codes - 1)
    cover = jnp.int32(0)
    for task in range(tasks):
        cover = cover | (one << jnp.where((best >> task) & 1 == 1, y[task], x[task]))
    place = jnp.int32(0)
    sizes = []
    for group in (cover, used & ~cover, ~used):
        for tile in range(tiles):
            member = (group >> tile) & 1 == 1

            @pl.when(member)
            def _():
                plan_ref[first["order"] + place] = jnp.int32(tile)
                work[4 * tasks + tile] = place

            place = place + member.astype(jnp.int32)
        sizes.append(place)
    fits = jnp.int32(len(classes) - 1)
    for at, (spread, listed) in sorted(enumerate(classes), key=lambda entry: -sum(entry[1])):
        fits = jnp.where((sizes[0] <= spread) & (sizes[1] <= listed), at, fits)
    size_ref[0] = fits
    for task in range(tasks):
        swap = (best >> task) & 1 == 0
        plan_ref[first["local"] + task] = work[4 * tasks + jnp.where(swap, y[task], x[task])]
        plan_ref[first["spread"] + task] = work[4 * tasks + jnp.where(swap, x[task], y[task])]
        plan_ref[first["amp"] + task] = work[task * 4 + 2]
        plan_ref[first["out"] + task] = work[task * 4 + 3]
        plan_ref[first["swap"] + task] = swap.astype(jnp.int32)


def make_plan(tasks, tiles, classes, task_list, counts):
    fields, length = plan_layout(tasks, tiles)
    most = task_list.shape[0] // counts.shape[0]
    smem = pl.BlockSpec(memory_space=pltpu.SMEM)
    plan, size = pl.pallas_call(
        functools.partial(plan_kernel, tasks, tiles, most, classes),
        out_shape=[jax.ShapeDtypeStruct((length,), jnp.int32), jax.ShapeDtypeStruct((1,), jnp.int32)],
        in_specs=[smem] * 2,
        out_specs=[smem] * 2,
        scratch_shapes=[pltpu.SMEM((4 * tasks + tiles,), jnp.int32)],
        name="plan",
    )(task_list.T, counts)
    return plan, {name: plan[at : at + held] for name, (at, held) in fields.items()}, size[0]


def collect_kernel(lists, plan, *refs):
    sources, refs = refs[: len(lists)], refs[len(lists) :]
    outs, refs = refs[: len(lists)], refs[len(lists) :]
    *held, sems = refs
    moves = []
    for (first, each), source, out, slot in zip(lists, sources, outs, held):
        begin = lax.axis_index("vec") * each + first
        moves += [(source.at[plan[begin + at]], slot.at[at], out.at[at]) for at in range(out.shape[0])]
    loads = [pltpu.make_async_copy(move[0], move[1], sems.at[0, at]) for at, move in enumerate(moves)]
    stores = [pltpu.make_async_copy(move[1], move[2], sems.at[1, at]) for at, move in enumerate(moves)]
    for load in loads:
        load.start()
    for load, store in zip(loads, stores):
        load.wait()
        store.start()
    for store in stores:
        store.wait()


def collect(plan, *wanted):
    shapes = [(count, *array.shape[1:]) for _, _, count, array in wanted]
    total = sum(shape[0] for shape in shapes)
    any_spec = pl.BlockSpec(memory_space=pl.ANY)
    return pl.pallas_call(
        functools.partial(collect_kernel, [want[:2] for want in wanted]),
        out_shape=[jax.ShapeDtypeStruct(shape, jnp.bfloat16) for shape in shapes],
        in_specs=[pl.BlockSpec(memory_space=pltpu.SMEM)] + [any_spec] * len(wanted),
        out_specs=[any_spec] * len(wanted),
        scratch_shapes=[pltpu.VMEM(shape, jnp.bfloat16) for shape in shapes]
        + [pltpu.SemaphoreType.DMA((2, total))],
        compiler_params=pltpu.CompilerParams(vmem_limit_bytes=VMEM),
        name="collect",
    )(plan, *[want[3] for want in wanted])


def swap_fours(blocks):
    group = lax.broadcasted_iota(jnp.int32, blocks[0].shape, 1) // VB
    for bit in (1, 2):
        right = (group & bit) != 0
        shift = bit * VB
        moved = list(blocks)
        for low in range(4):
            if low & bit:
                continue
            high = low | bit
            moved[low] = jnp.where(right, pltpu.roll(blocks[high], shift, 1), blocks[low])
            moved[high] = jnp.where(right, blocks[high], pltpu.roll(blocks[low], LANES - shift, 1))
        blocks = moved
    return blocks


ACROSS = (((1,), (1,)), ((), ()))
SOURCES = 10


def ladder_kernel(first, bits, plan, *refs):
    sources, refs = refs[:SOURCES], refs[SOURCES:]
    amp_own, amp_sib, *outs, rows, amps, products, integral, sems = refs
    own_a, own_b, sib_a, sib_b, fed_a, fed_b, sfed_a, sfed_b, mid_a, mid_b = sources
    pairs = ((own_a, own_b), (sib_a, sib_b), (fed_a, fed_b), (sfed_a, sfed_b))
    wide = (own_a, fed_a, mid_a, mid_b)
    slots, each_row, _ = own_a.shape
    each = amp_own.shape[2]
    step = pl.program_id(0)
    columns = amp_own.shape[0]
    column = lax.axis_index("vec")
    core = lax.rem(lax.axis_index("amp"), CORES)
    bit_of = lambda at: sum(jnp.where(at // each == which, bit, 0) for which, bit in enumerate(bits))
    task_of = lambda at: lax.rem(at, each) * columns + (bit_of(at) ^ column)
    part = lambda slot, side, block: rows.at[slot, side, pl.ds(block * each_row, each_row)]

    def amp_copies(task, slot):
        return [
            pltpu.make_async_copy(
                source.at[task // each, :, lax.rem(task, each)],
                amps.at[slot, :, holder],
                sems.at[slot, 2 * len(wide) + at],
            )
            for at, (source, holder) in enumerate(((amp_own, core), (amp_sib, 1 - core)))
        ]

    def start(task, slot):
        swap = plan[first["swap"] + task]
        at = plan[first["local"] + task]
        for block, (early, late) in enumerate(pairs):
            target, sem = part(slot, swap, block), sems.at[slot, block]

            @pl.when(at < slots)
            def _():
                pltpu.make_async_copy(early.at[at], target, sem).start()

            @pl.when(at >= slots)
            def _():
                pltpu.make_async_copy(late.at[at - slots], target, sem).start()

        at = plan[first["spread"] + task]
        for block, source in enumerate(wide):
            target, sem = part(slot, 1 - swap, block), sems.at[slot, len(wide) + block]
            pltpu.make_async_copy(source.at[at], target, sem).start()
        for copy in amp_copies(task, slot):
            copy.start()

    def wait(task, slot):
        swap = plan[first["swap"] + task]
        for block in range(len(wide)):
            for side, at in ((swap, block), (1 - swap, len(wide) + block)):
                pltpu.make_async_copy(own_a.at[0], part(slot, side, block), sems.at[slot, at]).wait()
        for copy in amp_copies(task, slot):
            copy.wait()

    @pl.when(step == 0)
    def _():
        start(task_of(0), 0)

    @pl.when(step + 1 < pl.num_programs(0))
    def _():
        start(task_of(step + 1), lax.rem(step + 1, 2))

    slot = lax.rem(step, 2)
    wait(task_of(step), slot)
    whole_products = lax.dot_general(
        rows[slot, 0], rows[slot, 1], ACROSS, preferred_element_type=jnp.float32
    )
    for block in range(products.shape[0]):
        products[block] = whole_products[:, block * LANES : (block + 1) * LANES]
    group = products.shape[1] // VB
    for high in range(VB // 4):
        for block in range(products.shape[0]):
            starts = [high * 4 + low for low in range(4)]
            blocks = [products[block, pl.ds(at, group, VB)].astype(jnp.bfloat16) for at in starts]
            for low, moved in enumerate(swap_fours(blocks)):
                to = (block * 4 + low) * group
                integral[to : to + group, high * LANES : (high + 1) * LANES] = moved
    upper = lax.axis_index("amp") >= CHIPS * CORES // 2
    order = [jnp.where(upper, CHIPS - 1 - chip, chip) for chip in range(CHIPS)]
    mine = jnp.concatenate([amps[slot, chip] for chip in order]).reshape(-1, amps.shape[-1])
    term = lax.dot_general(mine, integral[...], ACROSS, preferred_element_type=jnp.float32)
    for which, out in enumerate(outs):

        @pl.when(step // each == which)
        def _():
            out[0] = term.astype(jnp.bfloat16)


def ladder(first, bits, plan, blocks, amps):
    _, rows, depth = blocks[0].shape
    columns, chips, each, amp_rows, pairs = amps[0].shape
    occupied = chips * CORES * amp_rows
    side = 4 * rows
    terms = (side // VB) ** 2
    tasks = len(bits) * each

    def out_spec(which):
        half = lambda step: jnp.clip(step - which * each, 0, each - 1)
        return pl.BlockSpec((1, occupied, terms), lambda step, plan: (half(step), 0, 0))

    return pl.pallas_call(
        functools.partial(ladder_kernel, first, bits),
        out_shape=[jax.ShapeDtypeStruct((each, occupied, terms), jnp.bfloat16)] * len(bits),
        grid_spec=pltpu.PrefetchScalarGridSpec(
            num_scalar_prefetch=1,
            grid=(tasks,),
            in_specs=[pl.BlockSpec(memory_space=pl.ANY)] * (SOURCES + len(amps)),
            out_specs=[out_spec(which) for which in range(len(bits))],
            scratch_shapes=[
                pltpu.VMEM((2, 2, side, depth), jnp.bfloat16),
                pltpu.VMEM((2, chips, CORES, amp_rows, pairs), jnp.bfloat16),
                pltpu.VMEM((side // LANES, side, LANES), jnp.float32),
                pltpu.VMEM((terms, pairs), jnp.bfloat16),
                pltpu.SemaphoreType.DMA((2, 10)),
            ],
        ),
        compiler_params=pltpu.CompilerParams(vmem_limit_bytes=VMEM),
        cost_estimate=pl.CostEstimate(
            flops=tasks * 6 * (side * side * depth + occupied * terms * pairs),
            bytes_accessed=tasks * 2 * (2 * side * depth + occupied * pairs),
            transcendentals=0,
        ),
        name="ladder",
    )(plan, *blocks, *amps)


def routes():
    last = CHIPS - 1
    feed = [(0, 1), (last, last - 1)]
    middle = [(1, 2), (2, 1)]
    both = lambda hops: [(a * CORES + c, b * CORES + c) for a, b in hops for c in range(CORES)]
    sibling = [(a * CORES + c, a * CORES + 1 - c) for a in range(CHIPS) for c in range(CORES)]
    return both(feed), both(middle), sibling


def swap_columns(array, bit, columns):
    return lax.ppermute(array, "vec", perm=[(column, column ^ bit) for column in range(columns)])


def products(first, slots, listed, twice, chol, amplitudes, plan, each):
    feed, middle, sibling = routes()
    send = functools.partial(lax.ppermute, axis_name="amp")
    start = first["order"]
    (mine,) = collect(plan, (first["amp"], each, each, amplitudes))
    end = send(mine, perm=feed)
    (own_a,) = collect(plan, (start, 0, slots, chol))
    own_a, chol = lax.optimization_barrier((own_a, chol))
    mid_a = send(own_a, perm=middle)
    fed_a = send(own_a, perm=feed)
    (own_b,) = collect(plan, (start + slots, 0, listed - slots, chol))
    sib_a = send(own_a, perm=sibling)
    over = send(mine, perm=middle)
    far = send(end, perm=middle)
    line = jnp.stack([end, mine, over])
    own_b, fed_a, mid_a, sib_a, line, far = lax.optimization_barrier(
        (own_b, fed_a, mid_a, sib_a, line, far)
    )
    mid_b = send(fed_a, perm=middle)
    fed_b = send(own_b, perm=feed)
    sib_b = send(own_b, perm=sibling)
    sfed_a = send(fed_a, perm=sibling)
    amps = lax.all_gather(jnp.concatenate([line, far[None]]), "vec", axis=0, tiled=False)
    amps = (amps, send(amps, perm=sibling))
    fed_b, mid_b, sib_b, sfed_a, amps = lax.optimization_barrier((fed_b, mid_b, sib_b, sfed_a, amps))
    sfed_b = send(fed_b, perm=sibling)
    blocks = (own_a, own_b, sib_a, sib_b, fed_a, fed_b, sfed_a, sfed_b, mid_a, mid_b)
    columns = lax.axis_size("vec")
    away = list(range(columns))[:0:-1]
    arrived = []
    for call in ([away, [0]] if twice else [[*away, 0]]):
        for bit, term in zip(call, ladder(first, call, plan, blocks, amps)):
            arrived.append(swap_columns(term, bit, columns) if bit else term)
    return sum(term.astype(jnp.float32) for term in arrived).astype(jnp.bfloat16)


def target_columns(swap):
    worker, right, left = np.meshgrid(
        np.arange(2 * CORES), np.arange(VB // 2), np.arange(VB // 2), indexing="ij"
    )
    core = worker % CORES
    chip = 1 + worker // CORES
    near = np.where(chip == 1, 0, CHIPS - 1)
    far = np.where(chip == 1, 2, 1)
    end = np.where(chip == 1, CHIPS - 1, 0)
    each = VB // (CHIPS * CORES)

    def local(at):
        block = at // each
        home = np.where(block < 2, chip, near) * CORES + np.where(block % 2 == 0, core, 1 - core)
        return home * each + at % each

    def spread(at):
        return (np.choose(at // each, [chip, near, far, end]) * CORES + core) * each + at % each

    a, b = (spread(left), local(right)) if swap else (local(left), spread(right))
    return (a * VB + b).reshape(-1)


def scatter_terms(terms, named, tiles):
    columns = lax.axis_size("vec")
    column = lax.axis_index("vec")
    owners = lax.axis_size("amp")
    halves, rows, width = terms.shape
    each = rows // owners
    mine = terms.reshape(halves, owners, each, width).swapaxes(0, 1)
    mine = lax.all_to_all(mine, "amp", split_axis=0, concat_axis=0, tiled=True)
    mine = mine[CORES : CORES * (CHIPS - 1)].transpose(1, 2, 0, 3).reshape(halves * each, PAIRS)
    canonical = jnp.arange(PAIRS, dtype=jnp.int32)[None, :]
    one_hot = lambda to: (jnp.asarray(to, jnp.int32)[:, None] == canonical).astype(jnp.bfloat16)
    straight, turned = one_hot(target_columns(False)), one_hot(target_columns(True))
    dot = functools.partial(jnp.dot, preferred_element_type=jnp.float32)
    straight, turned = dot(mine, straight), dot(mine, turned)
    swap = named["swap"].reshape(halves, columns)
    out = named["out"].reshape(halves, columns)
    swapped = jnp.repeat(lax.dynamic_index_in_dim(swap, column, 1), each, axis=0) == 1
    placed = jnp.where(swapped, turned, straight).astype(jnp.bfloat16).reshape(halves, each, PAIRS)
    held = tiles // columns
    here = column * held + jnp.arange(held, dtype=jnp.int32)
    total = jnp.zeros((held, each, PAIRS), jnp.float32)
    for bit in range(columns):
        arrived = placed if bit == 0 else swap_columns(placed, bit, columns)
        targets = lax.dynamic_index_in_dim(out, column ^ bit, 1, keepdims=False)
        for half in range(halves):
            named_here = (here == targets[half])[:, None, None]
            total = total + jnp.where(named_here, arrived[half].astype(jnp.float32)[None], 0.0)
    return total.astype(jnp.bfloat16)


def line_local(chol, amplitudes, task_list, counts):
    tasks = lax.axis_size("amp")
    tiles = chol.shape[0]
    each = tasks // lax.axis_size("vec")
    half = tasks // 2
    classes = [(half + 1, tasks + 3), (half + 1, tasks + 2), (half, tasks + 1), (half + 2, tasks + 4)]
    classes.append((tasks, min(2 * tasks, tiles)))
    plan, named, branch = make_plan(tasks, tiles, classes, task_list, counts)
    first = {name: place[0] for name, place in plan_layout(tasks, tiles)[0].items()}
    def run(slots, listed):
        twice = slots < tasks
        return lambda: products(first, slots, listed, twice, chol, amplitudes, plan, each)

    terms = lax.switch(branch, [run(*sizes) for sizes in classes])
    return scatter_terms(terms, named, tiles)


def integral_tile(x_rows, y_rows):
    products = lax.dot_general(
        x_rows, y_rows, (((1,), (1,)), ((), ())), preferred_element_type=jnp.float32
    )
    return (
        products.reshape(VB, VB, VB, VB).transpose(0, 2, 1, 3).reshape(PAIRS, PAIRS).astype(jnp.bfloat16)
    )


def task_term(x_rows, y_rows, amp_rows):
    products = lax.dot_general(
        amp_rows, integral_tile(x_rows, y_rows), (((1,), (1,)), ((), ())), preferred_element_type=jnp.float32
    )
    return products.astype(jnp.bfloat16)


def spread_local(chol, amplitudes, task_list, counts):
    owners = lax.axis_size("amp")
    most = task_list.shape[0] // owners
    rank = jnp.arange(owners, dtype=jnp.int32)[:, None]
    offsets = jnp.cumsum(counts) - counts
    inside = (rank >= offsets) & (rank < offsets + counts)
    starts = jnp.arange(owners, dtype=jnp.int32) * most
    fields = task_list[jnp.sum(jnp.where(inside, starts + rank - offsets, 0), axis=1)]
    trade = functools.partial(lax.all_to_all, axis_name="amp", tiled=True)
    fetch = lambda array, which: trade(jnp.take(array, which, axis=0), split_axis=0, concat_axis=0).reshape(
        -1, array.shape[2]
    )
    term = task_term(fetch(chol, fields[:, 0]), fetch(chol, fields[:, 1]), fetch(amplitudes, fields[:, 2]))
    returned = trade(term.reshape(owners, -1, PAIRS), split_axis=0, concat_axis=0)
    tiles = amplitudes.shape[0]
    chosen = (jnp.arange(tiles, dtype=jnp.int32)[:, None] == fields[:, 3][None, :]).astype(jnp.bfloat16)
    summed = jnp.dot(chosen, returned.reshape(owners, -1), preferred_element_type=jnp.float32)
    summed = summed.reshape(tiles, -1, PAIRS)
    return lax.psum_scatter(summed, "vec", scatter_dimension=0, tiled=True).astype(jnp.bfloat16)


def solution(mesh):
    placed = (P(None, "amp", "vec"), P(None, "amp", None), P(), P())
    local = line_local if mesh.shape["amp"] == CHIPS * CORES else spread_local
    return jax.shard_map(
        local, mesh=mesh, in_specs=placed, out_specs=P("vec", "amp", None), check_vma=False
    )
```

```python
import functools

import jax
import jax.numpy as jnp
import numpy as np
from jax import lax
from jax.experimental import pallas as pl
from jax.experimental.pallas import tpu as pltpu
from jax.sharding import PartitionSpec as P

VB = 32
PAIRS = VB * VB
CORES = 2
CHIPS = 4
LANES = 128
VMEM = 60 * 1024 * 1024


def plan_layout(tasks, tiles):
    fields = {}
    at = 0
    for name, size in (("order", tiles), ("local", tasks), ("spread", tasks), ("amp", tasks),
                       ("out", tasks), ("swap", tasks)):
        fields[name] = (at, size)
        at += size
    return fields, at


def popcount(bits):
    bits = bits - ((bits >> 1) & 0x55555555)
    bits = (bits & 0x33333333) + ((bits >> 2) & 0x33333333)
    bits = (bits + (bits >> 4)) & 0x0F0F0F0F
    return (bits + (bits >> 8) + (bits >> 16) + (bits >> 24)) & 0xFF


def plan_kernel(tasks, tiles, most, classes, task_ref, count_ref, plan_ref, size_ref, work):
    fields, _ = plan_layout(tasks, tiles)
    first = {name: place[0] for name, place in fields.items()}
    at = jnp.int32(0)
    for owner in range(count_ref.shape[0]):
        for entry in range(most):
            live = entry < count_ref[owner]

            @pl.when(live)
            def _():
                for column in range(4):
                    work[at * 4 + column] = task_ref[column, owner * most + entry]

            at = at + live.astype(jnp.int32)
    x = [work[task * 4] for task in range(tasks)]
    y = [work[task * 4 + 1] for task in range(tasks)]
    one = jnp.int32(1)
    codes = 1 << tasks
    code = lax.broadcasted_iota(jnp.int32, (codes // LANES, LANES), 0) * LANES + lax.broadcasted_iota(
        jnp.int32, (codes // LANES, LANES), 1
    )
    bits = jnp.zeros_like(code)
    used = jnp.int32(0)
    for task in range(tasks):
        bits = bits | jnp.where((code >> task) & 1 == 1, one << y[task], one << x[task])
        used = used | (one << y[task]) | (one << x[task])
    best = jnp.min(popcount(bits) * codes + code) & (codes - 1)
    cover = jnp.int32(0)
    for task in range(tasks):
        cover = cover | (one << jnp.where((best >> task) & 1 == 1, y[task], x[task]))
    place = jnp.int32(0)
    sizes = []
    for group in (cover, used & ~cover, ~used):
        for tile in range(tiles):
            member = (group >> tile) & 1 == 1

            @pl.when(member)
            def _():
                plan_ref[first["order"] + place] = jnp.int32(tile)
                work[4 * tasks + tile] = place

            place = place + member.astype(jnp.int32)
        sizes.append(place)
    fits = jnp.int32(len(classes) - 1)
    for at, (spread, listed) in sorted(enumerate(classes), key=lambda entry: -sum(entry[1])):
        fits = jnp.where((sizes[0] <= spread) & (sizes[1] <= listed), at, fits)
    size_ref[0] = fits
    for task in range(tasks):
        swap = (best >> task) & 1 == 0
        plan_ref[first["local"] + task] = work[4 * tasks + jnp.where(swap, y[task], x[task])]
        plan_ref[first["spread"] + task] = work[4 * tasks + jnp.where(swap, x[task], y[task])]
        plan_ref[first["amp"] + task] = work[task * 4 + 2]
        plan_ref[first["out"] + task] = work[task * 4 + 3]
        plan_ref[first["swap"] + task] = swap.astype(jnp.int32)


def make_plan(tasks, tiles, classes, task_list, counts):
    fields, length = plan_layout(tasks, tiles)
    most = task_list.shape[0] // counts.shape[0]
    smem = pl.BlockSpec(memory_space=pltpu.SMEM)
    plan, size = pl.pallas_call(
        functools.partial(plan_kernel, tasks, tiles, most, classes),
        out_shape=[jax.ShapeDtypeStruct((length,), jnp.int32), jax.ShapeDtypeStruct((1,), jnp.int32)],
        in_specs=[smem] * 2,
        out_specs=[smem] * 2,
        scratch_shapes=[pltpu.SMEM((4 * tasks + tiles,), jnp.int32)],
        name="plan",
    )(task_list.T, counts)
    return plan, {name: plan[at : at + held] for name, (at, held) in fields.items()}, size[0]


def collect_kernel(lists, plan, *refs):
    sources, refs = refs[: len(lists)], refs[len(lists) :]
    outs, refs = refs[: len(lists)], refs[len(lists) :]
    *held, sems = refs
    moves = []
    for (first, each), source, out, slot in zip(lists, sources, outs, held):
        begin = lax.axis_index("vec") * each + first
        moves += [(source.at[plan[begin + at]], slot.at[at], out.at[at]) for at in range(out.shape[0])]
    loads = [pltpu.make_async_copy(move[0], move[1], sems.at[0, at]) for at, move in enumerate(moves)]
    stores = [pltpu.make_async_copy(move[1], move[2], sems.at[1, at]) for at, move in enumerate(moves)]
    for load in loads:
        load.start()
    for load, store in zip(loads, stores):
        load.wait()
        store.start()
    for store in stores:
        store.wait()


def collect(plan, *wanted):
    shapes = [(count, *array.shape[1:]) for _, _, count, array in wanted]
    total = sum(shape[0] for shape in shapes)
    any_spec = pl.BlockSpec(memory_space=pl.ANY)
    return pl.pallas_call(
        functools.partial(collect_kernel, [want[:2] for want in wanted]),
        out_shape=[jax.ShapeDtypeStruct(shape, jnp.bfloat16) for shape in shapes],
        in_specs=[pl.BlockSpec(memory_space=pltpu.SMEM)] + [any_spec] * len(wanted),
        out_specs=[any_spec] * len(wanted),
        scratch_shapes=[pltpu.VMEM(shape, jnp.bfloat16) for shape in shapes]
        + [pltpu.SemaphoreType.DMA((2, total))],
        compiler_params=pltpu.CompilerParams(vmem_limit_bytes=VMEM),
        name="collect",
    )(plan, *[want[3] for want in wanted])


def swap_fours(blocks):
    group = lax.broadcasted_iota(jnp.int32, blocks[0].shape, 1) // VB
    for bit in (1, 2):
        right = (group & bit) != 0
        shift = bit * VB
        moved = list(blocks)
        for low in range(4):
            if low & bit:
                continue
            high = low | bit
            moved[low] = jnp.where(right, pltpu.roll(blocks[high], shift, 1), blocks[low])
            moved[high] = jnp.where(right, blocks[high], pltpu.roll(blocks[low], LANES - shift, 1))
        blocks = moved
    return blocks


ACROSS = (((1,), (1,)), ((), ()))
SOURCES = 10


def ladder_kernel(first, bits, plan, *refs):
    sources, refs = refs[:SOURCES], refs[SOURCES:]
    amp_own, amp_sib, *outs, rows, amps, products, integral, sems = refs
    own_a, own_b, sib_a, sib_b, fed_a, fed_b, sfed_a, sfed_b, mid_a, mid_b = sources
    pairs = ((own_a, own_b), (sib_a, sib_b), (fed_a, fed_b), (sfed_a, sfed_b))
    wide = (own_a, fed_a, mid_a, mid_b)
    slots, each_row, _ = own_a.shape
    each = amp_own.shape[2]
    step = pl.program_id(0)
    columns = amp_own.shape[0]
    column = lax.axis_index("vec")
    core = lax.rem(lax.axis_index("amp"), CORES)
    bit_of = lambda at: sum(jnp.where(at // each == which, bit, 0) for which, bit in enumerate(bits))
    task_of = lambda at: lax.rem(at, each) * columns + (bit_of(at) ^ column)
    part = lambda slot, side, block: rows.at[slot, side, pl.ds(block * each_row, each_row)]

    def amp_copies(task, slot):
        return [
            pltpu.make_async_copy(
                source.at[task // each, :, lax.rem(task, each)],
                amps.at[slot, :, holder],
                sems.at[slot, 2 * len(wide) + at],
            )
            for at, (source, holder) in enumerate(((amp_own, core), (amp_sib, 1 - core)))
        ]

    def start(task, slot):
        swap = plan[first["swap"] + task]
        at = plan[first["local"] + task]
        for block, (early, late) in enumerate(pairs):
            target, sem = part(slot, swap, block), sems.at[slot, block]

            @pl.when(at < slots)
            def _():
                pltpu.make_async_copy(early.at[at], target, sem).start()

            @pl.when(at >= slots)
            def _():
                pltpu.make_async_copy(late.at[at - slots], target, sem).start()

        at = plan[first["spread"] + task]
        for block, source in enumerate(wide):
            target, sem = part(slot, 1 - swap, block), sems.at[slot, len(wide) + block]
            pltpu.make_async_copy(source.at[at], target, sem).start()
        for copy in amp_copies(task, slot):
            copy.start()

    def wait(task, slot):
        swap = plan[first["swap"] + task]
        for block in range(len(wide)):
            for side, at in ((swap, block), (1 - swap, len(wide) + block)):
                pltpu.make_async_copy(own_a.at[0], part(slot, side, block), sems.at[slot, at]).wait()
        for copy in amp_copies(task, slot):
            copy.wait()

    @pl.when(step == 0)
    def _():
        start(task_of(0), 0)

    @pl.when(step + 1 < pl.num_programs(0))
    def _():
        start(task_of(step + 1), lax.rem(step + 1, 2))

    slot = lax.rem(step, 2)
    wait(task_of(step), slot)
    whole_products = lax.dot_general(
        rows[slot, 0], rows[slot, 1], ACROSS, preferred_element_type=jnp.float32
    )
    for block in range(products.shape[0]):
        products[block] = whole_products[:, block * LANES : (block + 1) * LANES]
    group = products.shape[1] // VB
    for high in range(VB // 4):
        for block in range(products.shape[0]):
            starts = [high * 4 + low for low in range(4)]
            blocks = [products[block, pl.ds(at, group, VB)].astype(jnp.bfloat16) for at in starts]
            for low, moved in enumerate(swap_fours(blocks)):
                to = (block * 4 + low) * group
                integral[to : to + group, high * LANES : (high + 1) * LANES] = moved
    upper = lax.axis_index("amp") >= CHIPS * CORES // 2
    order = [jnp.where(upper, CHIPS - 1 - chip, chip) for chip in range(CHIPS)]
    mine = jnp.concatenate([amps[slot, chip] for chip in order]).reshape(-1, amps.shape[-1])
    term = lax.dot_general(mine, integral[...], ACROSS, preferred_element_type=jnp.float32)
    for which, out in enumerate(outs):

        @pl.when(step // each == which)
        def _():
            out[0] = term.astype(jnp.bfloat16)


def ladder(first, bits, plan, blocks, amps):
    _, rows, depth = blocks[0].shape
    columns, chips, each, amp_rows, pairs = amps[0].shape
    occupied = chips * CORES * amp_rows
    side = 4 * rows
    terms = (side // VB) ** 2
    tasks = len(bits) * each

    def out_spec(which):
        half = lambda step: jnp.clip(step - which * each, 0, each - 1)
        return pl.BlockSpec((1, occupied, terms), lambda step, plan: (half(step), 0, 0))

    return pl.pallas_call(
        functools.partial(ladder_kernel, first, bits),
        out_shape=[jax.ShapeDtypeStruct((each, occupied, terms), jnp.bfloat16)] * len(bits),
        grid_spec=pltpu.PrefetchScalarGridSpec(
            num_scalar_prefetch=1,
            grid=(tasks,),
            in_specs=[pl.BlockSpec(memory_space=pl.ANY)] * (SOURCES + len(amps)),
            out_specs=[out_spec(which) for which in range(len(bits))],
            scratch_shapes=[
                pltpu.VMEM((2, 2, side, depth), jnp.bfloat16),
                pltpu.VMEM((2, chips, CORES, amp_rows, pairs), jnp.bfloat16),
                pltpu.VMEM((side // LANES, side, LANES), jnp.float32),
                pltpu.VMEM((terms, pairs), jnp.bfloat16),
                pltpu.SemaphoreType.DMA((2, 10)),
            ],
        ),
        compiler_params=pltpu.CompilerParams(vmem_limit_bytes=VMEM),
        cost_estimate=pl.CostEstimate(
            flops=tasks * 6 * (side * side * depth + occupied * terms * pairs),
            bytes_accessed=tasks * 2 * (2 * side * depth + occupied * pairs),
            transcendentals=0,
        ),
        name="ladder",
    )(plan, *blocks, *amps)


def routes():
    last = CHIPS - 1
    feed = [(0, 1), (last, last - 1)]
    middle = [(1, 2), (2, 1)]
    both = lambda hops: [(a * CORES + c, b * CORES + c) for a, b in hops for c in range(CORES)]
    sibling = [(a * CORES + c, a * CORES + 1 - c) for a in range(CHIPS) for c in range(CORES)]
    return both(feed), both(middle), sibling


def swap_columns(array, bit, columns):
    return lax.ppermute(array, "vec", perm=[(column, column ^ bit) for column in range(columns)])


def products(first, slots, listed, twice, chol, amplitudes, plan, each):
    feed, middle, sibling = routes()
    send = functools.partial(lax.ppermute, axis_name="amp")
    start = first["order"]
    (mine,) = collect(plan, (first["amp"], each, each, amplitudes))
    end = send(mine, perm=feed)
    (own_a,) = collect(plan, (start, 0, slots, chol))
    own_a, chol = lax.optimization_barrier((own_a, chol))
    mid_a = send(own_a, perm=middle)
    fed_a = send(own_a, perm=feed)
    (own_b,) = collect(plan, (start + slots, 0, listed - slots, chol))
    sib_a = send(own_a, perm=sibling)
    over = send(mine, perm=middle)
    end, own_b = lax.optimization_barrier((end, own_b))
    far = send(end, perm=middle)
    line = jnp.stack([end, mine, over])
    own_b, fed_a, mid_a, sib_a, line, far = lax.optimization_barrier(
        (own_b, fed_a, mid_a, sib_a, line, far)
    )
    mid_b = send(fed_a, perm=middle)
    fed_b = send(own_b, perm=feed)
    sib_b = send(own_b, perm=sibling)
    sfed_a = send(fed_a, perm=sibling)
    amps = lax.all_gather(jnp.concatenate([line, far[None]]), "vec", axis=0, tiled=False)
    amps = (amps, send(amps, perm=sibling))
    fed_b, mid_b, sib_b, sfed_a, amps = lax.optimization_barrier((fed_b, mid_b, sib_b, sfed_a, amps))
    sfed_b = send(fed_b, perm=sibling)
    blocks = (own_a, own_b, sib_a, sib_b, fed_a, fed_b, sfed_a, sfed_b, mid_a, mid_b)
    columns = lax.axis_size("vec")
    away = list(range(columns))[:0:-1]
    arrived = []
    for call in ([away, [0]] if twice else [[*away, 0]]):
        for bit, term in zip(call, ladder(first, call, plan, blocks, amps)):
            arrived.append(swap_columns(term, bit, columns) if bit else term)
    return sum(term.astype(jnp.float32) for term in arrived).astype(jnp.bfloat16)


def target_columns(swap):
    worker, right, left = np.meshgrid(
        np.arange(2 * CORES), np.arange(VB // 2), np.arange(VB // 2), indexing="ij"
    )
    core = worker % CORES
    chip = 1 + worker // CORES
    near = np.where(chip == 1, 0, CHIPS - 1)
    far = np.where(chip == 1, 2, 1)
    end = np.where(chip == 1, CHIPS - 1, 0)
    each = VB // (CHIPS * CORES)

    def local(at):
        block = at // each
        home = np.where(block < 2, chip, near) * CORES + np.where(block % 2 == 0, core, 1 - core)
        return home * each + at % each

    def spread(at):
        return (np.choose(at // each, [chip, near, far, end]) * CORES + core) * each + at % each

    a, b = (spread(left), local(right)) if swap else (local(left), spread(right))
    return (a * VB + b).reshape(-1)


def scatter_terms(terms, named, tiles):
    columns = lax.axis_size("vec")
    column = lax.axis_index("vec")
    owners = lax.axis_size("amp")
    halves, rows, width = terms.shape
    each = rows // owners
    mine = terms.reshape(halves, owners, each, width).swapaxes(0, 1)
    mine = lax.all_to_all(mine, "amp", split_axis=0, concat_axis=0, tiled=True)
    mine = mine[CORES : CORES * (CHIPS - 1)].transpose(1, 2, 0, 3).reshape(halves * each, PAIRS)
    canonical = jnp.arange(PAIRS, dtype=jnp.int32)[None, :]
    one_hot = lambda to: (jnp.asarray(to, jnp.int32)[:, None] == canonical).astype(jnp.bfloat16)
    straight, turned = one_hot(target_columns(False)), one_hot(target_columns(True))
    dot = functools.partial(jnp.dot, preferred_element_type=jnp.float32)
    straight, turned = dot(mine, straight), dot(mine, turned)
    swap = named["swap"].reshape(halves, columns)
    out = named["out"].reshape(halves, columns)
    swapped = jnp.repeat(lax.dynamic_index_in_dim(swap, column, 1), each, axis=0) == 1
    placed = jnp.where(swapped, turned, straight).astype(jnp.bfloat16).reshape(halves, each, PAIRS)
    held = tiles // columns
    here = column * held + jnp.arange(held, dtype=jnp.int32)
    total = jnp.zeros((held, each, PAIRS), jnp.float32)
    for bit in range(columns):
        arrived = placed if bit == 0 else swap_columns(placed, bit, columns)
        targets = lax.dynamic_index_in_dim(out, column ^ bit, 1, keepdims=False)
        for half in range(halves):
            named_here = (here == targets[half])[:, None, None]
            total = total + jnp.where(named_here, arrived[half].astype(jnp.float32)[None], 0.0)
    return total.astype(jnp.bfloat16)


def line_local(chol, amplitudes, task_list, counts):
    tasks = lax.axis_size("amp")
    tiles = chol.shape[0]
    each = tasks // lax.axis_size("vec")
    half = tasks // 2
    classes = [(half + 1, tasks + 3), (half + 1, tasks + 2), (half, tasks + 1), (half + 2, tasks + 4)]
    classes.append((tasks, min(2 * tasks, tiles)))
    plan, named, branch = make_plan(tasks, tiles, classes, task_list, counts)
    first = {name: place[0] for name, place in plan_layout(tasks, tiles)[0].items()}
    def run(slots, listed):
        twice = slots < tasks
        return lambda: products(first, slots, listed, twice, chol, amplitudes, plan, each)

    terms = lax.switch(branch, [run(*sizes) for sizes in classes])
    return scatter_terms(terms, named, tiles)


def integral_tile(x_rows, y_rows):
    products = lax.dot_general(
        x_rows, y_rows, (((1,), (1,)), ((), ())), preferred_element_type=jnp.float32
    )
    return (
        products.reshape(VB, VB, VB, VB).transpose(0, 2, 1, 3).reshape(PAIRS, PAIRS).astype(jnp.bfloat16)
    )


def task_term(x_rows, y_rows, amp_rows):
    products = lax.dot_general(
        amp_rows, integral_tile(x_rows, y_rows), (((1,), (1,)), ((), ())), preferred_element_type=jnp.float32
    )
    return products.astype(jnp.bfloat16)


def spread_local(chol, amplitudes, task_list, counts):
    owners = lax.axis_size("amp")
    most = task_list.shape[0] // owners
    rank = jnp.arange(owners, dtype=jnp.int32)[:, None]
    offsets = jnp.cumsum(counts) - counts
    inside = (rank >= offsets) & (rank < offsets + counts)
    starts = jnp.arange(owners, dtype=jnp.int32) * most
    fields = task_list[jnp.sum(jnp.where(inside, starts + rank - offsets, 0), axis=1)]
    trade = functools.partial(lax.all_to_all, axis_name="amp", tiled=True)
    fetch = lambda array, which: trade(jnp.take(array, which, axis=0), split_axis=0, concat_axis=0).reshape(
        -1, array.shape[2]
    )
    term = task_term(fetch(chol, fields[:, 0]), fetch(chol, fields[:, 1]), fetch(amplitudes, fields[:, 2]))
    returned = trade(term.reshape(owners, -1, PAIRS), split_axis=0, concat_axis=0)
    tiles = amplitudes.shape[0]
    chosen = (jnp.arange(tiles, dtype=jnp.int32)[:, None] == fields[:, 3][None, :]).astype(jnp.bfloat16)
    summed = jnp.dot(chosen, returned.reshape(owners, -1), preferred_element_type=jnp.float32)
    summed = summed.reshape(tiles, -1, PAIRS)
    return lax.psum_scatter(summed, "vec", scatter_dimension=0, tiled=True).astype(jnp.bfloat16)


def solution(mesh):
    placed = (P(None, "amp", "vec"), P(None, "amp", None), P(), P())
    local = line_local if mesh.shape["amp"] == CHIPS * CORES else spread_local
    return jax.shard_map(
        local, mesh=mesh, in_specs=placed, out_specs=P("vec", "amp", None), check_vma=False
    )
```

```python
import functools

import jax
import jax.numpy as jnp
import numpy as np
from jax import lax
from jax.experimental import pallas as pl
from jax.experimental.pallas import tpu as pltpu
from jax.sharding import PartitionSpec as P

VB = 32
PAIRS = VB * VB
CORES = 2
CHIPS = 4
LANES = 128
VMEM = 60 * 1024 * 1024


def plan_layout(tasks, tiles):
    fields = {}
    at = 0
    for name, size in (("order", tiles), ("local", tasks), ("spread", tasks), ("amp", tasks),
                       ("out", tasks), ("swap", tasks)):
        fields[name] = (at, size)
        at += size
    return fields, at


def popcount(bits):
    bits = bits - ((bits >> 1) & 0x55555555)
    bits = (bits & 0x33333333) + ((bits >> 2) & 0x33333333)
    bits = (bits + (bits >> 4)) & 0x0F0F0F0F
    return (bits + (bits >> 8) + (bits >> 16) + (bits >> 24)) & 0xFF


def plan_kernel(tasks, tiles, most, classes, task_ref, count_ref, plan_ref, size_ref, work):
    fields, _ = plan_layout(tasks, tiles)
    first = {name: place[0] for name, place in fields.items()}
    at = jnp.int32(0)
    for owner in range(count_ref.shape[0]):
        for entry in range(most):
            live = entry < count_ref[owner]

            @pl.when(live)
            def _():
                for column in range(4):
                    work[at * 4 + column] = task_ref[column, owner * most + entry]

            at = at + live.astype(jnp.int32)
    x = [work[task * 4] for task in range(tasks)]
    y = [work[task * 4 + 1] for task in range(tasks)]
    one = jnp.int32(1)
    codes = 1 << tasks
    code = lax.broadcasted_iota(jnp.int32, (codes // LANES, LANES), 0) * LANES + lax.broadcasted_iota(
        jnp.int32, (codes // LANES, LANES), 1
    )
    bits = jnp.zeros_like(code)
    used = jnp.int32(0)
    for task in range(tasks):
        bits = bits | jnp.where((code >> task) & 1 == 1, one << y[task], one << x[task])
        used = used | (one << y[task]) | (one << x[task])
    best = jnp.min(popcount(bits) * codes + code) & (codes - 1)
    cover = jnp.int32(0)
    for task in range(tasks):
        cover = cover | (one << jnp.where((best >> task) & 1 == 1, y[task], x[task]))
    place = jnp.int32(0)
    sizes = []
    for group in (cover, used & ~cover, ~used):
        for tile in range(tiles):
            member = (group >> tile) & 1 == 1

            @pl.when(member)
            def _():
                plan_ref[first["order"] + place] = jnp.int32(tile)
                work[4 * tasks + tile] = place

            place = place + member.astype(jnp.int32)
        sizes.append(place)
    fits = jnp.int32(len(classes) - 1)
    for at, (spread, listed) in sorted(enumerate(classes), key=lambda entry: -sum(entry[1])):
        fits = jnp.where((sizes[0] <= spread) & (sizes[1] <= listed), at, fits)
    size_ref[0] = fits
    for task in range(tasks):
        swap = (best >> task) & 1 == 0
        plan_ref[first["local"] + task] = work[4 * tasks + jnp.where(swap, y[task], x[task])]
        plan_ref[first["spread"] + task] = work[4 * tasks + jnp.where(swap, x[task], y[task])]
        plan_ref[first["amp"] + task] = work[task * 4 + 2]
        plan_ref[first["out"] + task] = work[task * 4 + 3]
        plan_ref[first["swap"] + task] = swap.astype(jnp.int32)


def make_plan(tasks, tiles, classes, task_list, counts):
    fields, length = plan_layout(tasks, tiles)
    most = task_list.shape[0] // counts.shape[0]
    smem = pl.BlockSpec(memory_space=pltpu.SMEM)
    plan, size = pl.pallas_call(
        functools.partial(plan_kernel, tasks, tiles, most, classes),
        out_shape=[jax.ShapeDtypeStruct((length,), jnp.int32), jax.ShapeDtypeStruct((1,), jnp.int32)],
        in_specs=[smem] * 2,
        out_specs=[smem] * 2,
        scratch_shapes=[pltpu.SMEM((4 * tasks + tiles,), jnp.int32)],
        name="plan",
    )(task_list.T, counts)
    return plan, {name: plan[at : at + held] for name, (at, held) in fields.items()}, size[0]


def collect_kernel(lists, plan, *refs):
    sources, refs = refs[: len(lists)], refs[len(lists) :]
    outs, refs = refs[: len(lists)], refs[len(lists) :]
    *held, sems = refs
    moves = []
    for (first, each), source, out, slot in zip(lists, sources, outs, held):
        begin = lax.axis_index("vec") * each + first
        moves += [(source.at[plan[begin + at]], slot.at[at], out.at[at]) for at in range(out.shape[0])]
    loads = [pltpu.make_async_copy(move[0], move[1], sems.at[0, at]) for at, move in enumerate(moves)]
    stores = [pltpu.make_async_copy(move[1], move[2], sems.at[1, at]) for at, move in enumerate(moves)]
    for load in loads:
        load.start()
    for load, store in zip(loads, stores):
        load.wait()
        store.start()
    for store in stores:
        store.wait()


def collect(plan, *wanted):
    shapes = [(count, *array.shape[1:]) for _, _, count, array in wanted]
    total = sum(shape[0] for shape in shapes)
    any_spec = pl.BlockSpec(memory_space=pl.ANY)
    return pl.pallas_call(
        functools.partial(collect_kernel, [want[:2] for want in wanted]),
        out_shape=[jax.ShapeDtypeStruct(shape, jnp.bfloat16) for shape in shapes],
        in_specs=[pl.BlockSpec(memory_space=pltpu.SMEM)] + [any_spec] * len(wanted),
        out_specs=[any_spec] * len(wanted),
        scratch_shapes=[pltpu.VMEM(shape, jnp.bfloat16) for shape in shapes]
        + [pltpu.SemaphoreType.DMA((2, total))],
        compiler_params=pltpu.CompilerParams(vmem_limit_bytes=VMEM),
        name="collect",
    )(plan, *[want[3] for want in wanted])


def swap_fours(blocks):
    group = lax.broadcasted_iota(jnp.int32, blocks[0].shape, 1) // VB
    for bit in (1, 2):
        right = (group & bit) != 0
        shift = bit * VB
        moved = list(blocks)
        for low in range(4):
            if low & bit:
                continue
            high = low | bit
            moved[low] = jnp.where(right, pltpu.roll(blocks[high], shift, 1), blocks[low])
            moved[high] = jnp.where(right, blocks[high], pltpu.roll(blocks[low], LANES - shift, 1))
        blocks = moved
    return blocks


ACROSS = (((1,), (1,)), ((), ()))
SOURCES = 8


def ladder_kernel(first, bits, plan, *refs):
    sources, refs = refs[:SOURCES], refs[SOURCES:]
    amp_own, amp_sib, *outs, rows, amps, products, integral, sems = refs
    own, sib, fed_a, fed_b, sfed_a, sfed_b, mid_a, mid_b = sources
    whole, pairs = (own, sib), ((fed_a, fed_b), (sfed_a, sfed_b))
    wide = (own, fed_a, mid_a, mid_b)
    slots, each_row, _ = mid_a.shape
    each = amp_own.shape[2]
    step = pl.program_id(0)
    columns = amp_own.shape[0]
    column = lax.axis_index("vec")
    core = lax.rem(lax.axis_index("amp"), CORES)
    bit_of = lambda at: sum(jnp.where(at // each == which, bit, 0) for which, bit in enumerate(bits))
    task_of = lambda at: lax.rem(at, each) * columns + (bit_of(at) ^ column)
    part = lambda slot, side, block: rows.at[slot, side, pl.ds(block * each_row, each_row)]

    def amp_copies(task, slot):
        return [
            pltpu.make_async_copy(
                source.at[task // each, :, lax.rem(task, each)],
                amps.at[slot, :, holder],
                sems.at[slot, 2 * len(wide) + at],
            )
            for at, (source, holder) in enumerate(((amp_own, core), (amp_sib, 1 - core)))
        ]

    def start(task, slot):
        swap = plan[first["swap"] + task]
        at = plan[first["local"] + task]
        for block, source in enumerate(whole):
            pltpu.make_async_copy(source.at[at], part(slot, swap, block), sems.at[slot, block]).start()
        for block, (early, late) in enumerate(pairs, len(whole)):
            target, sem = part(slot, swap, block), sems.at[slot, block]

            @pl.when(at < slots)
            def _():
                pltpu.make_async_copy(early.at[at], target, sem).start()

            @pl.when(at >= slots)
            def _():
                pltpu.make_async_copy(late.at[at - slots], target, sem).start()

        at = plan[first["spread"] + task]
        for block, source in enumerate(wide):
            target, sem = part(slot, 1 - swap, block), sems.at[slot, len(wide) + block]
            pltpu.make_async_copy(source.at[at], target, sem).start()
        for copy in amp_copies(task, slot):
            copy.start()

    def wait(task, slot):
        swap = plan[first["swap"] + task]
        for block in range(len(wide)):
            for side, at in ((swap, block), (1 - swap, len(wide) + block)):
                pltpu.make_async_copy(own.at[0], part(slot, side, block), sems.at[slot, at]).wait()
        for copy in amp_copies(task, slot):
            copy.wait()

    @pl.when(step == 0)
    def _():
        start(task_of(0), 0)

    @pl.when(step + 1 < pl.num_programs(0))
    def _():
        start(task_of(step + 1), lax.rem(step + 1, 2))

    slot = lax.rem(step, 2)
    wait(task_of(step), slot)
    whole_products = lax.dot_general(
        rows[slot, 0], rows[slot, 1], ACROSS, preferred_element_type=jnp.float32
    )
    for block in range(products.shape[0]):
        products[block] = whole_products[:, block * LANES : (block + 1) * LANES]
    group = products.shape[1] // VB
    for high in range(VB // 4):
        for block in range(products.shape[0]):
            starts = [high * 4 + low for low in range(4)]
            blocks = [products[block, pl.ds(at, group, VB)].astype(jnp.bfloat16) for at in starts]
            for low, moved in enumerate(swap_fours(blocks)):
                to = (block * 4 + low) * group
                integral[to : to + group, high * LANES : (high + 1) * LANES] = moved
    upper = lax.axis_index("amp") >= CHIPS * CORES // 2
    order = [jnp.where(upper, CHIPS - 1 - chip, chip) for chip in range(CHIPS)]
    mine = jnp.concatenate([amps[slot, chip] for chip in order]).reshape(-1, amps.shape[-1])
    term = lax.dot_general(mine, integral[...], ACROSS, preferred_element_type=jnp.float32)
    for which, out in enumerate(outs):

        @pl.when(step // each == which)
        def _():
            out[0] = term.astype(jnp.bfloat16)


def ladder(first, bits, plan, blocks, amps):
    _, rows, depth = blocks[0].shape
    columns, chips, each, amp_rows, pairs = amps[0].shape
    occupied = chips * CORES * amp_rows
    side = 4 * rows
    terms = (side // VB) ** 2
    tasks = len(bits) * each

    def out_spec(which):
        half = lambda step: jnp.clip(step - which * each, 0, each - 1)
        return pl.BlockSpec((1, occupied, terms), lambda step, plan: (half(step), 0, 0))

    return pl.pallas_call(
        functools.partial(ladder_kernel, first, bits),
        out_shape=[jax.ShapeDtypeStruct((each, occupied, terms), jnp.bfloat16)] * len(bits),
        grid_spec=pltpu.PrefetchScalarGridSpec(
            num_scalar_prefetch=1,
            grid=(tasks,),
            in_specs=[pl.BlockSpec(memory_space=pl.ANY)] * (SOURCES + len(amps)),
            out_specs=[out_spec(which) for which in range(len(bits))],
            scratch_shapes=[
                pltpu.VMEM((2, 2, side, depth), jnp.bfloat16),
                pltpu.VMEM((2, chips, CORES, amp_rows, pairs), jnp.bfloat16),
                pltpu.VMEM((side // LANES, side, LANES), jnp.float32),
                pltpu.VMEM((terms, pairs), jnp.bfloat16),
                pltpu.SemaphoreType.DMA((2, 10)),
            ],
        ),
        compiler_params=pltpu.CompilerParams(vmem_limit_bytes=VMEM),
        cost_estimate=pl.CostEstimate(
            flops=tasks * 6 * (side * side * depth + occupied * terms * pairs),
            bytes_accessed=tasks * 2 * (2 * side * depth + occupied * pairs),
            transcendentals=0,
        ),
        name="ladder",
    )(plan, *blocks, *amps)


def routes():
    last = CHIPS - 1
    feed = [(0, 1), (last, last - 1)]
    middle = [(1, 2), (2, 1)]
    both = lambda hops: [(a * CORES + c, b * CORES + c) for a, b in hops for c in range(CORES)]
    sibling = [(a * CORES + c, a * CORES + 1 - c) for a in range(CHIPS) for c in range(CORES)]
    return both(feed), both(middle), both([(0, 2), (last, 1)]), sibling


def swap_columns(array, bit, columns):
    return lax.ppermute(array, "vec", perm=[(column, column ^ bit) for column in range(columns)])


def products(first, slots, listed, twice, chol, amplitudes, plan, each):
    feed, middle, across, sibling = routes()
    send = functools.partial(lax.ppermute, axis_name="amp")
    start = first["order"]
    (mine,) = collect(plan, (first["amp"], each, each, amplitudes))
    end = send(mine, perm=feed)
    (own_a,) = collect(plan, (start, 0, slots, chol))
    own_a, chol = lax.optimization_barrier((own_a, chol))
    mid_a = send(own_a, perm=middle)
    fed_a = send(own_a, perm=feed)
    own_b, own = collect(plan, (start + slots, 0, listed - slots, chol), (start, 0, listed, chol))
    over = send(mine, perm=middle)
    far = send(mine, perm=across)
    line = jnp.stack([end, mine, over])
    own_b, own, fed_a, mid_a, line, far = lax.optimization_barrier(
        (own_b, own, fed_a, mid_a, line, far)
    )
    mid_b = send(fed_a, perm=middle)
    fed_b = send(own_b, perm=feed)
    sib = send(own, perm=sibling)
    sfed_a = send(fed_a, perm=sibling)
    amps = lax.all_gather(jnp.concatenate([line, far[None]]), "vec", axis=0, tiled=False)
    amps = (amps, send(amps, perm=sibling))
    fed_b, mid_b, sib, sfed_a, amps = lax.optimization_barrier((fed_b, mid_b, sib, sfed_a, amps))
    sfed_b = send(fed_b, perm=sibling)
    blocks = (own, sib, fed_a, fed_b, sfed_a, sfed_b, mid_a, mid_b)
    columns = lax.axis_size("vec")
    away = list(range(columns))[:0:-1]
    arrived = []
    for call in ([away, [0]] if twice else [[*away, 0]]):
        for bit, term in zip(call, ladder(first, call, plan, blocks, amps)):
            arrived.append(swap_columns(term, bit, columns) if bit else term)
    return sum(term.astype(jnp.float32) for term in arrived).astype(jnp.bfloat16)


def target_columns(swap):
    worker, right, left = np.meshgrid(
        np.arange(2 * CORES), np.arange(VB // 2), np.arange(VB // 2), indexing="ij"
    )
    core = worker % CORES
    chip = 1 + worker // CORES
    near = np.where(chip == 1, 0, CHIPS - 1)
    far = np.where(chip == 1, 2, 1)
    end = np.where(chip == 1, CHIPS - 1, 0)
    each = VB // (CHIPS * CORES)

    def local(at):
        block = at // each
        home = np.where(block < 2, chip, near) * CORES + np.where(block % 2 == 0, core, 1 - core)
        return home * each + at % each

    def spread(at):
        return (np.choose(at // each, [chip, near, far, end]) * CORES + core) * each + at % each

    a, b = (spread(left), local(right)) if swap else (local(left), spread(right))
    return (a * VB + b).reshape(-1)


def scatter_terms(terms, named, tiles):
    columns = lax.axis_size("vec")
    column = lax.axis_index("vec")
    owners = lax.axis_size("amp")
    halves, rows, width = terms.shape
    each = rows // owners
    mine = terms.reshape(halves, owners, each, width).swapaxes(0, 1)
    mine = lax.all_to_all(mine, "amp", split_axis=0, concat_axis=0, tiled=True)
    mine = mine[CORES : CORES * (CHIPS - 1)].transpose(1, 2, 0, 3).reshape(halves * each, PAIRS)
    canonical = jnp.arange(PAIRS, dtype=jnp.int32)[None, :]
    one_hot = lambda to: (jnp.asarray(to, jnp.int32)[:, None] == canonical).astype(jnp.bfloat16)
    straight, turned = one_hot(target_columns(False)), one_hot(target_columns(True))
    dot = functools.partial(jnp.dot, preferred_element_type=jnp.float32)
    straight, turned = dot(mine, straight), dot(mine, turned)
    swap = named["swap"].reshape(halves, columns)
    out = named["out"].reshape(halves, columns)
    swapped = jnp.repeat(lax.dynamic_index_in_dim(swap, column, 1), each, axis=0) == 1
    placed = jnp.where(swapped, turned, straight).astype(jnp.bfloat16).reshape(halves, each, PAIRS)
    held = tiles // columns
    here = column * held + jnp.arange(held, dtype=jnp.int32)
    total = jnp.zeros((held, each, PAIRS), jnp.float32)
    for bit in range(columns):
        arrived = placed if bit == 0 else swap_columns(placed, bit, columns)
        targets = lax.dynamic_index_in_dim(out, column ^ bit, 1, keepdims=False)
        for half in range(halves):
            named_here = (here == targets[half])[:, None, None]
            total = total + jnp.where(named_here, arrived[half].astype(jnp.float32)[None], 0.0)
    return total.astype(jnp.bfloat16)


def line_local(chol, amplitudes, task_list, counts):
    tasks = lax.axis_size("amp")
    tiles = chol.shape[0]
    each = tasks // lax.axis_size("vec")
    half = tasks // 2
    classes = [(half + 1, tasks + 3), (half + 1, tasks + 2), (half, tasks + 1), (half + 2, tasks + 4)]
    classes.append((tasks, min(2 * tasks, tiles)))
    plan, named, branch = make_plan(tasks, tiles, classes, task_list, counts)
    first = {name: place[0] for name, place in plan_layout(tasks, tiles)[0].items()}
    def run(slots, listed):
        twice = slots < tasks
        return lambda: products(first, slots, listed, twice, chol, amplitudes, plan, each)

    terms = lax.switch(branch, [run(*sizes) for sizes in classes])
    return scatter_terms(terms, named, tiles)


def integral_tile(x_rows, y_rows):
    products = lax.dot_general(
        x_rows, y_rows, (((1,), (1,)), ((), ())), preferred_element_type=jnp.float32
    )
    return (
        products.reshape(VB, VB, VB, VB).transpose(0, 2, 1, 3).reshape(PAIRS, PAIRS).astype(jnp.bfloat16)
    )


def task_term(x_rows, y_rows, amp_rows):
    products = lax.dot_general(
        amp_rows, integral_tile(x_rows, y_rows), (((1,), (1,)), ((), ())), preferred_element_type=jnp.float32
    )
    return products.astype(jnp.bfloat16)


def spread_local(chol, amplitudes, task_list, counts):
    owners = lax.axis_size("amp")
    most = task_list.shape[0] // owners
    rank = jnp.arange(owners, dtype=jnp.int32)[:, None]
    offsets = jnp.cumsum(counts) - counts
    inside = (rank >= offsets) & (rank < offsets + counts)
    starts = jnp.arange(owners, dtype=jnp.int32) * most
    fields = task_list[jnp.sum(jnp.where(inside, starts + rank - offsets, 0), axis=1)]
    trade = functools.partial(lax.all_to_all, axis_name="amp", tiled=True)
    fetch = lambda array, which: trade(jnp.take(array, which, axis=0), split_axis=0, concat_axis=0).reshape(
        -1, array.shape[2]
    )
    term = task_term(fetch(chol, fields[:, 0]), fetch(chol, fields[:, 1]), fetch(amplitudes, fields[:, 2]))
    returned = trade(term.reshape(owners, -1, PAIRS), split_axis=0, concat_axis=0)
    tiles = amplitudes.shape[0]
    chosen = (jnp.arange(tiles, dtype=jnp.int32)[:, None] == fields[:, 3][None, :]).astype(jnp.bfloat16)
    summed = jnp.dot(chosen, returned.reshape(owners, -1), preferred_element_type=jnp.float32)
    summed = summed.reshape(tiles, -1, PAIRS)
    return lax.psum_scatter(summed, "vec", scatter_dimension=0, tiled=True).astype(jnp.bfloat16)


def solution(mesh):
    placed = (P(None, "amp", "vec"), P(None, "amp", None), P(), P())
    local = line_local if mesh.shape["amp"] == CHIPS * CORES else spread_local
    return jax.shard_map(
        local, mesh=mesh, in_specs=placed, out_specs=P("vec", "amp", None), check_vma=False
    )
```
